32 devices in a mesh: dp: 2 (over core), head: 4 (over y, x), mlp: 4 (over z).
Axes of the slice: x: 2, y: 2, z: 4, core: 2. Of those that a mesh axis runs over, the one named last changes fastest.
Arguments:
- tokens: bfloat16 [2048, 8, 1024], P('head', ('dp', 'mlp')), may hold values from -6 to 6
- first_values: bfloat16 [2048, 8, 1024], P(None, ('dp', 'mlp'), 'head'), may hold values from -10.5 to 10.5
- segment_ids: int32 [2048, 8], P(None, ('dp', 'mlp')), may hold values from 0 to 7, as said below
- positions: int32 [2048, 8], P(None, ('dp', 'mlp')), may hold values from 0 to 2047, as said below
- attn_gain: float32 [1024], replicated, may hold values from 0.5 to 1.5
- w_query: bfloat16 [1024, 1024], P(None, 'head'), may hold values from -0.1875 to 0.1875
- w_key: bfloat16 [1024, 1024], P(None, 'head'), may hold values from -0.1875 to 0.1875
- w_value: bfloat16 [1024, 1024], P(None, 'head'), may hold values from -0.1875 to 0.1875
- w_out: bfloat16 [1024, 1024], P('head'), may hold values from -2 to 2
- mlp_gain: float32 [1024], replicated, may hold values from 0.5 to 1.5
- w_gate: bfloat16 [1024, 2816], P(None, 'mlp'), may hold values from -0.1875 to 0.1875
- w_up: bfloat16 [1024, 2816], P(None, 'mlp'), may hold values from -0.1875 to 0.1875
- w_down: bfloat16 [2816, 1024], P('mlp'), may hold values from -0.109375 to 0.109375
- out_grad: bfloat16 [2048, 8, 1024], P('head', ('dp', 'mlp')), may hold values from -6 to 6
Outputs:
- output: bfloat16 [2048, 8, 1024], P('head', ('dp', 'mlp'))
- input_grad: bfloat16 [2048, 8, 1024], P('head', ('dp', 'mlp'))
- first_values_grad: bfloat16 [2048, 8, 1024], P(None, ('dp', 'mlp'), 'head')
- attn_gain_grad: float32 [1024], replicated
- w_query_grad: float32 [1024, 1024], P(None, 'head')
- w_key_grad: float32 [1024, 1024], P(None, 'head')
- w_value_grad: float32 [1024, 1024], P(None, 'head')
- w_out_grad: float32 [1024, 1024], P('head')
- mlp_gain_grad: float32 [1024], replicated
- w_gate_grad: float32 [1024, 2816], P(None, 'mlp')
- w_up_grad: float32 [1024, 2816], P(None, 'mlp')
- w_down_grad: float32 [2816, 1024], P('mlp')
- value_norms: float32 [2], replicated
The draws below stay inside these ranges and needn't reach their ends.
Inputs may be any that keep to these rules, and one draw needn't show every extreme that they name: `segment_ids`: along each packed row (dimension 0) the ids start at 0 and rise by at most one from one position to the next; packed row 0 holds a single document, every other packed row exactly 8. `positions`: 0 at a row's start and wherever the segment id changes, else one more than at the previous position.
All inputs are finite; a program needn't handle non-finite values.
Results may differ from the reference program's by a relative error of at most 0.019.
Values may be sent and summed in bfloat16 or wider, within the bound.
No kernel may reach another device: no remote copies, remote signals or barrier semaphores. Data moves between devices by JAX's collectives and lax.ppermute only.
A program may use at most 256 MiB of HBM per device.

```python
import jax
import jax.numpy as jnp
from jax import lax

D = 1024
HEADS = 16
HEAD_DIM = 64
FF = 2816
LEN = 2048
ROWS = 8


def doc_layout(key):
    shape = (LEN, ROWS)
    index = lax.broadcasted_iota(jnp.int32, shape, 0)
    column = lax.broadcasted_iota(jnp.int32, shape, 1)
    inner = jax.random.fold_in(key, 7)

    def pick_starts(number):
        order = jax.random.permutation(jax.random.fold_in(inner, number), LEN - 1)
        return (order[:7] + 1).astype(jnp.int32)
    chosen = jax.vmap(pick_starts)(jnp.arange(ROWS, dtype=jnp.int32))
    marked = jnp.any(index[:, :, None] == chosen[None, :, :], axis=-1)
    starts = marked & (column != 0) | (index == 0)
    segments = jnp.cumsum(starts.astype(jnp.int32), axis=0) - 1
    first_index = lax.cummax(jnp.where(starts, index, 0), axis=0)
    return (segments.astype(jnp.int32), (index - first_index).astype(jnp.int32))


def draw_segment_ids(key, part):
    return doc_layout(key)[0]


def draw_positions(key, part):
    return doc_layout(key)[1]


def draw_first_values(key, part):
    shape = (LEN, ROWS, HEADS * HEAD_DIM)
    head_number = lax.broadcasted_iota(jnp.int32, shape, 2) // HEAD_DIM
    factor = 1.0 + 2.0 * head_number.astype(jnp.float32) / max(HEADS - 1, 1)
    inner = jax.random.fold_in(key, 11)
    base = jax.random.truncated_normal(inner, -3.0, 3.0, shape, jnp.float32)
    return (base * factor).astype(jnp.bfloat16)


def block_scale(rng, extent, cuts, least, largest):
    factor_of = 1.0
    for dim, parts in cuts:
        heights = jax.random.uniform(jax.random.fold_in(jax.random.fold_in(rng, 6), dim), (parts,), jnp.float32, least / len(cuts), largest / len(cuts))
        factor_of = factor_of * jnp.repeat(jnp.exp(heights), extent[dim] // parts).reshape((-1,) + (1,) * (len(extent) - 1 - dim))
    return factor_of


def centred(stream_key, dims, spread, limit, pieces=(), held_as=jnp.bfloat16):
    drawn = jax.random.normal(stream_key, dims, jnp.float32) * spread
    if len(pieces) > 0:
        drawn = block_scale(stream_key, dims, pieces, -0.22, 0.18) * drawn
    return jnp.clip(drawn, min=-limit, max=limit).astype(held_as)


def setup_inputs(seed: int = 0) -> dict:
    key_list = jax.random.split(jax.random.key(seed), 15)
    tokens = centred(key_list[0], (LEN, ROWS, D), 1.0, 6.0, ((0, 4), (1, 8)))
    first_values = draw_first_values(jax.random.fold_in(key_list[14], 71), 0)
    segment_ids = draw_segment_ids(jax.random.fold_in(key_list[14], 71), 0)
    positions = draw_positions(jax.random.fold_in(key_list[14], 71), 0)
    attn_gain = jnp.clip(1.0 + 0.1 * jax.random.normal(key_list[4], (D,), jnp.float32), 0.5, 1.5)
    w_query = centred(key_list[5], (D, HEADS * HEAD_DIM), D ** -0.5, 0.1875, ((1, 4),))
    w_key = centred(key_list[6], (D, HEADS * HEAD_DIM), D ** -0.5, 0.1875, ((1, 4),))
    w_value = centred(key_list[7], (D, HEADS * HEAD_DIM), D ** -0.5, 0.1875, ((1, 4),))
    w_out = centred(key_list[8], (HEADS * HEAD_DIM, D), (HEADS * HEAD_DIM * 16 // LEN) ** -0.5, 2.0, ((0, 4),))
    mlp_gain = jnp.clip(1.0 + 0.1 * jax.random.normal(key_list[9], (D,), jnp.float32), 0.5, 1.5)
    w_gate = centred(key_list[10], (D, FF), D ** -0.5, 0.1875, ((1, 4),))
    w_up = centred(key_list[11], (D, FF), D ** -0.5, 0.1875, ((1, 4),))
    w_down = centred(key_list[12], (FF, D), FF ** -0.5, 0.109375, ((0, 4),))
    out_grad = centred(key_list[13], (LEN, ROWS, D), 1.0, 6.0, ((0, 4), (1, 8)))
    return dict(tokens=tokens, first_values=first_values, segment_ids=segment_ids, positions=positions, attn_gain=attn_gain, w_query=w_query, w_key=w_key, w_value=w_value, w_out=w_out, mlp_gain=mlp_gain, w_gate=w_gate, w_up=w_up, w_down=w_down, out_grad=out_grad)


epsilon = 1e-06
theta_base = 10000.0
blend_weight = 0.5
masked_score = -1e+30
highest = lax.Precision.HIGHEST

@jax.custom_vjp
def low(v):
    return lax.optimization_barrier(v.astype(jnp.bfloat16)).astype(jnp.float32)

@jax.custom_vjp
def low_back(v):
    return v

def low_keep(v):
    return (low(v), None)

def low_pass(kept, grad):
    return (grad,)

def back_keep(v):
    return (v, None)

def back_low(kept, grad):
    return (low(grad),)
low.defvjp(low_keep, low_pass)
low_back.defvjp(back_keep, back_low)

def rms_norm(rows, gain):
    scale = lax.rsqrt(lax.optimization_barrier(jnp.mean(rows * rows, axis=-1, keepdims=True)) + epsilon)
    return rows * scale * gain

def rotate(values, places):
    half = values.shape[-1] // 2
    freq = theta_base ** (-jnp.arange(half, dtype=jnp.float32) * 2.0 / values.shape[-1])
    angles = places.astype(jnp.float32)[..., None] * freq
    cosine = jnp.cos(angles)[:, :, None, :]
    sine = jnp.sin(angles)[:, :, None, :]
    first, second = (values[..., :half], values[..., half:])
    return jnp.concatenate([first * cosine - second * sine, second * cosine + first * sine], axis=-1)

def attend_row(item):
    queries, keys, values, segments = item
    scale = HEAD_DIM ** (-0.5)
    scores = jnp.einsum('qhd,khd->hqk', queries, keys, precision=highest) * scale
    index = jnp.arange(queries.shape[0], dtype=jnp.int32)
    allowed = (index[None, :] <= index[:, None]) & (segments[None, :] == segments[:, None])
    scores = low_back(jnp.where(allowed[None], scores, masked_score))
    probs = low(jax.nn.softmax(scores, axis=-1))
    return jnp.einsum('hqk,khd->qhd', probs, values, precision=highest)

def layer(tokens, firsts, attn_gain, w_query, w_key, w_value, w_out, mlp_gain, w_gate, w_up, w_down, segments, places):
    group = tokens.shape[0]
    a_in = low(rms_norm(tokens, attn_gain))

    def project(weight):
        return jnp.einsum('gld,dh->glh', a_in, weight, precision=highest).reshape(group, LEN, HEADS, HEAD_DIM)
    queries = low(rotate(low_back(project(w_query)), places))
    keys = low(rotate(low_back(project(w_key)), places))
    first_heads = firsts.reshape(group, LEN, HEADS, HEAD_DIM)
    blended = blend_weight * project(w_value) + (1.0 - blend_weight) * first_heads
    blended_low = low(low_back(blended))
    mixed = lax.map(jax.checkpoint(attend_row), (queries, keys, blended_low, segments))
    mixed_low = low(low_back(mixed.reshape(group, LEN, HEADS * HEAD_DIM)))
    branch = low_back(jnp.einsum('glh,hd->gld', mixed_low, w_out, precision=highest))
    hidden_state = tokens + branch
    m_in = low(rms_norm(hidden_state, mlp_gain))
    gate = low_back(jnp.einsum('gld,df->glf', m_in, w_gate, precision=highest))
    up = low_back(jnp.einsum('gld,df->glf', m_in, w_up, precision=highest))
    hidden = low(jax.nn.silu(gate) * up)
    result = hidden_state + jnp.einsum('glf,fd->gld', hidden, w_down, precision=highest)
    first_norm = jnp.sum(jnp.sqrt(lax.optimization_barrier(jnp.sum(first_heads * first_heads, axis=-1))))
    blend_norm = jnp.sum(jnp.sqrt(lax.optimization_barrier(jnp.sum(blended * blended, axis=-1))))
    return (result, jnp.stack([first_norm, blend_norm]))

def reference(tokens, first_values, segment_ids, positions, attn_gain, w_query, w_key, w_value, w_out, mlp_gain, w_gate, w_up, w_down, out_grad):
    group = 2
    inputs = jnp.transpose(tokens, (1, 0, 2)).astype(jnp.float32)
    firsts = jnp.transpose(first_values, (1, 0, 2)).astype(jnp.float32)
    cotangent = jnp.transpose(out_grad, (1, 0, 2)).astype(jnp.float32)
    segments = jnp.transpose(segment_ids, (1, 0))
    places = jnp.transpose(positions, (1, 0))
    params = tuple((w.astype(jnp.float32) for w in (attn_gain, w_query, w_key, w_value, w_out, mlp_gain, w_gate, w_up, w_down)))

    def pack(array):
        return array.reshape((ROWS // group, group) + array.shape[1:])

    def step(carry, item):
        totals, norm_sums = carry
        part_in, part_first, part_segments, part_places, part_cot = item

        def forward(x_part, first_part, *weights):
            return layer(x_part, first_part, *weights, part_segments, part_places)
        result, pull, norms = jax.vjp(forward, part_in, part_first, *params, has_aux=True)
        grads = pull(part_cot)
        totals = tuple((t + g for t, g in zip(totals, grads[2:])))
        return ((totals, norm_sums + norms), (result, grads[0], grads[1]))
    init = (tuple((jnp.zeros_like(p) for p in params)), jnp.zeros((2,), jnp.float32))
    (totals, norm_sums), (result, input_grads, first_grads) = lax.scan(step, init, (pack(inputs), pack(firsts), pack(segments), pack(places), pack(cotangent)))

    def unpack(array):
        return jnp.transpose(array.reshape((ROWS,) + array.shape[2:]), (1, 0, 2)).astype(jnp.bfloat16)
    value_norms = norm_sums / (ROWS * LEN * HEADS)
    return (unpack(result), unpack(input_grads), unpack(first_grads), totals[0], totals[1], totals[2], totals[3], totals[4], totals[5], totals[6], totals[7], totals[8], value_norms)
```

```python
import functools

import jax
import jax.numpy as jnp
from jax import lax
from jax.experimental import pallas as pl
from jax.experimental.pallas import tpu as pltpu
from jax.sharding import PartitionSpec as P

HEAD_DIM = 64


epsilon = 1e-06
theta_base = 10000.0
blend_weight = 0.5
masked_score = -1e30


def rms_scale(rows):
    return lax.rsqrt(jnp.mean(rows * rows, axis=-1, keepdims=True) + epsilon)


def norm_back(rows, scale, gain, grad):
    weighted = grad * gain
    row_grad = scale * weighted - rows * scale * scale * scale * jnp.mean(
        weighted * rows, axis=-1, keepdims=True
    )
    gain_grad = jnp.sum(grad * rows * scale, axis=(0, 1))
    return (row_grad, gain_grad)


def rotate(values, places, direction):
    half = values.shape[-1] // 2
    freq = theta_base ** (-jnp.arange(half, dtype=jnp.float32) * 2.0 / values.shape[-1])
    angles = places.astype(jnp.float32)[..., None] * freq
    cosine = jnp.cos(angles)[:, :, None, :]
    sine = direction * jnp.sin(angles)[:, :, None, :]
    first, second = (values[..., :half], values[..., half:])
    return jnp.concatenate(
        [first * cosine - second * sine, second * cosine + first * sine], axis=-1
    )


NT=(((1,),(1,)),((),()))
NN=(((1,),(0,)),((),()))
TN=(((0,),(0,)),((),()))
def dot(a,b,dims): return lax.dot_general(a,b,dims,preferred_element_type=jnp.float32)

def head_lanes(lanes):
    return lanes//HEAD_DIM

def only_head(x,number,lanes,other=0.0):
    if lanes==HEAD_DIM: return x
    lane=lax.broadcasted_iota(jnp.int32,x.shape,1)
    return jnp.where(lane//HEAD_DIM==number,x,jnp.asarray(other,x.dtype))

def fwd2_kernel(block,firsts,lasts,q_ref,k_ref,v_ref,start_ref,o_ref,lse_ref,vt_ref):
    i=pl.program_id(1)
    length,lanes=k_ref.shape
    heads=lanes//HEAD_DIM
    @pl.when(i==0)
    def _():
        for r in range(length//block):
            rows=pl.ds(r*block,block)
            t=jnp.transpose(v_ref[rows,:])
            for n in range(heads):
                vt_ref[n,0:HEAD_DIM,rows]=t[n*HEAD_DIM:(n+1)*HEAD_DIM]
                vt_ref[n,HEAD_DIM:,rows]=jnp.ones((16,block),jnp.bfloat16)
    q=q_ref[...]*jnp.asarray(HEAD_DIM**-0.5,q_ref.dtype)
    qs=[only_head(q,n,lanes) for n in range(heads)]
    start=start_ref[...]
    key=lax.broadcasted_iota(jnp.int32,(block,block),0)
    col=i*block+lax.broadcasted_iota(jnp.int32,(block,block),1)
    def step(masked,j,carry):
        rows=pl.ds(pl.multiple_of(j*block,block),block)
        k=k_ref[rows,:]
        out=[]
        if masked:
            c=key+j*block
            allowed=(c<=col)&(c>=start)
        for n in range(heads):
            m,acc=carry[n]
            s=dot(k,qs[n],NT)
            if masked: s=jnp.where(allowed,s,masked_score)
            m_new=jnp.maximum(m,jnp.max(s,axis=0,keepdims=True))
            p=jnp.exp(s-m_new).astype(jnp.bfloat16)
            acc=acc*jnp.exp(m-m_new)+dot(vt_ref[n,:,rows],p,NN)
            out.append((m_new,acc))
        return tuple(out)
    init=tuple((jnp.full((1,block),masked_score,jnp.float32),jnp.zeros((HEAD_DIM+16,block),jnp.float32)) for _ in range(heads))
    a=firsts[i]//block
    b=jnp.clip((lasts[i]+block-1)//block,a,i)
    carry=lax.fori_loop(a,b,functools.partial(step,True),init)
    carry=lax.fori_loop(b,i,functools.partial(step,False),carry)
    carry=step(True,i,carry)
    outs=[]
    for n in range(heads):
        m,acc=carry[n]
        l=acc[HEAD_DIM:HEAD_DIM+1]
        outs.append(acc[:HEAD_DIM]/l)
        lse_ref[0,n:n+1,:]=m+jnp.log(l)
    o=outs[0] if heads==1 else jnp.concatenate(outs,axis=0)
    o_ref[...]=jnp.transpose(o).astype(o_ref.dtype)

def attend_forward2(q,k,v,start,block):
    length,width=q.shape
    lanes=min(128,width); groups=width//lanes; nq=length//block
    firsts=start[::block]; lasts=start[block-1::block]
    spec=pltpu.PrefetchScalarGridSpec(num_scalar_prefetch=2,grid=(groups,nq),
        in_specs=[pl.BlockSpec((block,lanes),lambda g,i,*_:(i,g)),
                  pl.BlockSpec((length,lanes),lambda g,i,*_:(0,g)),
                  pl.BlockSpec((length,lanes),lambda g,i,*_:(0,g)),
                  pl.BlockSpec((1,block),lambda g,i,*_:(0,i))],
        out_specs=[pl.BlockSpec((block,lanes),lambda g,i,*_:(i,g)),
                   pl.BlockSpec((1,8,block),lambda g,i,*_:(g,0,i))],
        scratch_shapes=[pltpu.VMEM((lanes//HEAD_DIM,HEAD_DIM+16,length),jnp.bfloat16)])
    return pl.pallas_call(functools.partial(fwd2_kernel,block),grid_spec=spec,
        out_shape=[jax.ShapeDtypeStruct((length,width),jnp.bfloat16),jax.ShapeDtypeStruct((groups,8,length),jnp.float32)],
        compiler_params=pltpu.CompilerParams(vmem_limit_bytes=48*1024*1024),
        cost_estimate=pl.CostEstimate(flops=4*length*length*width,bytes_accessed=8*length*width,transcendentals=length*length*width//HEAD_DIM),
        name="attend_forward")(firsts,lasts,q,k,v,start[None,:])

def backward_kernel(block,full_end,some_end,q_ref,k_ref,v_ref,d_ref,o_ref,lse_ref,start_ref,dq_ref,dk_ref,dv_ref,delta_ref):
    j=pl.program_id(1)
    length,lanes=q_ref.shape
    heads=lanes//HEAD_DIM
    @pl.when(j==0)
    def _():
        dq_ref[...]=jnp.zeros_like(dq_ref)
        def fill(i,_):
            rows=pl.ds(i*block,block)
            prod=jnp.transpose(d_ref[rows,:].astype(jnp.float32)*o_ref[rows,:].astype(jnp.float32))
            for n in range(heads):
                delta_ref[n:n+1,rows]=jnp.sum(prod[n*HEAD_DIM:(n+1)*HEAD_DIM],axis=0,keepdims=True)
            return 0
        for i in range(length//block): fill(i,0)
    k=k_ref[...]; v=v_ref[...]
    scale=HEAD_DIM**-0.5
    kl=[only_head(k,n,lanes) for n in range(heads)]
    ks=[x*jnp.asarray(scale,k.dtype) for x in kl]
    vs=[only_head(v,n,lanes) for n in range(heads)]
    key=j*block+lax.broadcasted_iota(jnp.int32,(block,block),0)
    col=lax.broadcasted_iota(jnp.int32,(block,block),1)
    def step(masked,i,carry):
        dk,dv=carry
        rows=pl.ds(pl.multiple_of(i*block,block),block)
        q=q_ref[rows,:]; d=d_ref[rows,:]
        if masked:
            allowed=(key<=col+i*block)&(key>=start_ref[0:1,rows])
        dq=None; pk=[];pv=[]
        for n in range(heads):
            s=dot(ks[n],q,NT)
            if masked: s=jnp.where(allowed,s,masked_score)
            p=jnp.exp(s-lse_ref[0,n:n+1,rows])
            dp=dot(vs[n],d,NT)
            ds=(p*(dp-delta_ref[n:n+1,rows])).astype(jnp.bfloat16)
            pv.append(dot(p.astype(jnp.bfloat16),d,NN))
            pk.append(dot(ds,q,NN))
            t=dot(ds,kl[n],TN)
            dq=t if dq is None else dq+t
        dq_ref[rows,:]+=dq*scale
        if heads==2:
            lane=lax.broadcasted_iota(jnp.int32,pv[0].shape,1)<HEAD_DIM
            return dk+jnp.where(lane,pk[0],pk[1]),dv+jnp.where(lane,pv[0],pv[1])
        return dk+pk[0],dv+pv[0]
    zero=jnp.zeros((block,lanes),jnp.float32)
    carry=step(True,j,(zero,zero))
    carry=lax.fori_loop(j+1,full_end[j],functools.partial(step,False),carry)
    carry=lax.fori_loop(full_end[j],some_end[j],functools.partial(step,True),carry)
    dk_ref[...]=carry[0]*scale
    dv_ref[...]=carry[1]

def attend_backward(q,k,v,d,o,lse,start,block):
    length,width=q.shape
    lanes=min(128,width); groups=width//lanes; n=length//block
    lasts=start[block-1::block]
    edge=jnp.arange(n,dtype=jnp.int32)
    full_end=jnp.maximum(edge+1,jnp.sum((lasts[None,:]<=edge[:,None]*block).astype(jnp.int32),axis=1))
    reach=jnp.sum((start[None,:]<=edge[:,None]*block+block-1).astype(jnp.int32),axis=1)
    some_end=jnp.maximum(full_end,(reach+block-1)//block)
    whole=pl.BlockSpec((length,lanes),lambda g,j,*_:(0,g))
    part=pl.BlockSpec((block,lanes),lambda g,j,*_:(j,g))
    spec=pltpu.PrefetchScalarGridSpec(num_scalar_prefetch=2,grid=(groups,n),
        in_specs=[whole,part,part,whole,whole,pl.BlockSpec((1,8,length),lambda g,j,*_:(g,0,0)),pl.BlockSpec((1,length),lambda g,j,*_:(0,0))],
        out_specs=[whole,part,part],
        scratch_shapes=[pltpu.VMEM((8,length),jnp.float32)])
    return pl.pallas_call(functools.partial(backward_kernel,block),grid_spec=spec,
        out_shape=[jax.ShapeDtypeStruct((length,width),jnp.float32)]*3,
        compiler_params=pltpu.CompilerParams(vmem_limit_bytes=48*1024*1024),
        cost_estimate=pl.CostEstimate(flops=10*length*length*width,bytes_accessed=22*length*width,transcendentals=length*length*width//HEAD_DIM),
        name="attend_backward")(full_end,some_end,q,k,v,d,o,lse,start[None,:])


def on_device(
    tokens,
    first_values,
    segment_ids,
    positions,
    attn_gain,
    w_query,
    w_key,
    w_value,
    w_out,
    mlp_gain,
    w_gate,
    w_up,
    w_down,
    out_grad,
):
    width = w_query.shape[1]
    heads_here = width // HEAD_DIM
    length = segment_ids.shape[0]
    rows_here = tokens.shape[1]
    block = min(512, length)
    ff_here = w_gate.shape[1]
    residual = tokens.astype(jnp.float32)
    attn_scale = rms_scale(residual)
    attn_input = (residual * attn_scale * attn_gain).astype(jnp.bfloat16)
    w_project = jnp.concatenate([w_query, w_key, w_value], axis=1)
    piece = lax.all_gather(attn_input, "head", axis=0, tiled=True)
    count = piece.shape[0]
    joined = jnp.einsum("lrd,dh->lrh", piece, w_project, preferred_element_type=jnp.float32)
    query_part = joined[..., :width].reshape(count, rows_here, heads_here, HEAD_DIM)
    key_part = joined[..., width : 2 * width].reshape(count, rows_here, heads_here, HEAD_DIM)
    queries = (
        rotate(query_part, positions, 1.0).reshape(count, rows_here, width).astype(jnp.bfloat16)
    )
    keys = rotate(key_part, positions, 1.0).reshape(count, rows_here, width).astype(jnp.bfloat16)
    gathered, queries, keys, value_proj = (piece, queries, keys, joined[..., 2 * width :])
    firsts = first_values.astype(jnp.float32)
    blended = blend_weight * value_proj + (1.0 - blend_weight) * firsts
    blended_low = blended.astype(jnp.bfloat16)
    first_heads = firsts.reshape(length, rows_here, heads_here, HEAD_DIM)
    blend_heads = blended.reshape(length, rows_here, heads_here, HEAD_DIM)
    norm_local = jnp.stack(
        [
            jnp.sum(jnp.sqrt(jnp.sum(first_heads * first_heads, axis=-1))),
            jnp.sum(jnp.sqrt(jnp.sum(blend_heads * blend_heads, axis=-1))),
        ]
    )
    start = jnp.arange(length, dtype=jnp.int32) - positions[:, 0]
    query_rows = queries[:, 0]
    key_rows = keys[:, 0]
    value_rows = blended_low[:, 0]
    mixed, log_total = attend_forward2(query_rows, key_rows, value_rows, start, block)
    attn_mixed = mixed[:, None]
    part = attn_mixed
    attn_branch = lax.psum_scatter(
        jnp.einsum("lrh,hd->lrd", part, w_out, preferred_element_type=jnp.float32),
        "head",
        scatter_dimension=0,
        tiled=True,
    )
    hidden_state = residual + attn_branch
    mlp_scale = rms_scale(hidden_state)
    mlp_input = (hidden_state * mlp_scale * mlp_gain).astype(jnp.bfloat16)
    w_gate_up = jnp.concatenate([w_gate, w_up], axis=1)
    piece = lax.all_gather(mlp_input, "mlp", axis=1, tiled=True)
    joined = jnp.einsum("lrd,df->lrf", piece, w_gate_up, preferred_element_type=jnp.float32)
    gate = joined[..., :ff_here]
    up = joined[..., ff_here:]
    expand_hidden = (jax.nn.silu(gate) * up).astype(jnp.bfloat16)
    mlp_gathered = piece
    down_terms = jnp.einsum(
        "lrf,fd->lrd", expand_hidden, w_down, preferred_element_type=jnp.float32
    )
    mlp_branch = lax.psum_scatter(
        down_terms.astype(jnp.bfloat16), "mlp", scatter_dimension=1, tiled=True
    ).astype(jnp.float32)
    output = (hidden_state + mlp_branch).astype(jnp.bfloat16)
    piece = lax.all_gather(out_grad, "mlp", axis=1, tiled=True)
    down_sum = jnp.einsum("lrf,lrd->fd", expand_hidden, piece, preferred_element_type=jnp.float32)
    part_grad = jnp.einsum("lrd,fd->lrf", piece, w_down, preferred_element_type=jnp.float32)
    hidden_grad = part_grad
    gate, up = (gate, up)
    sigma = jax.nn.sigmoid(gate)
    gate_grad = (hidden_grad * up * sigma * (1.0 + gate * (1.0 - sigma))).astype(jnp.bfloat16)
    up_grad = (hidden_grad * gate * sigma).astype(jnp.bfloat16)
    gate_up_grad = jnp.concatenate([gate_grad, up_grad], axis=-1)
    gate_up_wgrad = jnp.einsum(
        "lrd,lrf->df", mlp_gathered, gate_up_grad, preferred_element_type=jnp.float32
    )
    input_terms = jnp.einsum(
        "lrf,df->lrd", gate_up_grad, w_gate_up, preferred_element_type=jnp.float32
    )
    mlp_normed_grad = lax.psum_scatter(
        input_terms.astype(jnp.bfloat16), "mlp", scatter_dimension=1, tiled=True
    ).astype(jnp.float32)
    state_norm_grad, mlp_gain_grad = norm_back(hidden_state, mlp_scale, mlp_gain, mlp_normed_grad)
    state_grad = out_grad.astype(jnp.float32) + state_norm_grad
    state_grad_low = state_grad.astype(jnp.bfloat16)
    piece = lax.all_gather(state_grad_low, "head", axis=0, tiled=True)
    out_sum = jnp.einsum("lrh,lrd->hd", attn_mixed, piece, preferred_element_type=jnp.float32)
    part_grad = jnp.einsum("lrd,hd->lrh", piece, w_out, preferred_element_type=jnp.float32)
    out_wgrad = out_sum
    mixed_grad_low = part_grad.astype(jnp.bfloat16)
    query_grad, key_grad, blend_grad = attend_backward(
        query_rows, key_rows, value_rows, mixed_grad_low[:, 0], mixed, log_total, start, block
    )
    query_grad = query_grad.reshape(length, rows_here, heads_here, HEAD_DIM)
    key_grad = key_grad.reshape(length, rows_here, heads_here, HEAD_DIM)
    blend_low = blend_grad[:, None].astype(jnp.bfloat16)
    query_pre = (
        rotate(query_grad, positions, -1.0).reshape(length, rows_here, width).astype(jnp.bfloat16)
    )
    key_pre = (
        rotate(key_grad, positions, -1.0).reshape(length, rows_here, width).astype(jnp.bfloat16)
    )
    value_pre = (blend_weight * blend_low.astype(jnp.float32)).astype(jnp.bfloat16)
    first_values_grad = ((1.0 - blend_weight) * blend_low.astype(jnp.float32)).astype(jnp.bfloat16)
    proj_grad = jnp.concatenate([query_pre, key_pre, value_pre], axis=-1)
    proj_wgrad = jnp.einsum("lrd,lrh->dh", gathered, proj_grad, preferred_element_type=jnp.float32)
    part = proj_grad
    attn_normed_grad = lax.psum_scatter(
        jnp.einsum("lrh,dh->lrd", part, w_project, preferred_element_type=jnp.float32).astype(
            jnp.bfloat16
        ),
        "head",
        scatter_dimension=0,
        tiled=True,
    ).astype(jnp.float32)
    input_norm_grad, attn_gain_grad = norm_back(residual, attn_scale, attn_gain, attn_normed_grad)
    input_grad = (state_grad + input_norm_grad).astype(jnp.bfloat16)
    query_wgrad, key_wgrad, value_wgrad, out_wgrad = (
        lax.psum(proj_wgrad[:, :width].astype(jnp.bfloat16), ("dp", "mlp")).astype(jnp.float32),
        lax.psum(proj_wgrad[:, width : 2 * width].astype(jnp.bfloat16), ("dp", "mlp")).astype(
            jnp.float32
        ),
        lax.psum(proj_wgrad[:, 2 * width :].astype(jnp.bfloat16), ("dp", "mlp")).astype(
            jnp.float32
        ),
        lax.psum(out_wgrad.astype(jnp.bfloat16), ("dp", "mlp")).astype(jnp.float32),
    )
    gate_wgrad, up_wgrad, down_wgrad = (
        lax.psum(gate_up_wgrad[:, :ff_here].astype(jnp.bfloat16), ("dp", "head")).astype(
            jnp.float32
        ),
        lax.psum(gate_up_wgrad[:, ff_here:].astype(jnp.bfloat16), ("dp", "head")).astype(
            jnp.float32
        ),
        lax.psum(down_sum.astype(jnp.bfloat16), ("dp", "head")).astype(jnp.float32),
    )
    attn_gain_total, mlp_gain_total, norm_total = lax.psum(
        (attn_gain_grad, mlp_gain_grad, norm_local), ("dp", "head", "mlp")
    )
    count_all = (
        length
        * rows_here
        * heads_here
        * lax.axis_size("dp")
        * lax.axis_size("head")
        * lax.axis_size("mlp")
    )
    value_norms = norm_total / count_all
    return (
        output,
        input_grad,
        first_values_grad,
        attn_gain_total,
        query_wgrad,
        key_wgrad,
        value_wgrad,
        out_wgrad,
        mlp_gain_total,
        gate_wgrad,
        up_wgrad,
        down_wgrad,
        value_norms,
    )


def solution(mesh):
    placed = (
        P("head", ("dp", "mlp"), None),
        P(None, ("dp", "mlp"), "head"),
        P(None, ("dp", "mlp")),
        P(None, ("dp", "mlp")),
        P(),
        P(None, "head"),
        P(None, "head"),
        P(None, "head"),
        P("head", None),
        P(),
        P(None, "mlp"),
        P(None, "mlp"),
        P("mlp", None),
        P("head", ("dp", "mlp"), None),
    )
    return jax.shard_map(
        on_device,
        mesh=mesh,
        in_specs=placed,
        out_specs=(
            P("head", ("dp", "mlp"), None),
            P("head", ("dp", "mlp"), None),
            P(None, ("dp", "mlp"), "head"),
            P(),
            P(None, "head"),
            P(None, "head"),
            P(None, "head"),
            P("head", None),
            P(),
            P(None, "mlp"),
            P(None, "mlp"),
            P("mlp", None),
            P(),
        ),
        check_vma=False,
    )
```

```python
import functools

import jax
import jax.numpy as jnp
from jax import lax
from jax.experimental import pallas as pl
from jax.experimental.pallas import tpu as pltpu
from jax.sharding import PartitionSpec as P

HEAD_DIM = 64
epsilon = 1e-06
theta_base = 10000.0
blend_weight = 0.5
masked_score = -1e30
NT=(((1,),(1,)),((),()))
NN=(((1,),(0,)),((),()))
TN=(((0,),(0,)),((),()))
def dot(a,b,dims): return lax.dot_general(a,b,dims,preferred_element_type=jnp.float32)

def head_lanes(lanes):
    return lanes//HEAD_DIM

def only_head(x,number,lanes,other=0.0):
    if lanes==HEAD_DIM: return x
    lane=lax.broadcasted_iota(jnp.int32,x.shape,1)
    return jnp.where(lane//HEAD_DIM==number,x,jnp.asarray(other,x.dtype))

def fwd2_kernel(block,firsts,lasts,q_ref,k_ref,v_ref,start_ref,o_ref,lse_ref,vt_ref):
    i=pl.program_id(1)
    length,lanes=k_ref.shape
    heads=lanes//HEAD_DIM
    @pl.when(i==0)
    def _():
        for r in range(length//block):
            rows=pl.ds(r*block,block)
            t=jnp.transpose(v_ref[rows,:])
            for n in range(heads):
                vt_ref[n,0:HEAD_DIM,rows]=t[n*HEAD_DIM:(n+1)*HEAD_DIM]
                vt_ref[n,HEAD_DIM:,rows]=jnp.ones((16,block),jnp.bfloat16)
    q=q_ref[...]*jnp.asarray(HEAD_DIM**-0.5,q_ref.dtype)
    qs=[only_head(q,n,lanes) for n in range(heads)]
    start=start_ref[...]
    key=lax.broadcasted_iota(jnp.int32,(block,block),0)
    col=i*block+lax.broadcasted_iota(jnp.int32,(block,block),1)
    def step(masked,j,carry):
        rows=pl.ds(pl.multiple_of(j*block,block),block)
        k=k_ref[rows,:]
        out=[]
        if masked:
            c=key+j*block
            allowed=(c<=col)&(c>=start)
        for n in range(heads):
            m,acc=carry[n]
            s=dot(k,qs[n],NT)
            if masked: s=jnp.where(allowed,s,masked_score)
            m_new=jnp.maximum(m,jnp.max(s,axis=0,keepdims=True))
            p=jnp.exp(s-m_new).astype(jnp.bfloat16)
            acc=acc*jnp.exp(m-m_new)+dot(vt_ref[n,:,rows],p,NN)
            out.append((m_new,acc))
        return tuple(out)
    init=tuple((jnp.full((1,block),masked_score,jnp.float32),jnp.zeros((HEAD_DIM+16,block),jnp.float32)) for _ in range(heads))
    a=firsts[i]//block
    b=jnp.clip((lasts[i]+block-1)//block,a,i)
    carry=lax.fori_loop(a,b,functools.partial(step,True),init)
    carry=lax.fori_loop(b,i,functools.partial(step,False),carry)
    carry=step(True,i,carry)
    outs=[]
    for n in range(heads):
        m,acc=carry[n]
        l=acc[HEAD_DIM:HEAD_DIM+1]
        outs.append(acc[:HEAD_DIM]/l)
        lse_ref[0,n:n+1,:]=m+jnp.log(l)
    o=outs[0] if heads==1 else jnp.concatenate(outs,axis=0)
    o_ref[...]=jnp.transpose(o).astype(o_ref.dtype)

def attend_forward2(q,k,v,start,block):
    length,width=q.shape
    lanes=min(128,width); groups=width//lanes; nq=length//block
    firsts=start[::block]; lasts=start[block-1::block]
    spec=pltpu.PrefetchScalarGridSpec(num_scalar_prefetch=2,grid=(groups,nq),
        in_specs=[pl.BlockSpec((block,lanes),lambda g,i,*_:(i,g)),
                  pl.BlockSpec((length,lanes),lambda g,i,*_:(0,g)),
                  pl.BlockSpec((length,lanes),lambda g,i,*_:(0,g)),
                  pl.BlockSpec((1,block),lambda g,i,*_:(0,i))],
        out_specs=[pl.BlockSpec((block,lanes),lambda g,i,*_:(i,g)),
                   pl.BlockSpec((1,8,block),lambda g,i,*_:(g,0,i))],
        scratch_shapes=[pltpu.VMEM((lanes//HEAD_DIM,HEAD_DIM+16,length),jnp.bfloat16)])
    return pl.pallas_call(functools.partial(fwd2_kernel,block),grid_spec=spec,
        out_shape=[jax.ShapeDtypeStruct((length,width),jnp.bfloat16),jax.ShapeDtypeStruct((groups,8,length),jnp.float32)],
        compiler_params=pltpu.CompilerParams(vmem_limit_bytes=48*1024*1024),
        cost_estimate=pl.CostEstimate(flops=24*length*length*width,bytes_accessed=8*length*width,transcendentals=0),
        name="attend_forward")(firsts,lasts,q,k,v,start[None,:])

def backward_kernel(block,full_end,some_end,q_ref,k_ref,v_ref,d_ref,o_ref,lse_ref,start_ref,*rest):
    dq_ref,dk_ref,dv_ref,delta_ref=rest[-4:]
    j=pl.program_id(1)
    length,lanes=q_ref.shape
    heads=lanes//HEAD_DIM
    @pl.when(j==0)
    def _():
        dq_ref[...]=jnp.zeros_like(dq_ref)
        def fill(i,_):
            rows=pl.ds(i*block,block)
            prod=jnp.transpose(d_ref[rows,:].astype(jnp.float32)*o_ref[rows,:].astype(jnp.float32))
            for n in range(heads):
                delta_ref[n:n+1,rows]=jnp.sum(prod[n*HEAD_DIM:(n+1)*HEAD_DIM],axis=0,keepdims=True)
            return 0
        for i in range(length//block): fill(i,0)
    k=k_ref[...]; v=v_ref[...]
    scale=HEAD_DIM**-0.5
    kl=[only_head(k,n,lanes) for n in range(heads)]
    ks=[x*jnp.asarray(scale,k.dtype) for x in kl]
    vs=[only_head(v,n,lanes) for n in range(heads)]
    key=j*block+lax.broadcasted_iota(jnp.int32,(block,block),0)
    col=lax.broadcasted_iota(jnp.int32,(block,block),1)
    def step(masked,i,carry):
        dk,dv=carry
        rows=pl.ds(pl.multiple_of(i*block,block),block)
        q=q_ref[rows,:]; d=d_ref[rows,:]
        if masked:
            allowed=(key<=col+i*block)&(key>=start_ref[0:1,rows])
        dq=None; pk=[];pv=[]
        for n in range(heads):
            s=dot(ks[n],q,NT)
            if masked: s=jnp.where(allowed,s,masked_score)
            p=jnp.exp(s-lse_ref[0,n:n+1,rows])
            dp=dot(vs[n],d,NT)
            ds=(p*(dp-delta_ref[n:n+1,rows])).astype(jnp.bfloat16)
            pv.append(dot(p.astype(jnp.bfloat16),d,NN))
            pk.append(dot(ds,q,NN))
            t=dot(ds,kl[n],TN)
            dq=t if dq is None else dq+t
        dq_ref[rows,:]+=dq*scale
        if heads==2:
            lane=lax.broadcasted_iota(jnp.int32,pv[0].shape,1)<HEAD_DIM
            return dk+jnp.where(lane,pk[0],pk[1]),dv+jnp.where(lane,pv[0],pv[1])
        return dk+pk[0],dv+pv[0]
    zero=jnp.zeros((block,lanes),jnp.float32)
    carry=step(True,j,(zero,zero))
    carry=lax.fori_loop(j+1,full_end[j],functools.partial(step,False),carry)
    carry=lax.fori_loop(full_end[j],some_end[j],functools.partial(step,True),carry)
    dk_ref[...]=carry[0]*scale
    dv_ref[...]=carry[1]

def attend_backward(q,k,v,d,o,lse,start,block,group,earlier=()):
    length,width=q.shape
    lanes=min(128,width); n=length//block
    lasts=start[block-1::block]
    edge=jnp.arange(n,dtype=jnp.int32)
    full_end=jnp.maximum(edge+1,jnp.sum((lasts[None,:]<=edge[:,None]*block).astype(jnp.int32),axis=1))
    reach=jnp.sum((start[None,:]<=edge[:,None]*block+block-1).astype(jnp.int32),axis=1)
    some_end=jnp.maximum(full_end,(reach+block-1)//block)
    whole=pl.BlockSpec((length,lanes),lambda g,j,*_:(0,group))
    part=pl.BlockSpec((block,lanes),lambda g,j,*_:(j,group))
    spec=pltpu.PrefetchScalarGridSpec(num_scalar_prefetch=2,grid=(1,n),
        in_specs=[whole,part,part,whole,whole,pl.BlockSpec((1,8,length),lambda g,j,*_:(group,0,0)),pl.BlockSpec((1,length),lambda g,j,*_:(0,0))]+[pl.BlockSpec(memory_space=pl.ANY)]*len(earlier),
        out_specs=[pl.BlockSpec((length,lanes),lambda g,j,*_:(0,0))]+[pl.BlockSpec((block,lanes),lambda g,j,*_:(j,0))]*2,
        scratch_shapes=[pltpu.VMEM((8,length),jnp.float32)])
    return pl.pallas_call(functools.partial(backward_kernel,block),grid_spec=spec,
        out_shape=[jax.ShapeDtypeStruct((length,lanes),jnp.float32)]*3,
        compiler_params=pltpu.CompilerParams(vmem_limit_bytes=48*1024*1024),
        cost_estimate=pl.CostEstimate(flops=36*length*length*lanes,bytes_accessed=22*length*lanes,transcendentals=0),
        name="attend_backward")(full_end,some_end,q,k,v,d,o,lse,start[None,:],*earlier)


f32 = jnp.float32
bf16 = jnp.bfloat16
everywhere = pl.BlockSpec(memory_space=pl.ANY)


def swap(x, axis, mask):
    return lax.ppermute(x, axis, [(i, i ^ mask) for i in range(lax.axis_size(axis))])


def cut_of(rows):
    half = rows // 2
    return half - half % 8 if half >= 8 else half


def after(x, *earlier):
    def kernel(*refs):
        pass

    return pl.pallas_call(
        kernel,
        in_specs=[everywhere] * (1 + len(earlier)),
        out_specs=everywhere,
        out_shape=jax.ShapeDtypeStruct(x.shape, x.dtype),
        input_output_aliases={0: 0},
        name="after",
    )(x, *earlier)


def spread_relay(x, axis):
    count = lax.axis_size(axis)
    if count != 4:
        return [[x]] + [[swap(x, axis, e)] for e in range(1, count)]
    cut = cut_of(x.shape[0])
    one, two = swap(x, axis, 1), swap(x, axis, 2)
    return [[x], [one], [two], [swap(two[:cut], axis, 1), swap(one[cut:], axis, 2)]]


def spread(x, axis):
    return [x] + [swap(x, axis, e) for e in range(1, lax.axis_size(axis))]


def add_low(*terms):
    return sum(t.astype(f32) for t in terms).astype(bf16)


def collect(parts, axis):
    return sum((swap(p, axis, e) if e else p).astype(f32) for e, p in enumerate(parts))


def collect_relay(parts, axis, earlier):
    if lax.axis_size(axis) != 4:
        return collect(parts, axis), parts[0]
    own, one, two, three = parts
    cut = cut_of(own.shape[0])
    for_two = swap(three[:cut], axis, 1)
    for_one = swap(three[cut:], axis, 2)
    for_one, for_two = after(for_one, earlier), after(for_two, earlier)
    one = jnp.concatenate([one[:cut], add_low(one[cut:], for_one)])
    two = jnp.concatenate([add_low(two[:cut], for_two), two[cut:]])
    one_got, two_got = swap(one, axis, 1), swap(two, axis, 2)
    return own.astype(f32) + one_got.astype(f32) + two_got.astype(f32), two


def in_order(parts, rank):
    rows = parts[0].shape[0]
    whole = jnp.zeros((len(parts) * rows,) + parts[0].shape[1:], parts[0].dtype)
    for e, part in enumerate(parts):
        whole = lax.dynamic_update_slice_in_dim(whole, part, (rank ^ e) * rows, 0)
    return whole


def block_of(x, number, rows):
    return lax.dynamic_slice_in_dim(x, number * rows, rows, 0)


def both_cores(own, other, core):
    first = core == 0
    return jnp.concatenate([jnp.where(first, own, other), jnp.where(first, other, own)])


def sum_over_all(x):
    for axis in ("dp", "head", "mlp"):
        count = lax.axis_size(axis)
        if count == 4:
            x = (x + swap(x, axis, 1)) + (swap(x, axis, 2) + swap(x, axis, 3))
        else:
            mask = 1
            while mask < count:
                x = x + swap(x, axis, mask)
                mask *= 2
    return x


def rms_scale(rows):
    return lax.rsqrt(jnp.mean(rows * rows, axis=-1, keepdims=True) + epsilon)


def norm_back(rows, scale, gain, grad):
    weighted = grad * gain
    return scale * weighted - rows * scale * scale * scale * jnp.mean(
        weighted * rows, axis=-1, keepdims=True
    )


def turned(x, cosine, sine):
    half = HEAD_DIM // 2
    if x.shape[1] == HEAD_DIM:
        other = jnp.concatenate([x[:, half:], x[:, :half]], axis=1)
    else:
        lanes = x.shape[1]
        lane = lax.broadcasted_iota(jnp.int32, x.shape, 1)
        other = jnp.where(
            lane % HEAD_DIM < half, pltpu.roll(x, lanes - half, 1), pltpu.roll(x, half, 1)
        )
    return x * cosine + other * sine


def load_rows(refs, counts, number, target):
    at = 0
    for k, pieces in enumerate(counts):
        mine = refs[at : at + pieces]
        at += pieces

        @pl.when(number == k)
        def _(mine=mine):
            row = 0
            for ref in mine:
                target[row : row + ref.shape[0], :] = ref[...]
                row += ref.shape[0]


def project_kernel(counts, rank_ref, *refs):
    total = sum(counts)
    parts, (w_ref, gain_ref, cos_ref, sin_ref, first_ref) = refs[:total], refs[total : total + 5]
    a_ref, q_ref, k_ref, v_ref, norm_ref, rows_ref = refs[total + 5 :]
    e = pl.program_id(0)
    load_rows(parts, counts, e, rows_ref)
    x = rows_ref[...].astype(f32)
    a = (x * rms_scale(x) * gain_ref[...]).astype(bf16)
    a_ref[...] = a
    width = q_ref.shape[1]
    lanes = cos_ref.shape[1]
    cosine, sine = cos_ref[...], sin_ref[...]
    joined = dot(a, w_ref[...], NN)
    for g in range(width // lanes):
        at = slice(g * lanes, (g + 1) * lanes)
        q_ref[:, at] = turned(joined[:, at], cosine, sine).astype(bf16)
        at_k = slice(width + g * lanes, width + (g + 1) * lanes)
        k_ref[:, at] = turned(joined[:, at_k], cosine, sine).astype(bf16)
    first = first_ref[...].astype(f32)
    blended = blend_weight * joined[:, 2 * width :] + (1.0 - blend_weight) * first
    v_ref[...] = blended.astype(bf16)
    of = lax.broadcasted_iota(jnp.int32, (width, 128), 0) // HEAD_DIM
    one_hot = (of == lax.broadcasted_iota(jnp.int32, (width, 128), 1)).astype(f32)

    def norms(value):
        squares = lax.dot_general(
            value * value, one_hot, NN, precision=lax.Precision.HIGHEST, preferred_element_type=f32
        )
        return jnp.sum(jnp.sqrt(jnp.maximum(squares, 0.0)), axis=0, keepdims=True)

    @pl.when(e == 0)
    def _():
        norm_ref[...] = jnp.zeros_like(norm_ref)

    norm_ref[0:1, :] += norms(first)
    norm_ref[1:2, :] += norms(blended)


def spec_whole(x):
    return pl.BlockSpec(x.shape, lambda *_: (0,) * x.ndim)


def cost(us):
    return pl.CostEstimate(flops=int(us * 9e8), bytes_accessed=int(us * 1e5), transcendentals=0)


big = pltpu.CompilerParams(vmem_limit_bytes=56 * 1024 * 1024)


def project(rank, parts, weights, gain, cosine, sine, firsts):
    counts = tuple(len(p) for p in parts)
    flat = [x for p in parts for x in p]
    ranks, chunk = len(parts), parts[0][0].shape[0]
    length, width = firsts.shape
    model, lanes = flat[0].shape[1], cosine.shape[1]
    there = lambda e, r: (r[0] ^ e, 0)
    block = lambda n: pl.BlockSpec((chunk, n), there)
    spec = pltpu.PrefetchScalarGridSpec(
        num_scalar_prefetch=1,
        grid=(ranks,),
        in_specs=[spec_whole(x) for x in flat]
        + [spec_whole(weights), spec_whole(gain), block(lanes), block(lanes), block(width)],
        out_specs=[block(model), block(width), block(width), block(width)]
        + [pl.BlockSpec((8, 128), lambda e, r: (0, 0))],
        scratch_shapes=[pltpu.VMEM((chunk, model), bf16)],
    )
    low = jax.ShapeDtypeStruct((length, width), bf16)
    return pl.pallas_call(
        functools.partial(project_kernel, counts),
        grid_spec=spec,
        out_shape=[jax.ShapeDtypeStruct((length, model), bf16), low, low, low]
        + [jax.ShapeDtypeStruct((8, 128), f32)],
        compiler_params=big,
        cost_estimate=cost(9),
        name="project",
    )(rank[None], *flat, weights, gain, cosine, sine, firsts)


def feed_kernel(x_ref, g_ref, *refs):
    sources, (act_ref, in_ref, sum_ref) = (refs[0:3], refs[3:6], refs[6:9]), refs[-3:]
    f = pl.program_id(0)
    steps = pl.num_programs(0)

    @pl.when(f == 0)
    def _():
        sum_ref[...] = jnp.zeros_like(sum_ref)

    def work(gate_w, up_w, down_w):
        x, g = x_ref[...], g_ref[...]
        gate, up = dot(gate_w[...], x, NT), dot(up_w[...], x, NT)
        hidden_grad = dot(down_w[...], g, NT)
        sigma = 1.0 / (1.0 + jnp.exp(-gate))
        gate_sigma = gate * sigma
        hidden = (gate_sigma * up).astype(bf16)
        gate_grad = (hidden_grad * up * (sigma + gate_sigma * (1.0 - sigma))).astype(bf16)
        up_grad = (hidden_grad * gate_sigma).astype(bf16)
        act_ref[0, 0], act_ref[0, 1], act_ref[0, 2] = gate_grad, up_grad, hidden
        sum_ref[...] += dot(gate_grad, gate_w[...], TN) + dot(up_grad, up_w[...], TN)

    for k, condition in enumerate((f < 2, f == 2, f == 3)):

        @pl.when(condition)
        def _(k=k):
            work(*sources[k])

    @pl.when(f == steps - 1)
    def _():
        in_ref[...] = sum_ref[...].astype(in_ref.dtype)


def feed(x, grad, own, far, far_other, dtype, earlier=()):
    tokens, model = x.shape
    part = own.shape[0] // 6
    block = lambda at: pl.BlockSpec((part, model), at)
    return pl.pallas_call(
        feed_kernel,
        grid=(4,),
        in_specs=[spec_whole(x), spec_whole(grad)]
        + [block(lambda f, a=a: (2 * a + jnp.minimum(f, 1), 0)) for a in range(3)]
        + [block(lambda f, a=a: (a, 0)) for a in range(3)] * 2
        + [everywhere] * len(earlier),
        out_specs=[
            pl.BlockSpec((1, 3, part, tokens), lambda f: (f, 0, 0, 0)),
            pl.BlockSpec((tokens, model), lambda f: (0, 0)),
        ],
        out_shape=[
            jax.ShapeDtypeStruct((4, 3, part, tokens), bf16),
            jax.ShapeDtypeStruct((tokens, model), dtype),
        ],
        scratch_shapes=[pltpu.VMEM((tokens, model), f32)],
        compiler_params=big,
        cost_estimate=cost(14),
        name="feed",
    )(x, grad, *([own] * 3), *([far] * 3), *([far_other] * 3), *earlier)


def half_grads(act_ref, near_ref, x_ref, xn_ref, g_ref, gn_ref, result_ref):
    a = pl.program_id(0)

    @pl.when(a < 2)
    def _():
        result_ref[...] = dot(act_ref[0, 0], x_ref[...], NN) + dot(near_ref[0, 0], xn_ref[...], NN)

    @pl.when(a == 2)
    def _():
        result_ref[...] = dot(act_ref[0, 0], g_ref[...], NN) + dot(near_ref[0, 0], gn_ref[...], NN)


def other_grads_kernel(scalars, *refs):
    out_ref, result_ref = refs[-2:]
    half_grads(*refs[:6], result_ref)
    out_ref[...] = result_ref[...].astype(bf16)


def far_grads_kernel(ranks, scalars, *refs):
    got_ref, out_refs, result_ref = refs[6], refs[7 : 7 + ranks], refs[-1]
    half_grads(*refs[:6], result_ref)
    rows = result_ref.shape[0] // ranks
    for e in range(ranks):
        at = slice(e * rows, (e + 1) * rows)
        out_refs[e][0] = (result_ref[at, :] + got_ref[at, :].astype(f32)).astype(bf16)


def own_grads_kernel(ranks, scalars, *refs):
    got_ref, out_ref, out_got_ref = refs[6:9]
    own_refs, result_ref = refs[9 : 9 + ranks], refs[-1]
    half_grads(*refs[:6], result_ref)
    i = pl.program_id(0)
    rows = result_ref.shape[0] // ranks
    result_ref[...] += got_ref[...].astype(f32)

    @pl.when(i == 0)
    def _():
        for e in range(ranks):
            number = scalars[1] ^ e
            both = out_ref[number].astype(f32) + out_got_ref[number].astype(f32)
            own_refs[e][3 * rows :, :] = both.astype(bf16)

    for a in range(3):

        @pl.when(i == a)
        def _(a=a):
            to = slice(a * rows, (a + 1) * rows)
            for e in range(ranks):
                if rows % 8 == 0:
                    at = pl.ds(pl.multiple_of((scalars[1] ^ e) * rows, 8), rows)
                    own_refs[e][to, :] = result_ref[at, :].astype(bf16)
                else:
                    for h in range(ranks):

                        @pl.when(scalars[1] ^ e == h)
                        def _(e=e, h=h):
                            own_refs[e][to, :] = result_ref[h * rows : (h + 1) * rows, :].astype(bf16)


def shard_grads(scalars, ranks, far, here, near, x, x_near, grad, grad_near, got=None):
    _, _, part, tokens = here.shape
    model = x.shape[1]
    if got is None:
        number = lambda c: 3 if far else 1 - c[0]
    else:
        number = lambda c: 2 if far else c[0]
    act = pl.BlockSpec((1, 1, part, tokens), lambda i, c: (number(c), i, 0, 0))
    in_specs = [act, act] + [spec_whole(x)] * 4
    args = [here, near, x, x_near, grad, grad_near]
    row_block = pl.BlockSpec((part, model), lambda i, c: (i, 0))
    rows = part // ranks
    if got is None:
        kernel, out_specs = other_grads_kernel, row_block
        out_shape = jax.ShapeDtypeStruct((3 * part, model), bf16)
    elif far:
        kernel = functools.partial(far_grads_kernel, ranks)
        in_specs.append(row_block)
        args += got
        out_specs = [pl.BlockSpec((1, rows, model), lambda i, c: (i, 0, 0))] * ranks
        out_shape = [jax.ShapeDtypeStruct((3, rows, model), bf16)] * ranks
    else:
        kernel = functools.partial(own_grads_kernel, ranks)
        in_specs += [row_block] + [spec_whole(g) for g in got[1:]]
        args += got
        wide = 3 * rows + got[1].shape[1]
        out_specs = [pl.BlockSpec((wide, model), lambda i, c: (0, 0))] * ranks
        out_shape = [jax.ShapeDtypeStruct((wide, model), bf16)] * ranks
    spec = pltpu.PrefetchScalarGridSpec(
        num_scalar_prefetch=1,
        grid=(3,),
        in_specs=in_specs,
        out_specs=out_specs,
        scratch_shapes=[pltpu.VMEM((part, model), f32)],
    )
    return pl.pallas_call(
        kernel,
        grid_spec=spec,
        out_shape=out_shape,
        compiler_params=big,
        cost_estimate=cost(6),
        name=("far" if far else "own") + ("_other" if got is None else "_sum"),
    )(scalars, *args)


def down_kernel(here_ref, near_ref, own_ref, far_ref, other_ref, out_ref, out_near_ref, sum_ref):
    f = pl.program_id(0)
    steps = pl.num_programs(0)

    @pl.when(f == 0)
    def _():
        sum_ref[...] = jnp.zeros_like(sum_ref)

    for condition, ref in ((f < 2, own_ref), (f == 2, far_ref), (f == 3, other_ref)):

        @pl.when(condition)
        def _(ref=ref):
            sum_ref[0] += dot(here_ref[0, 0], ref[...], TN)
            sum_ref[1] += dot(near_ref[0, 0], ref[...], TN)

    @pl.when(f == steps - 1)
    def _():
        out_ref[...] = sum_ref[0]
        out_near_ref[...] = sum_ref[1].astype(bf16)


def down(here, near, own, far, far_other):
    steps, _, part, tokens = here.shape
    model = own.shape[1]
    act = pl.BlockSpec((1, 1, part, tokens), lambda f: (f, 2, 0, 0))
    return pl.pallas_call(
        down_kernel,
        grid=(steps,),
        in_specs=[act, act]
        + [pl.BlockSpec((part, model), lambda f: (4 + jnp.minimum(f, 1), 0))]
        + [pl.BlockSpec((part, model), lambda f: (2, 0))] * 2,
        out_specs=[pl.BlockSpec((tokens, model), lambda f: (0, 0))] * 2,
        out_shape=[
            jax.ShapeDtypeStruct((tokens, model), f32),
            jax.ShapeDtypeStruct((tokens, model), bf16),
        ],
        scratch_shapes=[pltpu.VMEM((2, tokens, model), f32)],
        compiler_params=big,
        cost_estimate=cost(8),
        name="down",
    )(here, near, own, far, far_other)


def unproject_kernel(counts, groups, rank_ref, *refs):
    total = sum(counts)
    parts = refs[:total]
    w_ref, cos_ref, sin_ref = refs[total : total + 3]
    grads = refs[total + 3 : total + 3 + 3 * groups]
    p_ref, first_ref, g_ref, gain_ref, rows_ref = refs[-5:]
    e = pl.program_id(0)
    load_rows(parts, counts, e, rows_ref)
    x = rows_ref[...].astype(f32)
    width, lanes = first_ref.shape[1], cos_ref.shape[1]
    cosine, sine = cos_ref[...], -sin_ref[...]
    for g in range(groups):
        dq_ref, dk_ref, dv_ref = grads[3 * g : 3 * g + 3]
        at = slice(g * lanes, (g + 1) * lanes)
        at_k = slice(width + g * lanes, width + (g + 1) * lanes)
        at_v = slice(2 * width + g * lanes, 2 * width + (g + 1) * lanes)
        p_ref[:, at] = turned(dq_ref[...], cosine, sine).astype(bf16)
        p_ref[:, at_k] = turned(dk_ref[...], cosine, sine).astype(bf16)
        blend = dv_ref[...].astype(bf16).astype(f32)
        p_ref[:, at_v] = (blend_weight * blend).astype(bf16)
        first_ref[:, at] = ((1.0 - blend_weight) * blend).astype(bf16)
    grad = dot(p_ref[...], w_ref[...], NT)
    g_ref[0] = grad.astype(bf16)

    @pl.when(e == 0)
    def _():
        gain_ref[...] = jnp.zeros_like(gain_ref)

    gain_ref[...] += jnp.sum(grad * (x * rms_scale(x)), axis=0, keepdims=True)


def unproject(rank, parts, weights, cosine, sine, grads, earlier):
    counts = tuple(len(p) for p in parts)
    flat = [x for p in parts for x in p]
    ranks, chunk = len(parts), parts[0][0].shape[0]
    length, lanes = grads[0].shape
    groups = len(grads) // 3
    width, model = groups * lanes, flat[0].shape[1]
    there = lambda e, r: (r[0] ^ e, 0)
    block = lambda n: pl.BlockSpec((chunk, n), there)
    spec = pltpu.PrefetchScalarGridSpec(
        num_scalar_prefetch=1,
        grid=(ranks,),
        in_specs=[spec_whole(x) for x in flat]
        + [spec_whole(weights), block(lanes), block(lanes)]
        + [block(lanes)] * (3 * groups)
        + [everywhere] * len(earlier),
        out_specs=[
            block(3 * width),
            block(width),
            pl.BlockSpec((1, chunk, model), lambda e, r: (e, 0, 0)),
            pl.BlockSpec((1, model), lambda e, r: (0, 0)),
        ],
        scratch_shapes=[pltpu.VMEM((chunk, model), bf16)],
    )
    return pl.pallas_call(
        functools.partial(unproject_kernel, counts, groups),
        grid_spec=spec,
        out_shape=[
            jax.ShapeDtypeStruct((length, 3 * width), bf16),
            jax.ShapeDtypeStruct((length, width), bf16),
            jax.ShapeDtypeStruct((ranks, chunk, model), bf16),
            jax.ShapeDtypeStruct((1, model), f32),
        ],
        compiler_params=big,
        cost_estimate=cost(12),
        name="unproject",
    )(rank[None], *flat, weights, cosine, sine, *grads, *earlier)


def on_device(
    tokens,
    first_values,
    segment_ids,
    positions,
    attn_gain,
    w_query,
    w_key,
    w_value,
    w_out,
    mlp_gain,
    w_gate,
    w_up,
    w_down,
    out_grad,
):
    core, rank = lax.axis_index("dp"), lax.axis_index("head")
    ranks = lax.axis_size("head")
    chunk, width = tokens.shape[0], w_query.shape[1]
    model = tokens.shape[2]
    length, ff = segment_ids.shape[0], w_gate.shape[1]
    block = min(512, length)
    tokens, firsts, out_grad = tokens[:, 0], first_values[:, 0], out_grad[:, 0]
    places = positions[:, 0]
    start = jnp.arange(length, dtype=jnp.int32) - places

    row_parts = spread_relay(tokens, "head")

    part = ff // 2
    rows = part // ranks
    stack = jnp.concatenate([w_gate.T, w_up.T, w_down])
    cut_stack = stack.reshape(3, 2 * ranks, rows, model)
    far_piece = swap(
        lax.dynamic_index_in_dim(cut_stack, core * ranks + rank, 1, False), "mlp", 2
    ).reshape(3 * rows, model)
    out_grad_near = swap(out_grad, "mlp", 1)
    half_out = width // 2
    bundle = jnp.concatenate([far_piece, block_of(w_out, core, half_out)])
    bundle = after(bundle, *row_parts[-1])
    bundles = spread(bundle, "head")

    w_project = jnp.concatenate([w_query, w_key, w_value], axis=1)
    lanes = min(128, width)
    lane = jnp.arange(lanes)
    freq = theta_base ** (-(lane % (HEAD_DIM // 2)).astype(f32) * 2.0 / HEAD_DIM)
    angles = places.astype(f32)[:, None] * freq
    cosine = jnp.cos(angles)
    sine = jnp.sin(angles) * jnp.where(lane % HEAD_DIM < HEAD_DIM // 2, -1.0, 1.0)
    gathered, queries, keys, values, norms = project(
        rank, row_parts, w_project, attn_gain[None], cosine, sine, firsts
    )
    mixed, log_total = attend_forward2(queries, keys, values, start, block)

    mixed_here = lax.all_to_all(mixed, "head", 0, 0, tiled=True).reshape(ranks, chunk, width)

    bundles = [bundles[0]] + [after(b, mixed) for b in bundles[1:]]
    far_half = jnp.stack([b[: 3 * rows].reshape(3, rows, model) for b in bundles], axis=1)
    far_half = far_half.reshape(3 * part, model)
    out_half = in_order([b[3 * rows :] for b in bundles], rank).reshape(ranks, half_out, model)
    far_other, out_other = swap(far_half, "dp", 1), swap(out_half, "dp", 1)
    first = core == 0
    out_all = jnp.concatenate(
        [jnp.where(first, out_half, out_other), jnp.where(first, out_other, out_half)], axis=1
    )

    residual = tokens.astype(f32)
    hidden_state = residual + jnp.einsum("htk,hkd->td", mixed_here, out_all, preferred_element_type=f32)
    mlp_scale = rms_scale(hidden_state)
    mlp_input = (hidden_state * mlp_scale * mlp_gain).astype(bf16)
    mlp_input_near = swap(mlp_input, "mlp", 1)

    acts, terms = feed(mlp_input, out_grad, stack, far_half, far_other, f32)
    acts_near, terms_near = feed(
        mlp_input_near, out_grad_near, stack, far_half, far_other, bf16, (terms,)
    )
    terms_back = swap(terms_near, "mlp", 1)
    scalars = jnp.stack([core, rank]).astype(jnp.int32)
    tokens_two = (acts, acts_near, mlp_input, mlp_input_near, out_grad, out_grad_near)
    far_other_grads = shard_grads(scalars, ranks, True, *tokens_two)
    own_other_grads = shard_grads(scalars, ranks, False, *tokens_two)
    far_half_got = swap(far_other_grads, "dp", 1)
    own_half_got = swap(after(own_other_grads, far_half_got), "dp", 1)
    down_here, down_near = down(acts, acts_near, stack, far_half, far_other)

    far_chip = shard_grads(scalars, ranks, True, *tokens_two, [far_half_got])
    far_got = [swap(f, "head", e) for e, f in enumerate(far_chip) if e]
    mlp_normed_grad = after(terms_back, down_near, far_chip[0]).astype(f32) + terms
    mlp_gain_grad = jnp.sum(mlp_normed_grad * hidden_state * mlp_scale, axis=0)
    state_grad = out_grad.astype(f32) + norm_back(hidden_state, mlp_scale, mlp_gain, mlp_normed_grad)
    state_grad_low = state_grad.astype(bf16)

    mixed_grad = jnp.einsum(
        "td,hkd->htk", state_grad_low, out_all, preferred_element_type=f32
    ).astype(bf16)
    mixed_grad_rows = lax.all_to_all(mixed_grad, "head", 0, 0, tiled=True).reshape(length, width)

    out_grads = jnp.einsum(
        "htk,td->hkd", mixed_here, state_grad_low, preferred_element_type=f32
    ).astype(bf16).reshape(ranks, 2, half_out, model)
    out_got = swap(lax.dynamic_index_in_dim(out_grads, 1 - core, 1, False), "dp", 1)
    out_own = lax.dynamic_index_in_dim(out_grads, core, 1, False)
    far_sum = add_low(far_chip[0], *far_got)
    own_half_got = after(own_half_got, mixed_grad, far_sum)
    own_chip = shard_grads(scalars, ranks, False, *tokens_two, [own_half_got, out_own, out_got])
    mixed_grad_rows = after(mixed_grad_rows, own_chip[0])
    down_back = swap(after(down_near, mixed_grad_rows), "mlp", 1)
    output = (hidden_state + down_back.astype(f32) + down_here).astype(bf16)

    far_here = swap(far_sum, "mlp", 2)
    own_chip = [own_chip[0]] + [after(f, mixed_grad_rows) for f in own_chip[1:]]
    own_got = [swap(f, "head", e) for e, f in enumerate(own_chip) if e]
    grads = []
    earlier = (far_sum, *own_chip[1:])
    for g in range(width // lanes):
        grads += attend_backward(
            queries, keys, values, mixed_grad_rows, mixed, log_total, start, block, g, earlier
        )
        earlier = (grads[-1],)
    own_sum = sum(f.astype(f32) for f in (own_chip[0], *own_got))
    piece_sum = add_low(own_sum[: 3 * rows].reshape(3, rows, model), far_here)
    out_sum = own_sum[3 * rows :].astype(bf16)

    proj_grad, first_values_grad, normed, attn_gain_grad = unproject(
        rank, row_parts, w_project, cosine, sine, grads, (piece_sum,)
    )
    pieces = spread(piece_sum, "head")
    half_sum = jnp.zeros((3, ranks, rows, model), bf16)
    for e, piece in enumerate(pieces):
        half_sum = lax.dynamic_update_slice_in_dim(half_sum, piece[:, None], rank ^ e, 1)
    half_sum = half_sum.reshape(3, part, model)
    other_sum = swap(half_sum, "dp", 1)
    ff_grads = jnp.concatenate(
        [jnp.where(first, half_sum, other_sum), jnp.where(first, other_sum, half_sum)], axis=1
    ).astype(f32)
    gate_wgrad, up_wgrad, down_wgrad = ff_grads[0].T, ff_grads[1].T, ff_grads[2]

    proj_wgrad = dot(gathered, proj_grad, TN).astype(bf16)
    half_proj = model // 2
    proj_mine = add_low(
        block_of(proj_wgrad, core, half_proj),
        swap(block_of(proj_wgrad, 1 - core, half_proj), "dp", 1),
    )
    attn_normed_grad, last = collect_relay([normed[e] for e in range(ranks)], "head", proj_mine)
    input_grad = (
        state_grad + norm_back(residual, rms_scale(residual), attn_gain, attn_normed_grad)
    ).astype(bf16)
    line, count = lax.axis_index("mlp"), lax.axis_size("mlp")

    def over_line(x):
        part = x.shape[0] // count
        piece = collect([block_of(x, line ^ e, part) for e in range(count)], "mlp").astype(bf16)
        got = spread(piece, "mlp")
        return in_order(got, line), got[-1]

    proj_half, proj_last = over_line(proj_mine)
    proj_sum = both_cores(proj_half, swap(proj_half, "dp", 1), core).astype(f32)
    out_half_sum, _ = over_line(after(out_sum, proj_last))
    out_wgrad = both_cores(out_half_sum, swap(out_half_sum, "dp", 1), core).astype(f32)

    norm_row = jnp.zeros((model,), f32).at[:2].set(jnp.sum(norms[:2], axis=1))
    small = sum_over_all(after(jnp.stack([attn_gain_grad[0], mlp_gain_grad, norm_row]), proj_last))
    devices = lax.axis_size("dp") * ranks * count
    value_norms = small[2, :2] / (length * (width // HEAD_DIM) * devices)
    return (
        output[:, None],
        input_grad[:, None],
        first_values_grad[:, None],
        small[0],
        proj_sum[:, :width],
        proj_sum[:, width : 2 * width],
        proj_sum[:, 2 * width :],
        out_wgrad,
        small[1],
        gate_wgrad,
        up_wgrad,
        down_wgrad,
        value_norms,
    )


def solution(mesh):
    placed = (
        P("head", ("dp", "mlp"), None),
        P(None, ("dp", "mlp"), "head"),
        P(None, ("dp", "mlp")),
        P(None, ("dp", "mlp")),
        P(),
        P(None, "head"),
        P(None, "head"),
        P(None, "head"),
        P("head", None),
        P(),
        P(None, "mlp"),
        P(None, "mlp"),
        P("mlp", None),
        P("head", ("dp", "mlp"), None),
    )
    return jax.shard_map(
        on_device,
        mesh=mesh,
        in_specs=placed,
        out_specs=(
            P("head", ("dp", "mlp"), None),
            P("head", ("dp", "mlp"), None),
            P(None, ("dp", "mlp"), "head"),
            P(),
            P(None, "head"),
            P(None, "head"),
            P(None, "head"),
            P("head", None),
            P(),
            P(None, "mlp"),
            P(None, "mlp"),
            P("mlp", None),
            P(),
        ),
        check_vma=False,
    )
```

```python
import functools

import jax
import jax.numpy as jnp
from jax import lax
from jax.experimental import pallas as pl
from jax.experimental.pallas import tpu as pltpu
from jax.sharding import PartitionSpec as P

HEAD_DIM = 64
epsilon = 1e-06
theta_base = 10000.0
blend_weight = 0.5
masked_score = -1e30
NT=(((1,),(1,)),((),()))
NN=(((1,),(0,)),((),()))
TN=(((0,),(0,)),((),()))
def dot(a,b,dims): return lax.dot_general(a,b,dims,preferred_element_type=jnp.float32)

def head_lanes(lanes):
    return lanes//HEAD_DIM

def only_head(x,number,lanes,other=0.0):
    if lanes==HEAD_DIM: return x
    lane=lax.broadcasted_iota(jnp.int32,x.shape,1)
    return jnp.where(lane//HEAD_DIM==number,x,jnp.asarray(other,x.dtype))

def fwd2_kernel(block,firsts,lasts,q_ref,k_ref,v_ref,start_ref,*rest):
    o_ref,lse_ref,vt_ref=rest[-3:]
    i=pl.program_id(1)
    length,lanes=k_ref.shape
    heads=lanes//HEAD_DIM
    @pl.when(i==0)
    def _():
        for r in range(length//block):
            rows=pl.ds(r*block,block)
            t=jnp.transpose(v_ref[rows,:])
            for n in range(heads):
                vt_ref[n,0:HEAD_DIM,rows]=t[n*HEAD_DIM:(n+1)*HEAD_DIM]
                vt_ref[n,HEAD_DIM:,rows]=jnp.ones((16,block),jnp.bfloat16)
    q=q_ref[...]*jnp.asarray(HEAD_DIM**-0.5,q_ref.dtype)
    qs=[only_head(q,n,lanes) for n in range(heads)]
    start=start_ref[...]
    key=lax.broadcasted_iota(jnp.int32,(block,block),0)
    col=i*block+lax.broadcasted_iota(jnp.int32,(block,block),1)
    def step(masked,j,carry):
        rows=pl.ds(pl.multiple_of(j*block,block),block)
        k=k_ref[rows,:]
        out=[]
        if masked:
            c=key+j*block
            allowed=(c<=col)&(c>=start)
        for n in range(heads):
            m,acc=carry[n]
            s=dot(k,qs[n],NT)
            if masked: s=jnp.where(allowed,s,masked_score)
            m_new=jnp.maximum(m,jnp.max(s,axis=0,keepdims=True))
            p=jnp.exp(s-m_new).astype(jnp.bfloat16)
            acc=acc*jnp.exp(m-m_new)+dot(vt_ref[n,:,rows],p,NN)
            out.append((m_new,acc))
        return tuple(out)
    init=tuple((jnp.full((1,block),masked_score,jnp.float32),jnp.zeros((HEAD_DIM+16,block),jnp.float32)) for _ in range(heads))
    a=firsts[i]//block
    b=jnp.clip((lasts[i]+block-1)//block,a,i)
    carry=lax.fori_loop(a,b,functools.partial(step,True),init)
    carry=lax.fori_loop(b,i,functools.partial(step,False),carry)
    carry=step(True,i,carry)
    outs=[]
    for n in range(heads):
        m,acc=carry[n]
        l=acc[HEAD_DIM:HEAD_DIM+1]
        outs.append(acc[:HEAD_DIM]/l)
        lse_ref[0,n:n+1,:]=m+jnp.log(l)
    o=outs[0] if heads==1 else jnp.concatenate(outs,axis=0)
    o_ref[...]=jnp.transpose(o).astype(o_ref.dtype)

def attend_forward2(q,k,v,start,block,group,earlier=()):
    length,width=q.shape
    lanes=min(128,width); nq=length//block
    firsts=start[::block]; lasts=start[block-1::block]
    spec=pltpu.PrefetchScalarGridSpec(num_scalar_prefetch=2,grid=(1,nq),
        in_specs=[pl.BlockSpec((block,lanes),lambda g,i,*_:(i,group)),
                  pl.BlockSpec((length,lanes),lambda g,i,*_:(0,group)),
                  pl.BlockSpec((length,lanes),lambda g,i,*_:(0,group)),
                  pl.BlockSpec((1,block),lambda g,i,*_:(0,i))]+[pl.BlockSpec(memory_space=pl.ANY)]*len(earlier),
        out_specs=[pl.BlockSpec((block,lanes),lambda g,i,*_:(i,g)),
                   pl.BlockSpec((1,8,block),lambda g,i,*_:(g,0,i))],
        scratch_shapes=[pltpu.VMEM((lanes//HEAD_DIM,HEAD_DIM+16,length),jnp.bfloat16)])
    return pl.pallas_call(functools.partial(fwd2_kernel,block),grid_spec=spec,
        out_shape=[jax.ShapeDtypeStruct((length,lanes),jnp.bfloat16),jax.ShapeDtypeStruct((1,8,length),jnp.float32)],
        compiler_params=pltpu.CompilerParams(vmem_limit_bytes=60*1024*1024),
        cost_estimate=pl.CostEstimate(flops=29*length*length*lanes,bytes_accessed=8*length*lanes,transcendentals=0),
        name="attend_forward")(firsts,lasts,q,k,v,start[None,:],*earlier)

def backward_kernel(block,full_end,some_end,q_ref,k_ref,v_ref,d_ref,o_ref,lse_ref,start_ref,cos_ref,sin_ref,*rest):
    p_ref,first_ref,dq_ref,delta_ref=rest[-4:]
    j=pl.program_id(1)
    length,lanes=q_ref.shape
    heads=lanes//HEAD_DIM
    @pl.when(j==0)
    def _():
        dq_ref[...]=jnp.zeros_like(dq_ref)
        for i in range(length//block):
            rows=pl.ds(i*block,block)
            prod=jnp.transpose(d_ref[rows,:].astype(jnp.float32)*o_ref[rows,:].astype(jnp.float32))
            for n in range(heads):
                delta_ref[n:n+1,rows]=jnp.sum(prod[n*HEAD_DIM:(n+1)*HEAD_DIM],axis=0,keepdims=True)
    k=k_ref[...]; v=v_ref[...]
    scale=HEAD_DIM**-0.5
    kl=[only_head(k,n,lanes) for n in range(heads)]
    ks=[x*jnp.asarray(scale,k.dtype) for x in kl]
    vs=[only_head(v,n,lanes) for n in range(heads)]
    key=j*block+lax.broadcasted_iota(jnp.int32,(block,block),0)
    col=lax.broadcasted_iota(jnp.int32,(block,block),1)
    def step(masked,i,carry):
        dk,dv=carry
        rows=pl.ds(pl.multiple_of(i*block,block),block)
        q=q_ref[rows,:]; d=d_ref[rows,:]
        if masked:
            allowed=(key<=col+i*block)&(key>=start_ref[0:1,rows])
        dq=None; pk=[];pv=[]
        for n in range(heads):
            s=dot(ks[n],q,NT)
            if masked: s=jnp.where(allowed,s,masked_score)
            p=jnp.exp(s-lse_ref[0,n:n+1,rows])
            dp=dot(vs[n],d,NT)
            ds=(p*(dp-delta_ref[n:n+1,rows])).astype(jnp.bfloat16)
            pv.append(dot(p.astype(jnp.bfloat16),d,NN))
            pk.append(dot(ds,q,NN))
            t=dot(ds,kl[n],TN)
            dq=t if dq is None else dq+t
        dq_ref[rows,:]+=dq*scale
        if heads==2:
            lane=lax.broadcasted_iota(jnp.int32,pv[0].shape,1)<HEAD_DIM
            return dk+jnp.where(lane,pk[0],pk[1]),dv+jnp.where(lane,pv[0],pv[1])
        return dk+pk[0],dv+pv[0]
    zero=jnp.zeros((block,lanes),jnp.float32)
    carry=step(True,j,(zero,zero))
    carry=lax.fori_loop(j+1,full_end[j],functools.partial(step,False),carry)
    dk,dv=lax.fori_loop(full_end[j],some_end[j],functools.partial(step,True),carry)
    here=pl.ds(pl.multiple_of(j*block,block),block)
    p_ref[here,lanes:2*lanes]=turned(dk*scale,cos_ref[here,:],-sin_ref[here,:]).astype(jnp.bfloat16)
    blend=dv.astype(jnp.bfloat16).astype(jnp.float32)
    p_ref[here,2*lanes:]=(blend_weight*blend).astype(jnp.bfloat16)
    first_ref[...]=((1.0-blend_weight)*blend).astype(jnp.bfloat16)
    @pl.when(j==pl.num_programs(1)-1)
    def _():
        for i in range(length//block):
            rows=pl.ds(i*block,block)
            p_ref[rows,:lanes]=turned(dq_ref[rows,:],cos_ref[rows,:],-sin_ref[rows,:]).astype(jnp.bfloat16)

def attend_backward(q,k,v,d,start,cosine,sine,block,group,o,lse,before=(),earlier=()):
    length,width=q.shape
    lanes=cosine.shape[1]; n=length//block
    lasts=start[block-1::block]
    edge=jnp.arange(n,dtype=jnp.int32)
    full_end=jnp.maximum(edge+1,jnp.sum((lasts[None,:]<=edge[:,None]*block).astype(jnp.int32),axis=1))
    reach=jnp.sum((start[None,:]<=edge[:,None]*block+block-1).astype(jnp.int32),axis=1)
    some_end=jnp.maximum(full_end,(reach+block-1)//block)
    whole=pl.BlockSpec((length,lanes),lambda g,j,*_:(0,group))
    part=pl.BlockSpec((block,lanes),lambda g,j,*_:(j,group))
    table=pl.BlockSpec((length,lanes),lambda g,j,*_:(0,0))
    more=list(earlier)+list(before)
    spec=pltpu.PrefetchScalarGridSpec(num_scalar_prefetch=2,grid=(1,n),
        in_specs=[whole,part,part,whole,table,pl.BlockSpec((1,8,length),lambda g,j,*_:(0,0,0)),pl.BlockSpec((1,length),lambda g,j,*_:(0,0)),table,table]+[pl.BlockSpec(memory_space=pl.ANY)]*len(more),
        out_specs=[pl.BlockSpec((length,3*lanes),lambda g,j,*_:(0,group)),part],
        scratch_shapes=[pltpu.VMEM((length,lanes),jnp.float32),pltpu.VMEM((8,length),jnp.float32)])
    return pl.pallas_call(functools.partial(backward_kernel,block),grid_spec=spec,
        out_shape=[jax.ShapeDtypeStruct((length,3*width),jnp.bfloat16),jax.ShapeDtypeStruct((length,width),jnp.bfloat16)],
        input_output_aliases={11+len(earlier)+k:k for k in range(len(before))},
        compiler_params=pltpu.CompilerParams(vmem_limit_bytes=56*1024*1024),
        cost_estimate=pl.CostEstimate(flops=52*length*length*lanes,bytes_accessed=22*length*lanes,transcendentals=0),
        name="attend_backward")(full_end,some_end,q,k,v,d,o,lse,start[None,:],cosine,sine,*more)


f32 = jnp.float32
bf16 = jnp.bfloat16
everywhere = pl.BlockSpec(memory_space=pl.ANY)


def swap(x, axis, mask):
    return lax.ppermute(x, axis, [(i, i ^ mask) for i in range(lax.axis_size(axis))])


def cut_of(rows):
    half = rows // 2
    return half - half % 8 if half >= 8 else half


def after(x, *earlier):
    def kernel(*refs):
        pass

    return pl.pallas_call(
        kernel,
        in_specs=[everywhere] * (1 + len(earlier)),
        out_specs=everywhere,
        out_shape=jax.ShapeDtypeStruct(x.shape, x.dtype),
        input_output_aliases={0: 0},
        name="after",
    )(x, *earlier)


def spread_relay(x, axis):
    count = lax.axis_size(axis)
    if count != 4:
        return [[x]] + [[swap(x, axis, e)] for e in range(1, count)]
    cut = cut_of(x.shape[0])
    one, two = swap(x, axis, 1), swap(x, axis, 2)
    return [[x], [one], [two], [swap(two[:cut], axis, 1), swap(one[cut:], axis, 2)]]


def spread(x, axis):
    return [x] + [swap(x, axis, e) for e in range(1, lax.axis_size(axis))]


def add_low(*terms):
    return sum(t.astype(f32) for t in terms).astype(bf16)


def collect(parts, axis):
    return sum((swap(p, axis, e) if e else p).astype(f32) for e, p in enumerate(parts))


def in_order(parts, rank):
    rows = parts[0].shape[0]
    whole = jnp.zeros((len(parts) * rows,) + parts[0].shape[1:], parts[0].dtype)
    for e, part in enumerate(parts):
        whole = lax.dynamic_update_slice_in_dim(whole, part, (rank ^ e) * rows, 0)
    return whole


def block_of(x, number, rows):
    return lax.dynamic_slice_in_dim(x, number * rows, rows, 0)


def both_cores(own, other, core):
    first = core == 0
    return jnp.concatenate([jnp.where(first, own, other), jnp.where(first, other, own)])


def sum_over_all(x):
    for axis in ("dp", "head", "mlp"):
        mask = 1
        while mask < lax.axis_size(axis):
            x = x + swap(x, axis, mask)
            mask *= 2
    return x


def rms_scale(rows):
    return lax.rsqrt(jnp.mean(rows * rows, axis=-1, keepdims=True) + epsilon)


def norm_back(rows, scale, gain, grad):
    weighted = grad * gain
    return scale * weighted - rows * scale * scale * scale * jnp.mean(
        weighted * rows, axis=-1, keepdims=True
    )


def turned(x, cosine, sine):
    half = HEAD_DIM // 2
    if x.shape[1] == HEAD_DIM:
        other = jnp.concatenate([x[:, half:], x[:, :half]], axis=1)
    else:
        lanes = x.shape[1]
        lane = lax.broadcasted_iota(jnp.int32, x.shape, 1)
        other = jnp.where(
            lane % HEAD_DIM < half, pltpu.roll(x, lanes - half, 1), pltpu.roll(x, half, 1)
        )
    return x * cosine + other * sine


def load_rows(refs, counts, number, target):
    at = 0
    for k, pieces in enumerate(counts):
        mine = refs[at : at + pieces]
        at += pieces

        @pl.when(number == k)
        def _(mine=mine):
            row = 0
            for ref in mine:
                target[row : row + ref.shape[0], :] = ref[...]
                row += ref.shape[0]


def project_kernel(counts, rank_ref, *refs):
    total = sum(counts)
    parts, (w_ref, gain_ref, cos_ref, sin_ref, first_ref) = refs[:total], refs[total : total + 5]
    a_ref, q_ref, k_ref, v_ref, norm_ref, rows_ref = refs[-6:]
    i = pl.program_id(0)
    load_rows(parts, counts, i, rows_ref)
    x = rows_ref[...].astype(f32)
    a = (x * rms_scale(x) * gain_ref[...]).astype(bf16)
    a_ref[...] = a
    width = q_ref.shape[1]
    lanes = cos_ref.shape[1]
    cosine, sine = cos_ref[...], sin_ref[...]
    joined = dot(a, w_ref[...], NN)
    of = lax.broadcasted_iota(jnp.int32, (lanes, 128), 0) // HEAD_DIM
    one_hot = (of == lax.broadcasted_iota(jnp.int32, (lanes, 128), 1)).astype(f32)

    def norms(value):
        squares = lax.dot_general(
            value * value, one_hot, NN, precision=lax.Precision.HIGHEST, preferred_element_type=f32
        )
        return jnp.sum(jnp.sqrt(jnp.maximum(squares, 0.0)), axis=0, keepdims=True)

    @pl.when(i == 0)
    def _():
        norm_ref[...] = jnp.zeros_like(norm_ref)

    for g in range(width // lanes):
        at = slice(g * lanes, (g + 1) * lanes)
        query, key, value = (
            joined[:, (3 * g + k) * lanes : (3 * g + k + 1) * lanes] for k in range(3)
        )
        q_ref[:, at] = turned(query, cosine, sine).astype(bf16)
        k_ref[:, at] = turned(key, cosine, sine).astype(bf16)
        first = first_ref[:, at].astype(f32)
        blended = blend_weight * value + (1.0 - blend_weight) * first
        v_ref[:, at] = blended.astype(bf16)
        norm_ref[0:1, :] += norms(first)
        norm_ref[1:2, :] += norms(blended)


def spec_whole(x):
    return pl.BlockSpec(x.shape, lambda *_: (0,) * x.ndim)


def cost(us):
    return pl.CostEstimate(flops=int(us * 1.1e9), bytes_accessed=int(us * 1e5), transcendentals=0)


big = pltpu.CompilerParams(vmem_limit_bytes=56 * 1024 * 1024)


def project(rank, parts, base, weights, gain, cosine, sine, firsts, before=()):
    counts = tuple(len(p) for p in parts)
    flat = [x for p in parts for x in p]
    chunk = sum(x.shape[0] for x in parts[0])
    length, width = firsts.shape
    model, lanes = flat[0].shape[1], cosine.shape[1]
    there = lambda i, r: (r[0] ^ (base + i), 0)
    block = lambda n: pl.BlockSpec((chunk, n), there)
    spec = pltpu.PrefetchScalarGridSpec(
        num_scalar_prefetch=1,
        grid=(len(parts),),
        in_specs=[spec_whole(x) for x in flat]
        + [spec_whole(weights), spec_whole(gain), block(lanes), block(lanes), block(width)]
        + [everywhere] * len(before),
        out_specs=[block(model), block(width), block(width), block(width)]
        + [pl.BlockSpec((8, 128), lambda i, r: (0, 0))],
        scratch_shapes=[pltpu.VMEM((chunk, model), bf16)],
    )
    low = jax.ShapeDtypeStruct((length, width), bf16)
    return pl.pallas_call(
        functools.partial(project_kernel, counts),
        grid_spec=spec,
        out_shape=[jax.ShapeDtypeStruct((length, model), bf16), low, low, low]
        + [jax.ShapeDtypeStruct((8, 128), f32)],
        input_output_aliases={len(flat) + 6 + k: k for k in range(len(before))},
        compiler_params=big,
        cost_estimate=cost(4.5 * len(parts)),
        name="project",
    )(rank[None], *flat, weights, gain, cosine, sine, firsts, *before)


def assemble_kernel(ranks, rank_ref, *refs):
    far_ref, out_ref = refs[-2:]
    rows = far_ref.shape[2]
    e = pl.program_id(0)
    for k in range(ranks):

        @pl.when(e == k)
        def _(ref=refs[k]):
            for a in range(3):
                far_ref[a, 0] = ref[a * rows : (a + 1) * rows, :]
            out_ref[0] = ref[3 * rows :, :]


def assemble(rank, bundles, rows, earlier):
    ranks = len(bundles)
    wide, model = bundles[0].shape
    spec = pltpu.PrefetchScalarGridSpec(
        num_scalar_prefetch=1,
        grid=(ranks,),
        in_specs=[spec_whole(b) for b in bundles] + [everywhere] * len(earlier),
        out_specs=[
            pl.BlockSpec((3, 1, rows, model), lambda e, r: (0, e, 0, 0)),
            pl.BlockSpec((1, wide - 3 * rows, model), lambda e, r: (r[0] ^ e, 0, 0)),
        ],
    )
    return pl.pallas_call(
        functools.partial(assemble_kernel, ranks),
        grid_spec=spec,
        out_shape=[
            jax.ShapeDtypeStruct((3, ranks, rows, model), bf16),
            jax.ShapeDtypeStruct((ranks, wide - 3 * rows, model), bf16),
        ],
        compiler_params=big,
        cost_estimate=cost(3),
        name="assemble",
    )(rank[None], *bundles, *earlier)


def feed_kernel(x_ref, g_ref, *refs):
    sources, (act_ref, in_ref, sum_ref) = (refs[0:3], refs[3:6], refs[6:9]), refs[-3:]
    f = pl.program_id(0)
    steps = pl.num_programs(0)

    @pl.when(f == 0)
    def _():
        sum_ref[...] = jnp.zeros_like(sum_ref)

    def work(gate_w, up_w, down_w):
        x, g = x_ref[...], g_ref[...]
        gate, up = dot(gate_w[...], x, NT), dot(up_w[...], x, NT)
        hidden_grad = dot(down_w[...], g, NT)
        sigma = 1.0 / (1.0 + jnp.exp(-gate))
        gate_sigma = gate * sigma
        hidden = (gate_sigma * up).astype(bf16)
        gate_grad = (hidden_grad * up * (sigma + gate_sigma * (1.0 - sigma))).astype(bf16)
        up_grad = (hidden_grad * gate_sigma).astype(bf16)
        act_ref[0, 0], act_ref[0, 1], act_ref[0, 2] = gate_grad, up_grad, hidden
        sum_ref[...] += dot(gate_grad, gate_w[...], TN) + dot(up_grad, up_w[...], TN)

    for k, condition in enumerate((f < 2, f == 2, f == 3)):

        @pl.when(condition)
        def _(k=k):
            work(*sources[k])

    @pl.when(f == steps - 1)
    def _():
        in_ref[...] = sum_ref[...].astype(in_ref.dtype)


def feed(x, grad, own, far, far_other, dtype, earlier=()):
    tokens, model = x.shape
    part = own.shape[0] // 6
    block = lambda at: pl.BlockSpec((part, model), at)
    return pl.pallas_call(
        feed_kernel,
        grid=(4,),
        in_specs=[spec_whole(x), spec_whole(grad)]
        + [block(lambda f, a=a: (2 * a + jnp.minimum(f, 1), 0)) for a in range(3)]
        + [block(lambda f, a=a: (a, 0)) for a in range(3)] * 2
        + [everywhere] * len(earlier),
        out_specs=[
            pl.BlockSpec((1, 3, part, tokens), lambda f: (f, 0, 0, 0)),
            pl.BlockSpec((tokens, model), lambda f: (0, 0)),
        ],
        out_shape=[
            jax.ShapeDtypeStruct((4, 3, part, tokens), bf16),
            jax.ShapeDtypeStruct((tokens, model), dtype),
        ],
        scratch_shapes=[pltpu.VMEM((tokens, model), f32)],
        compiler_params=big,
        cost_estimate=cost(16),
        name="feed",
    )(x, grad, *([own] * 3), *([far] * 3), *([far_other] * 3), *earlier)


def half_grads(act_ref, near_ref, x_ref, xn_ref, g_ref, gn_ref, result_ref):
    a = pl.program_id(0)

    @pl.when(a < 2)
    def _():
        result_ref[...] = dot(act_ref[0, 0], x_ref[...], NN) + dot(near_ref[0, 0], xn_ref[...], NN)

    @pl.when(a == 2)
    def _():
        result_ref[...] = dot(act_ref[0, 0], g_ref[...], NN) + dot(near_ref[0, 0], gn_ref[...], NN)


def other_grads_kernel(scalars, *refs):
    out_ref, result_ref = refs[-2:]
    half_grads(*refs[:6], result_ref)
    out_ref[...] = result_ref[...].astype(bf16)


def far_grads_kernel(ranks, scalars, *refs):
    got_ref, out_refs, result_ref = refs[6], refs[7 : 7 + ranks], refs[-1]
    half_grads(*refs[:6], result_ref)
    rows = result_ref.shape[0] // ranks
    for e in range(ranks):
        at = slice(e * rows, (e + 1) * rows)
        out_refs[e][0] = (result_ref[at, :] + got_ref[at, :].astype(f32)).astype(bf16)


def own_grads_kernel(ranks, scalars, *refs):
    got_ref, out_ref, out_got_ref = refs[6:9]
    own_refs, result_ref = refs[9 : 9 + ranks], refs[-1]
    half_grads(*refs[:6], result_ref)
    i = pl.program_id(0)
    rows = result_ref.shape[0] // ranks
    result_ref[...] += got_ref[...].astype(f32)

    @pl.when(i == 0)
    def _():
        for e in range(ranks):
            number = scalars[1] ^ e
            both = out_ref[number].astype(f32) + out_got_ref[number].astype(f32)
            own_refs[e][3 * rows :, :] = both.astype(bf16)

    for a in range(3):

        @pl.when(i == a)
        def _(a=a):
            to = slice(a * rows, (a + 1) * rows)
            for e in range(ranks):
                if rows % 8 == 0:
                    at = pl.ds(pl.multiple_of((scalars[1] ^ e) * rows, 8), rows)
                    own_refs[e][to, :] = result_ref[at, :].astype(bf16)
                else:
                    for h in range(ranks):

                        @pl.when(scalars[1] ^ e == h)
                        def _(e=e, h=h):
                            own_refs[e][to, :] = result_ref[h * rows : (h + 1) * rows, :].astype(bf16)


def shard_grads(scalars, ranks, far, here, near, x, x_near, grad, grad_near, got=None):
    _, _, part, tokens = here.shape
    model = x.shape[1]
    if got is None:
        number = lambda c: 3 if far else 1 - c[0]
    else:
        number = lambda c: 2 if far else c[0]
    act = pl.BlockSpec((1, 1, part, tokens), lambda i, c: (number(c), i, 0, 0))
    in_specs = [act, act] + [spec_whole(x)] * 4
    args = [here, near, x, x_near, grad, grad_near]
    row_block = pl.BlockSpec((part, model), lambda i, c: (i, 0))
    rows = part // ranks
    if got is None:
        kernel, out_specs = other_grads_kernel, row_block
        out_shape = jax.ShapeDtypeStruct((3 * part, model), bf16)
    elif far:
        kernel = functools.partial(far_grads_kernel, ranks)
        in_specs.append(row_block)
        args += got
        out_specs = [pl.BlockSpec((1, rows, model), lambda i, c: (i, 0, 0))] * ranks
        out_shape = [jax.ShapeDtypeStruct((3, rows, model), bf16)] * ranks
    else:
        kernel = functools.partial(own_grads_kernel, ranks)
        in_specs += [row_block] + [spec_whole(g) for g in got[1:]]
        args += got
        wide = 3 * rows + got[1].shape[1]
        out_specs = [pl.BlockSpec((wide, model), lambda i, c: (0, 0))] * ranks
        out_shape = [jax.ShapeDtypeStruct((wide, model), bf16)] * ranks
    spec = pltpu.PrefetchScalarGridSpec(
        num_scalar_prefetch=1,
        grid=(3,),
        in_specs=in_specs,
        out_specs=out_specs,
        scratch_shapes=[pltpu.VMEM((part, model), f32)],
    )
    return pl.pallas_call(
        kernel,
        grid_spec=spec,
        out_shape=out_shape,
        compiler_params=big,
        cost_estimate=cost(8),
        name=("far" if far else "own") + ("_other" if got is None else "_sum"),
    )(scalars, *args)


def others_kernel(scalars, act_ref, near_ref, x_ref, xn_ref, g_ref, gn_ref, *refs):
    own_ref, far_ref, far_other_ref, far_out, own_out, out_ref, out_near_ref, sum_ref = refs
    i = pl.program_id(0)
    for a in range(6):

        @pl.when(i == a)
        def _(a=a):
            first, second = (x_ref, xn_ref) if a % 3 < 2 else (g_ref, gn_ref)
            target = far_out if a < 3 else own_out
            target[...] = (
                dot(act_ref[0, 0], first[...], NN) + dot(near_ref[0, 0], second[...], NN)
            ).astype(bf16)

    @pl.when(i == 5)
    def _():
        sum_ref[...] = jnp.zeros_like(sum_ref)

    for condition, ref in (((i == 6) | (i == 7), own_ref), (i == 8, far_ref), (i == 9, far_other_ref)):

        @pl.when(condition)
        def _(ref=ref):
            sum_ref[0] += dot(act_ref[0, 0], ref[...], TN)
            sum_ref[1] += dot(near_ref[0, 0], ref[...], TN)

    @pl.when(i == 9)
    def _():
        out_ref[...] = sum_ref[0]
        out_near_ref[...] = sum_ref[1].astype(bf16)


def others(scalars, here, near, x, x_near, grad, grad_near, own, far, far_other):
    _, _, part, tokens = here.shape
    model = x.shape[1]

    def act_at(i, c):
        number = jnp.where(i < 3, 3, jnp.where(i < 6, 1 - c[0], i - 6))
        return (number, jnp.where(i < 6, i % 3, 2), 0, 0)

    act = pl.BlockSpec((1, 1, part, tokens), act_at)
    row = lambda at: pl.BlockSpec((part, model), at)
    spec = pltpu.PrefetchScalarGridSpec(
        num_scalar_prefetch=1,
        grid=(10,),
        in_specs=[act, act]
        + [spec_whole(x)] * 4
        + [row(lambda i, c: (4 + jnp.clip(i - 6, 0, 1), 0))]
        + [row(lambda i, c: (2, 0))] * 2,
        out_specs=[
            row(lambda i, c: (jnp.minimum(i, 2), 0)),
            row(lambda i, c: (jnp.clip(i - 3, 0, 2), 0)),
            spec_whole(x),
            spec_whole(x),
        ],
        scratch_shapes=[pltpu.VMEM((2, tokens, model), f32)],
    )
    half = jax.ShapeDtypeStruct((3 * part, model), bf16)
    return pl.pallas_call(
        others_kernel,
        grid_spec=spec,
        out_shape=[half, half]
        + [jax.ShapeDtypeStruct((tokens, model), f32), jax.ShapeDtypeStruct((tokens, model), bf16)],
        compiler_params=big,
        cost_estimate=cost(19),
        name="others",
    )(scalars, here, near, x, x_near, grad, grad_near, own, far, far_other)


def regroup_kernel(ranks, rank_ref, *refs):
    out_ref = refs[-1]
    rows = out_ref.shape[2]
    e = pl.program_id(0)
    for k in range(ranks):

        @pl.when(e == k)
        def _(k=k):
            low, high = refs[2 * k], refs[2 * k + 1]
            cut = low.shape[0]
            for a in range(3):
                first, last = a * rows, (a + 1) * rows
                if last <= cut:
                    out_ref[a, 0] = low[first:last, :]
                elif first >= cut:
                    out_ref[a, 0] = high[first - cut : last - cut, :]
                else:
                    out_ref[a, 0, : cut - first] = low[first:, :]
                    out_ref[a, 0, cut - first :] = high[: last - cut, :]


def regroup(rank, pieces, rows, earlier=()):
    ranks = len(pieces)
    flat, specs = [], []
    for low, high in pieces:
        for x, at, size in (low, high):
            flat.append(x)
            specs.append(pl.BlockSpec((size, x.shape[1]), lambda e, r, at=at: (at, 0)))
    model = flat[0].shape[1]
    spec = pltpu.PrefetchScalarGridSpec(
        num_scalar_prefetch=1,
        grid=(ranks,),
        in_specs=specs + [everywhere] * len(earlier),
        out_specs=pl.BlockSpec((3, 1, rows, model), lambda e, r: (0, r[0] ^ e, 0, 0)),
    )
    return pl.pallas_call(
        functools.partial(regroup_kernel, ranks),
        grid_spec=spec,
        out_shape=jax.ShapeDtypeStruct((3, ranks, rows, model), bf16),
        compiler_params=big,
        cost_estimate=cost(2),
        name="regroup",
    )(rank[None], *flat, *earlier)


def unproject_kernel(counts, cuts, rank_ref, *refs):
    total = sum(counts)
    parts, w_ref, p_ref = refs[:total], refs[total], refs[total + 1]
    pieces = sum(len(c) for c in cuts)
    outs, gain_ref, rows_ref = refs[-2 - pieces : -2], refs[-2], refs[-1]
    i = pl.program_id(0)
    load_rows(parts, counts, i, rows_ref)
    x = rows_ref[...].astype(f32)
    grad = dot(p_ref[...], w_ref[...], NT)
    at = 0
    for k, sizes in enumerate(cuts):
        mine = outs[at : at + len(sizes)]
        at += len(sizes)

        @pl.when(i == k)
        def _(mine=mine):
            row = 0
            for ref in mine:
                ref[...] = grad[row : row + ref.shape[0]].astype(bf16)
                row += ref.shape[0]

    @pl.when(i == 0)
    def _():
        gain_ref[...] = jnp.zeros_like(gain_ref)

    gain_ref[...] += jnp.sum(grad * (x * rms_scale(x)), axis=0, keepdims=True)


def unproject(rank, parts, base, cuts, weights, grads, earlier=()):
    counts = tuple(len(p) for p in parts)
    flat = [x for p in parts for x in p]
    chunk, model = sum(x.shape[0] for x in parts[0]), flat[0].shape[1]
    block = lambda n: pl.BlockSpec((chunk, n), lambda i, r: (r[0] ^ (base + i), 0))
    sizes = [n for c in cuts for n in c]
    spec = pltpu.PrefetchScalarGridSpec(
        num_scalar_prefetch=1,
        grid=(len(parts),),
        in_specs=[spec_whole(x) for x in flat]
        + [spec_whole(weights)]
        + [block(grads.shape[1])]
        + [everywhere] * len(earlier),
        out_specs=[pl.BlockSpec((n, model), lambda i, r: (0, 0)) for n in sizes]
        + [pl.BlockSpec((1, model), lambda i, r: (0, 0))],
        scratch_shapes=[pltpu.VMEM((chunk, model), bf16)],
    )
    out = pl.pallas_call(
        functools.partial(unproject_kernel, counts, cuts),
        grid_spec=spec,
        out_shape=[jax.ShapeDtypeStruct((n, model), bf16) for n in sizes]
        + [jax.ShapeDtypeStruct((1, model), f32)],
        compiler_params=big,
        cost_estimate=cost(3.5 * len(parts)),
        name="unproject",
    )(rank[None], *flat, weights, grads, *earlier)
    return out[:-1], out[-1]


def on_device(
    tokens,
    first_values,
    segment_ids,
    positions,
    attn_gain,
    w_query,
    w_key,
    w_value,
    w_out,
    mlp_gain,
    w_gate,
    w_up,
    w_down,
    out_grad,
):
    core, rank = lax.axis_index("dp"), lax.axis_index("head")
    ranks = lax.axis_size("head")
    chunk, width = tokens.shape[0], w_query.shape[1]
    model = tokens.shape[2]
    length, ff = segment_ids.shape[0], w_gate.shape[1]
    block = min(512, length)
    tokens, firsts, out_grad = tokens[:, 0], first_values[:, 0], out_grad[:, 0]
    places = positions[:, 0]
    start = jnp.arange(length, dtype=jnp.int32) - places

    row_parts = spread_relay(tokens, "head")

    part = ff // 2
    rows = part // ranks
    stack = jnp.concatenate([w_gate.T, w_up.T, w_down])
    cut_stack = stack.reshape(3, 2 * ranks, rows, model)
    far_piece = swap(
        lax.dynamic_index_in_dim(cut_stack, core * ranks + rank, 1, False), "mlp", 2
    ).reshape(3 * rows, model)
    out_grad_near = swap(out_grad, "mlp", 1)
    half_out = width // 2
    far_piece = after(far_piece, *row_parts[-1])
    bundle = jnp.concatenate([far_piece, block_of(w_out, core, half_out)])
    bundles = spread(bundle, "head")

    lanes = min(128, width)
    w_project = jnp.concatenate(
        [
            w[:, g * lanes : (g + 1) * lanes]
            for g in range(width // lanes)
            for w in (w_query, w_key, w_value)
        ],
        axis=1,
    )
    lane = jnp.arange(lanes)
    freq = theta_base ** (-(lane % (HEAD_DIM // 2)).astype(f32) * 2.0 / HEAD_DIM)
    angles = places.astype(f32)[:, None] * freq
    cosine = jnp.cos(angles)
    sine = jnp.sin(angles) * jnp.where(lane % HEAD_DIM < HEAD_DIM // 2, -1.0, 1.0)
    heads_args = (w_project, attn_gain[None], cosine, sine, firsts)
    soon = 3 if ranks == 4 else ranks
    *projected, norms = project(rank, row_parts[:soon], 0, *heads_args)
    if soon < ranks:
        *projected, more = project(rank, row_parts[soon:], soon, *heads_args, projected)
        norms = norms + more
    gathered, queries, keys, values = projected
    groups = width // lanes
    mixed, log_total, mixed_here = [], [], []
    for g in range(groups):
        one_mixed, one_total = attend_forward2(
            queries, keys, values, start, block, g, tuple(mixed[-1:])
        )
        mixed.append(one_mixed)
        log_total.append(one_total)
        mixed_here.append(
            lax.all_to_all(one_mixed, "head", 0, 0, tiled=True).reshape(ranks, chunk, lanes)
        )

    far_half, out_half = assemble(rank, bundles, rows, (mixed_here[0], mixed[-1]))
    far_half = far_half.reshape(3 * part, model)
    far_other, out_other = swap(far_half, "dp", 1), swap(out_half, "dp", 1)
    first = core == 0
    out_all = jnp.concatenate(
        [jnp.where(first, out_half, out_other), jnp.where(first, out_other, out_half)], axis=1
    )

    residual = tokens.astype(f32)
    hidden_state = residual + sum(
        jnp.einsum("htk,hkd->td", m, out_all[:, g * lanes : (g + 1) * lanes], preferred_element_type=f32)
        for g, m in enumerate(mixed_here)
    )
    mlp_scale = rms_scale(hidden_state)
    mlp_input = (hidden_state * mlp_scale * mlp_gain).astype(bf16)
    mlp_input_near = swap(mlp_input, "mlp", 1)

    acts, terms = feed(mlp_input, out_grad, stack, far_half, far_other, f32)
    acts_near, terms_near = feed(
        mlp_input_near, out_grad_near, stack, far_half, far_other, bf16, (terms,)
    )
    terms_back = swap(terms_near, "mlp", 1)
    scalars = jnp.stack([core, rank]).astype(jnp.int32)
    tokens_two = (acts, acts_near, mlp_input, mlp_input_near, out_grad, out_grad_near)
    far_other_grads, own_other_grads, down_here, down_near = others(
        scalars, *tokens_two, stack, far_half, far_other
    )
    terms_back = after(terms_back, down_near)
    far_half_got = swap(after(far_other_grads, terms_back), "dp", 1)
    own_half_got = swap(after(own_other_grads, far_half_got), "dp", 1)
    mlp_normed_grad = terms_back.astype(f32) + terms
    mlp_gain_grad = jnp.sum(mlp_normed_grad * hidden_state * mlp_scale, axis=0)
    state_grad = out_grad.astype(f32) + norm_back(hidden_state, mlp_scale, mlp_gain, mlp_normed_grad)
    state_grad_low = state_grad.astype(bf16)

    mixed_grad = jnp.einsum(
        "td,hkd->htk", state_grad_low, out_all, preferred_element_type=f32
    ).astype(bf16)
    mixed_grad_rows = lax.all_to_all(mixed_grad, "head", 0, 0, tiled=True).reshape(length, width)

    low_grad = after(state_grad_low, mixed_grad)
    out_grads = [
        jnp.einsum("htk,td->hkd", m, low_grad, preferred_element_type=f32).astype(bf16)
        for m in mixed_here
    ]
    out_grads = jnp.concatenate(out_grads, axis=1).reshape(ranks, 2, half_out, model)
    out_got = swap(lax.dynamic_index_in_dim(out_grads, 1 - core, 1, False), "dp", 1)
    out_own = lax.dynamic_index_in_dim(out_grads, core, 1, False)
    far_half_got = after(far_half_got, mixed_grad)
    far_chip = shard_grads(scalars, ranks, True, *tokens_two, [far_half_got])
    far_got = [swap(f, "head", e) for e, f in enumerate(far_chip) if e]
    own_half_got = after(own_half_got, far_chip[0])
    own_chip = shard_grads(scalars, ranks, False, *tokens_two, [own_half_got, out_own, out_got])
    mixed_grad_rows = after(mixed_grad_rows, own_chip[0])

    down_back = swap(after(down_near, mixed_grad_rows), "mlp", 1)
    back_args = (queries, keys, values, mixed_grad_rows, start, cosine, sine, block)
    grads = attend_backward(*back_args, 0, mixed[0], log_total[0])
    far_got = [after(f, grads[0]) for f in far_got]
    far_sum = add_low(far_chip[0], *far_got)
    far_here = swap(far_sum, "mlp", 2)
    own_chip = [own_chip[0]] + [after(f, far_sum) for f in own_chip[1:]]
    own_got = [swap(f, "head", e) for e, f in enumerate(own_chip) if e]
    for g in range(1, width // lanes):
        grads = attend_backward(
            *back_args, g, mixed[g], log_total[g], grads, (far_sum, down_back, *own_chip[1:])
        )
    proj_grad, first_values_grad = grads
    cut = cut_of(chunk)
    half_proj = model // 2
    proj_wgrad = dot(gathered, proj_grad, TN).astype(bf16)
    proj_got = swap(block_of(proj_wgrad, 1 - core, half_proj), "dp", 1)
    if ranks == 4:
        (low, high), gain_last = unproject(
            rank, row_parts[3:], 3, ((cut, chunk - cut),), w_project, proj_grad, (proj_wgrad,)
        )
        for_two, for_one = swap(low, "head", 1), swap(high, "head", 2)
        own_got = [after(f, low) for f in own_got]
    else:
        own_got = [after(f, proj_grad) for f in own_got]
    own_all = (own_chip[0], *own_got)
    piece_sum = add_low(*(f[: 3 * rows] for f in own_all), far_here.reshape(3 * rows, model))
    out_sum = add_low(*(f[3 * rows :] for f in own_all))
    proj_mine = add_low(block_of(proj_wgrad, core, half_proj), proj_got)
    both_mine = jnp.concatenate([proj_mine, out_sum.reshape(half_proj, -1)], axis=1)
    line, count = lax.axis_index("mlp"), lax.axis_size("mlp")

    def line_sum(x):
        size = x.shape[0] // count
        return collect([block_of(x, line ^ e, size) for e in range(count)], "mlp").astype(bf16)

    if ranks == 4:
        cut_p = cut_of(3 * rows)
        cut_q = 3 * rows - cut_p
        low_p, high_p = piece_sum[:cut_p], piece_sum[cut_p:]
        low_x, high_y = swap(low_p, "head", 1), swap(high_p, "head", 2)
        low_yy = swap(jnp.concatenate([low_p, low_x]), "head", 2)
        high_xx = swap(jnp.concatenate([high_p, high_y]), "head", 1)
        (own, one, two), gain_rest = unproject(
            rank,
            row_parts[:3],
            0,
            ((chunk,),) * 3,
            w_project,
            proj_grad,
            (piece_sum, both_mine),
        )
        attn_gain_grad = gain_last + gain_rest
        one = after(one.at[cut:].set(add_low(one[cut:], for_one)), low_yy, high_xx)
        two = after(two.at[:cut].set(add_low(two[:cut], for_two)), low_yy, high_xx)
        one_got, two_got = swap(one, "head", 1), swap(two, "head", 2)
        half_sum = regroup(
            rank,
            [
                ((low_p, 0, cut_p), (high_p, 0, cut_q)),
                ((low_x, 0, cut_p), (high_xx, 0, cut_q)),
                ((low_yy, 0, cut_p), (high_y, 0, cut_q)),
                ((low_yy, 1, cut_p), (high_xx, 1, cut_q)),
            ],
            rows,
        )
        line_piece = after(line_sum(both_mine), one, two, half_sum)
        attn_normed_grad = own.astype(f32) + one_got.astype(f32) + two_got.astype(f32)
        ended = (one_got, two_got)
    else:
        parts, attn_gain_grad = unproject(
            rank, row_parts, 0, ((chunk,),) * ranks, w_project, proj_grad
        )
        half_sum = jnp.zeros((3, ranks, rows, model), bf16)
        for e, piece in enumerate(spread(piece_sum, "head")):
            piece = piece.reshape(3, 1, rows, model)
            half_sum = lax.dynamic_update_slice_in_dim(half_sum, piece, rank ^ e, 1)
        attn_normed_grad = collect(parts, "head")
        ended = (attn_normed_grad,)
        line_piece = line_sum(both_mine)
    half_sum = half_sum.reshape(3, part, model)

    norm_row = jnp.zeros((model,), f32).at[:2].set(jnp.sum(norms[:2], axis=1))
    if count == 4:
        line_one = swap(line_piece, "mlp", 1)
        line_two = swap(jnp.concatenate([line_piece, line_one]), "mlp", 2)
        size = line_piece.shape[0]
        line_got = [line_piece, line_one, line_two[:size], line_two[size:]]
    else:
        line_got = spread(line_piece, "mlp")
    small = jnp.stack([attn_gain_grad[0], mlp_gain_grad, norm_row])
    small = sum_over_all(after(small, line_got[1]))
    output = (hidden_state + after(down_back, line_piece).astype(f32) + down_here).astype(bf16)

    half_sum = after(half_sum, line_piece)
    other_sum = swap(half_sum, "dp", 1)
    ff_grads = jnp.concatenate(
        [jnp.where(first, half_sum, other_sum), jnp.where(first, other_sum, half_sum)], axis=1
    ).astype(f32)
    gate_wgrad, up_wgrad, down_wgrad = ff_grads[0].T, ff_grads[1].T, ff_grads[2]
    input_grad = (
        state_grad + norm_back(residual, rms_scale(residual), attn_gain, attn_normed_grad)
    ).astype(bf16)

    line_got = [after(line_got[0], output, input_grad, down_wgrad, small)] + line_got[1:]
    both_half = in_order(line_got, line)
    both_other = swap(both_half, "dp", 1)
    proj_sum = both_cores(both_half[:, : 3 * width], both_other[:, : 3 * width], core).astype(f32)
    query_wgrad, key_wgrad, value_wgrad = (
        jnp.concatenate(
            [proj_sum[:, (3 * g + k) * lanes : (3 * g + k + 1) * lanes] for g in range(width // lanes)],
            axis=1,
        )
        for k in range(3)
    )
    out_wgrad = both_cores(
        both_half[:, 3 * width :].reshape(half_out, model),
        both_other[:, 3 * width :].reshape(half_out, model),
        core,
    ).astype(f32)

    devices = lax.axis_size("dp") * ranks * count
    value_norms = small[2, :2] / (length * (width // HEAD_DIM) * devices)
    return (
        output[:, None],
        input_grad[:, None],
        first_values_grad[:, None],
        small[0],
        query_wgrad,
        key_wgrad,
        value_wgrad,
        out_wgrad,
        small[1],
        gate_wgrad,
        up_wgrad,
        down_wgrad,
        value_norms,
    )


def solution(mesh):
    placed = (
        P("head", ("dp", "mlp"), None),
        P(None, ("dp", "mlp"), "head"),
        P(None, ("dp", "mlp")),
        P(None, ("dp", "mlp")),
        P(),
        P(None, "head"),
        P(None, "head"),
        P(None, "head"),
        P("head", None),
        P(),
        P(None, "mlp"),
        P(None, "mlp"),
        P("mlp", None),
        P("head", ("dp", "mlp"), None),
    )
    return jax.shard_map(
        on_device,
        mesh=mesh,
        in_specs=placed,
        out_specs=(
            P("head", ("dp", "mlp"), None),
            P("head", ("dp", "mlp"), None),
            P(None, ("dp", "mlp"), "head"),
            P(),
            P(None, "head"),
            P(None, "head"),
            P(None, "head"),
            P("head", None),
            P(),
            P(None, "mlp"),
            P(None, "mlp"),
            P("mlp", None),
            P(),
        ),
        check_vma=False,
    )
```

```python
import functools

import jax
import jax.numpy as jnp
from jax import lax
from jax.experimental import pallas as pl
from jax.experimental.pallas import tpu as pltpu
from jax.sharding import PartitionSpec as P

HEAD_DIM = 64
epsilon = 1e-06
theta_base = 10000.0
blend_weight = 0.5
masked_score = -1e30
NT=(((1,),(1,)),((),()))
NN=(((1,),(0,)),((),()))
TN=(((0,),(0,)),((),()))
def dot(a,b,dims): return lax.dot_general(a,b,dims,preferred_element_type=jnp.float32)

def head_lanes(lanes):
    return lanes//HEAD_DIM

def only_head(x,number,lanes,other=0.0):
    if lanes==HEAD_DIM: return x
    lane=lax.broadcasted_iota(jnp.int32,x.shape,1)
    return jnp.where(lane//HEAD_DIM==number,x,jnp.asarray(other,x.dtype))

def fwd2_kernel(block,firsts,lasts,q_ref,k_ref,v_ref,start_ref,*rest):
    o_ref,lse_ref,vt_ref=rest[-3:]
    i=pl.program_id(1)
    length,lanes=k_ref.shape
    heads=lanes//HEAD_DIM
    @pl.when(i==0)
    def _():
        for r in range(length//block):
            rows=pl.ds(r*block,block)
            t=jnp.transpose(v_ref[rows,:])
            for n in range(heads):
                vt_ref[n,0:HEAD_DIM,rows]=t[n*HEAD_DIM:(n+1)*HEAD_DIM]
                vt_ref[n,HEAD_DIM:,rows]=jnp.ones((16,block),jnp.bfloat16)
    q=q_ref[...]*jnp.asarray(HEAD_DIM**-0.5,q_ref.dtype)
    qs=[only_head(q,n,lanes) for n in range(heads)]
    part=256 if block%256==0 else block
    def update(masked,at,size,first,carry):
        rows=pl.ds(pl.multiple_of(at,part),size)
        k=k_ref[rows,:]
        ss=[dot(k,x[first:],NT) for x in qs]
        if masked:
            shape=ss[0].shape
            key=at+lax.broadcasted_iota(jnp.int32,shape,0)
            query=i*block+first+lax.broadcasted_iota(jnp.int32,shape,1)
            allowed=(key<=query)&(key>=start_ref[:,first:])
            ss=[jnp.where(allowed,s,masked_score) for s in ss]
        ms=[jnp.maximum(carry[n][0],jnp.max(ss[n],axis=0,keepdims=True)) for n in range(heads)]
        ps=[jnp.exp(ss[n]-ms[n]).astype(jnp.bfloat16) for n in range(heads)]
        return tuple((ms[n],carry[n][1]*jnp.exp(carry[n][0]-ms[n])+dot(vt_ref[n,:,rows],ps[n],NN)) for n in range(heads))
    def step(masked,j,carry):
        return update(masked,j*block,block,0,carry)
    carry=tuple((jnp.full((1,block),masked_score,jnp.float32),jnp.zeros((HEAD_DIM+16,block),jnp.float32)) for _ in range(heads))
    a=firsts[i]//block
    b=jnp.clip((lasts[i]+block-1)//block,a,i)
    carry=lax.fori_loop(a,b,functools.partial(step,True),carry)
    carry=lax.fori_loop(b,i,functools.partial(step,False),carry)
    for at in range(0,block,part):
        late=update(True,i*block+at,part,at,tuple((m[:,at:],x[:,at:]) for m,x in carry))
        if at: late=tuple(tuple(jnp.concatenate([x[:,:at],y],axis=1) for x,y in zip(c,l)) for c,l in zip(carry,late))
        carry=late
    outs=[]
    for n in range(heads):
        m,acc=carry[n]
        l=acc[HEAD_DIM:HEAD_DIM+1]
        outs.append(acc[:HEAD_DIM]/l)
        lse_ref[0,n:n+1,:]=m+jnp.log(l)
    o=outs[0] if heads==1 else jnp.concatenate(outs,axis=0)
    o_ref[...]=jnp.transpose(o).astype(o_ref.dtype)

def attend_forward2(q,k,v,start,block,group,earlier=()):
    length,width=q.shape
    lanes=min(128,width); nq=length//block
    firsts=start[::block]; lasts=start[block-1::block]
    spec=pltpu.PrefetchScalarGridSpec(num_scalar_prefetch=2,grid=(1,nq),
        in_specs=[pl.BlockSpec((block,lanes),lambda g,i,*_:(i,group)),
                  pl.BlockSpec((length,lanes),lambda g,i,*_:(0,group)),
                  pl.BlockSpec((length,lanes),lambda g,i,*_:(0,group)),
                  pl.BlockSpec((1,block),lambda g,i,*_:(0,i))]+[pl.BlockSpec(memory_space=pl.ANY)]*len(earlier),
        out_specs=[pl.BlockSpec((block,lanes),lambda g,i,*_:(i,g)),
                   pl.BlockSpec((1,8,block),lambda g,i,*_:(g,0,i))],
        scratch_shapes=[pltpu.VMEM((lanes//HEAD_DIM,HEAD_DIM+16,length),jnp.bfloat16)])
    return pl.pallas_call(functools.partial(fwd2_kernel,block),grid_spec=spec,
        out_shape=[jax.ShapeDtypeStruct((length,lanes),jnp.bfloat16),jax.ShapeDtypeStruct((1,8,length),jnp.float32)],
        compiler_params=pltpu.CompilerParams(vmem_limit_bytes=60*1024*1024),
        cost_estimate=pl.CostEstimate(flops=29*length*length*lanes,bytes_accessed=8*length*lanes,transcendentals=0),
        name="attend_forward")(firsts,lasts,q,k,v,start[None,:],*earlier)

def backward_kernel(block,full_end,some_end,q_ref,k_ref,v_ref,d_ref,o_ref,lse_ref,start_ref,cos_ref,sin_ref,*rest):
    p_ref,first_ref,dq_ref,delta_ref=rest[-4:]
    j=pl.program_id(1)
    length,lanes=q_ref.shape
    heads=lanes//HEAD_DIM
    @pl.when(j==0)
    def _():
        dq_ref[...]=jnp.zeros_like(dq_ref)
        for i in range(length//block):
            rows=pl.ds(i*block,block)
            prod=jnp.transpose(d_ref[rows,:].astype(jnp.float32)*o_ref[rows,:].astype(jnp.float32))
            for n in range(heads):
                delta_ref[n:n+1,rows]=jnp.sum(prod[n*HEAD_DIM:(n+1)*HEAD_DIM],axis=0,keepdims=True)
    k=k_ref[...]; v=v_ref[...]
    scale=HEAD_DIM**-0.5
    kl=[only_head(k,n,lanes) for n in range(heads)]
    ks=[x*jnp.asarray(scale,k.dtype) for x in kl]
    vs=[only_head(v,n,lanes) for n in range(heads)]
    part=256 if block%256==0 else block
    def terms(masked,keys,at,size):
        rows=pl.ds(pl.multiple_of(at,part),size)
        q=q_ref[rows,:]; d=d_ref[rows,:]
        ss=[dot(x[keys],q,NT) for x in ks]
        dps=[dot(x[keys],d,NT) for x in vs]
        if masked:
            shape=ss[0].shape
            key=j*block+keys.start+lax.broadcasted_iota(jnp.int32,shape,0)
            query=at+lax.broadcasted_iota(jnp.int32,shape,1)
            allowed=(key<=query)&(key>=start_ref[0:1,rows])
            ss=[jnp.where(allowed,s,masked_score) for s in ss]
        ps=[jnp.exp(ss[n]-lse_ref[0,n:n+1,rows]) for n in range(heads)]
        dss=[(ps[n]*(dps[n]-delta_ref[n:n+1,rows])).astype(jnp.bfloat16) for n in range(heads)]
        pv=[dot(p.astype(jnp.bfloat16),d,NN) for p in ps]
        pk=[dot(x,q,NN) for x in dss]
        dq_ref[rows,:]+=sum(dot(dss[n],ks[n][keys],TN) for n in range(heads))
        if heads==2:
            lane=lax.broadcasted_iota(jnp.int32,pv[0].shape,1)<HEAD_DIM
            return jnp.where(lane,pk[0],pk[1]),jnp.where(lane,pv[0],pv[1])
        return pk[0],pv[0]
    def step(masked,i,carry):
        dk,dv=terms(masked,slice(0,block),i*block,block)
        return carry[0]+dk,carry[1]+dv
    pieces=[terms(True,slice(at,at+part),j*block+at,block-at) for at in range(0,block,part)]
    carry=tuple(jnp.concatenate(x,axis=0) if len(x)>1 else x[0] for x in zip(*pieces))
    carry=lax.fori_loop(j+1,full_end[j],functools.partial(step,False),carry)
    dk,dv=lax.fori_loop(full_end[j],some_end[j],functools.partial(step,True),carry)
    here=pl.ds(pl.multiple_of(j*block,block),block)
    p_ref[here,lanes:2*lanes]=turned(dk*scale,cos_ref[here,:],-sin_ref[here,:]).astype(jnp.bfloat16)
    blend=dv.astype(jnp.bfloat16).astype(jnp.float32)
    p_ref[here,2*lanes:]=(blend_weight*blend).astype(jnp.bfloat16)
    first_ref[...]=((1.0-blend_weight)*blend).astype(jnp.bfloat16)
    @pl.when(j==pl.num_programs(1)-1)
    def _():
        for i in range(length//block):
            rows=pl.ds(i*block,block)
            p_ref[rows,:lanes]=turned(dq_ref[rows,:],cos_ref[rows,:],-sin_ref[rows,:]).astype(jnp.bfloat16)

def attend_backward(q,k,v,d,start,cosine,sine,block,group,o,lse,before=(),earlier=()):
    length,width=q.shape
    lanes=cosine.shape[1]; n=length//block
    lasts=start[block-1::block]
    edge=jnp.arange(n,dtype=jnp.int32)
    full_end=jnp.maximum(edge+1,jnp.sum((lasts[None,:]<=edge[:,None]*block).astype(jnp.int32),axis=1))
    reach=jnp.sum((start[None,:]<=edge[:,None]*block+block-1).astype(jnp.int32),axis=1)
    some_end=jnp.maximum(full_end,(reach+block-1)//block)
    whole=pl.BlockSpec((length,lanes),lambda g,j,*_:(0,group))
    part=pl.BlockSpec((block,lanes),lambda g,j,*_:(j,group))
    table=pl.BlockSpec((length,lanes),lambda g,j,*_:(0,0))
    more=list(earlier)+list(before)
    spec=pltpu.PrefetchScalarGridSpec(num_scalar_prefetch=2,grid=(1,n),
        in_specs=[whole,part,part,whole,table,pl.BlockSpec((1,8,length),lambda g,j,*_:(0,0,0)),pl.BlockSpec((1,length),lambda g,j,*_:(0,0)),table,table]+[pl.BlockSpec(memory_space=pl.ANY)]*len(more),
        out_specs=[pl.BlockSpec((length,3*lanes),lambda g,j,*_:(0,group)),part],
        scratch_shapes=[pltpu.VMEM((length,lanes),jnp.float32),pltpu.VMEM((8,length),jnp.float32)])
    return pl.pallas_call(functools.partial(backward_kernel,block),grid_spec=spec,
        out_shape=[jax.ShapeDtypeStruct((length,3*width),jnp.bfloat16),jax.ShapeDtypeStruct((length,width),jnp.bfloat16)],
        input_output_aliases={11+len(earlier)+k:k for k in range(len(before))},
        compiler_params=pltpu.CompilerParams(vmem_limit_bytes=56*1024*1024),
        cost_estimate=pl.CostEstimate(flops=52*length*length*lanes,bytes_accessed=22*length*lanes,transcendentals=0),
        name="attend_backward")(full_end,some_end,q,k,v,d,o,lse,start[None,:],cosine,sine,*more)


f32 = jnp.float32
bf16 = jnp.bfloat16
everywhere = pl.BlockSpec(memory_space=pl.ANY)


def swap(x, axis, mask):
    return lax.ppermute(x, axis, [(i, i ^ mask) for i in range(lax.axis_size(axis))])


def cut_of(rows):
    half = rows // 2
    return half - half % 8 if half >= 8 else half


def after(x, *earlier):
    def kernel(*refs):
        pass

    return pl.pallas_call(
        kernel,
        in_specs=[everywhere] * (1 + len(earlier)),
        out_specs=everywhere,
        out_shape=jax.ShapeDtypeStruct(x.shape, x.dtype),
        input_output_aliases={0: 0},
        name="after",
    )(x, *earlier)


def spread_relay(x, axis):
    count = lax.axis_size(axis)
    if count != 4:
        return [[x]] + [[swap(x, axis, e)] for e in range(1, count)]
    cut = cut_of(x.shape[0])
    one, two = swap(x, axis, 1), swap(x, axis, 2)
    return [[x], [one], [two], [swap(two[:cut], axis, 1), swap(one[cut:], axis, 2)]]


def spread(x, axis):
    return [x] + [swap(x, axis, e) for e in range(1, lax.axis_size(axis))]


def add_low(*terms):
    return sum(t.astype(f32) for t in terms).astype(bf16)


def collect(parts, axis):
    return sum((swap(p, axis, e) if e else p).astype(f32) for e, p in enumerate(parts))


def in_order(parts, rank):
    rows = parts[0].shape[0]
    whole = jnp.zeros((len(parts) * rows,) + parts[0].shape[1:], parts[0].dtype)
    for e, part in enumerate(parts):
        whole = lax.dynamic_update_slice_in_dim(whole, part, (rank ^ e) * rows, 0)
    return whole


def block_of(x, number, rows):
    return lax.dynamic_slice_in_dim(x, number * rows, rows, 0)


def both_cores(own, other, core):
    first = core == 0
    return jnp.concatenate([jnp.where(first, own, other), jnp.where(first, other, own)])


def sum_over_all(x):
    for axis in ("mlp", "dp", "head"):
        mask = 1
        while mask < lax.axis_size(axis):
            x = x + swap(x, axis, mask)
            mask *= 2
    return x


def rms_scale(rows):
    return lax.rsqrt(jnp.mean(rows * rows, axis=-1, keepdims=True) + epsilon)


def norm_back(rows, scale, gain, grad):
    weighted = grad * gain
    return scale * weighted - rows * scale * scale * scale * jnp.mean(
        weighted * rows, axis=-1, keepdims=True
    )


def turned(x, cosine, sine):
    half = HEAD_DIM // 2
    if x.shape[1] == HEAD_DIM:
        other = jnp.concatenate([x[:, half:], x[:, :half]], axis=1)
    else:
        lanes = x.shape[1]
        lane = lax.broadcasted_iota(jnp.int32, x.shape, 1)
        other = jnp.where(
            lane % HEAD_DIM < half, pltpu.roll(x, lanes - half, 1), pltpu.roll(x, half, 1)
        )
    return x * cosine + other * sine


def load_rows(refs, counts, number, target):
    at = 0
    for k, pieces in enumerate(counts):
        mine = refs[at : at + pieces]
        at += pieces

        @pl.when(number == k)
        def _(mine=mine):
            row = 0
            for ref in mine:
                target[row : row + ref.shape[0], :] = ref[...]
                row += ref.shape[0]


def project_kernel(counts, rank_ref, *refs):
    total = sum(counts)
    parts, (w_ref, gain_ref, cos_ref, sin_ref, first_ref) = refs[:total], refs[total : total + 5]
    a_ref, q_ref, k_ref, v_ref, norm_ref, rows_ref = refs[-6:]
    i = pl.program_id(0)
    load_rows(parts, counts, i, rows_ref)
    x = rows_ref[...].astype(f32)
    a = (x * rms_scale(x) * gain_ref[...]).astype(bf16)
    a_ref[...] = a
    width = q_ref.shape[1]
    lanes = cos_ref.shape[1]
    cosine, sine = cos_ref[...], sin_ref[...]
    joined = dot(a, w_ref[...], NN)
    of = lax.broadcasted_iota(jnp.int32, (lanes, 128), 0) // HEAD_DIM
    one_hot = (of == lax.broadcasted_iota(jnp.int32, (lanes, 128), 1)).astype(f32)

    def norms(value):
        squares = lax.dot_general(
            value * value, one_hot, NN, precision=lax.Precision.HIGHEST, preferred_element_type=f32
        )
        return jnp.sum(jnp.sqrt(jnp.maximum(squares, 0.0)), axis=0, keepdims=True)

    @pl.when(i == 0)
    def _():
        norm_ref[...] = jnp.zeros_like(norm_ref)

    for g in range(width // lanes):
        at = slice(g * lanes, (g + 1) * lanes)
        query, key, value = (
            joined[:, (3 * g + k) * lanes : (3 * g + k + 1) * lanes] for k in range(3)
        )
        q_ref[:, at] = turned(query, cosine, sine).astype(bf16)
        k_ref[:, at] = turned(key, cosine, sine).astype(bf16)
        first = first_ref[:, at].astype(f32)
        blended = blend_weight * value + (1.0 - blend_weight) * first
        v_ref[:, at] = blended.astype(bf16)
        norm_ref[0:1, :] += norms(first)
        norm_ref[1:2, :] += norms(blended)


def spec_whole(x):
    return pl.BlockSpec(x.shape, lambda *_: (0,) * x.ndim)


def cost(us):
    return pl.CostEstimate(flops=int(us * 1.1e9), bytes_accessed=int(us * 1e5), transcendentals=0)


big = pltpu.CompilerParams(vmem_limit_bytes=56 * 1024 * 1024)


def project(rank, parts, base, weights, gain, cosine, sine, firsts, before=()):
    counts = tuple(len(p) for p in parts)
    flat = [x for p in parts for x in p]
    chunk = sum(x.shape[0] for x in parts[0])
    length, width = firsts.shape
    model, lanes = flat[0].shape[1], cosine.shape[1]
    there = lambda i, r: (r[0] ^ (base + i), 0)
    block = lambda n: pl.BlockSpec((chunk, n), there)
    spec = pltpu.PrefetchScalarGridSpec(
        num_scalar_prefetch=1,
        grid=(len(parts),),
        in_specs=[spec_whole(x) for x in flat]
        + [spec_whole(weights), spec_whole(gain), block(lanes), block(lanes), block(width)]
        + [everywhere] * len(before),
        out_specs=[block(model), block(width), block(width), block(width)]
        + [pl.BlockSpec((8, 128), lambda i, r: (0, 0))],
        scratch_shapes=[pltpu.VMEM((chunk, model), bf16)],
    )
    low = jax.ShapeDtypeStruct((length, width), bf16)
    return pl.pallas_call(
        functools.partial(project_kernel, counts),
        grid_spec=spec,
        out_shape=[jax.ShapeDtypeStruct((length, model), bf16), low, low, low]
        + [jax.ShapeDtypeStruct((8, 128), f32)],
        input_output_aliases={len(flat) + 6 + k: k for k in range(len(before))},
        compiler_params=big,
        cost_estimate=cost(4.5 * len(parts)),
        name="project",
    )(rank[None], *flat, weights, gain, cosine, sine, firsts, *before)


def assemble_kernel(ranks, rank_ref, *refs):
    far_ref, out_ref = refs[-2:]
    rows = far_ref.shape[2]
    e = pl.program_id(0)
    for k in range(ranks):

        @pl.when(e == k)
        def _(ref=refs[k]):
            for a in range(3):
                far_ref[a, 0] = ref[a * rows : (a + 1) * rows, :]
            out_ref[0] = ref[3 * rows :, :]


def assemble(rank, bundles, rows, earlier):
    ranks = len(bundles)
    wide, model = bundles[0].shape
    spec = pltpu.PrefetchScalarGridSpec(
        num_scalar_prefetch=1,
        grid=(ranks,),
        in_specs=[spec_whole(b) for b in bundles] + [everywhere] * len(earlier),
        out_specs=[
            pl.BlockSpec((3, 1, rows, model), lambda e, r: (0, e, 0, 0)),
            pl.BlockSpec((1, wide - 3 * rows, model), lambda e, r: (r[0] ^ e, 0, 0)),
        ],
    )
    return pl.pallas_call(
        functools.partial(assemble_kernel, ranks),
        grid_spec=spec,
        out_shape=[
            jax.ShapeDtypeStruct((3, ranks, rows, model), bf16),
            jax.ShapeDtypeStruct((ranks, wide - 3 * rows, model), bf16),
        ],
        compiler_params=big,
        cost_estimate=cost(3),
        name="assemble",
    )(rank[None], *bundles, *earlier)


def feed_kernel(x_ref, g_ref, *refs):
    sources, (act_ref, in_ref, sum_ref) = (refs[0:3], refs[3:6], refs[6:9]), refs[-3:]
    f = pl.program_id(0)
    steps = pl.num_programs(0)

    @pl.when(f == 0)
    def _():
        sum_ref[...] = jnp.zeros_like(sum_ref)

    def work(gate_w, up_w, down_w):
        x, g = x_ref[...], g_ref[...]
        gate, up = dot(gate_w[...], x, NT), dot(up_w[...], x, NT)
        hidden_grad = dot(down_w[...], g, NT)
        sigma = 1.0 / (1.0 + jnp.exp(-gate))
        gate_sigma = gate * sigma
        hidden = (gate_sigma * up).astype(bf16)
        gate_grad = (hidden_grad * up * (sigma + gate_sigma * (1.0 - sigma))).astype(bf16)
        up_grad = (hidden_grad * gate_sigma).astype(bf16)
        act_ref[0, 0], act_ref[0, 1], act_ref[0, 2] = gate_grad, up_grad, hidden
        sum_ref[...] += dot(gate_grad, gate_w[...], TN) + dot(up_grad, up_w[...], TN)

    for k, condition in enumerate((f < 2, f == 2, f == 3)):

        @pl.when(condition)
        def _(k=k):
            work(*sources[k])

    @pl.when(f == steps - 1)
    def _():
        in_ref[...] = sum_ref[...].astype(in_ref.dtype)


def feed(x, grad, own, far, far_other, dtype, earlier=()):
    tokens, model = x.shape
    part = own.shape[0] // 6
    block = lambda at: pl.BlockSpec((part, model), at)
    return pl.pallas_call(
        feed_kernel,
        grid=(4,),
        in_specs=[spec_whole(x), spec_whole(grad)]
        + [block(lambda f, a=a: (2 * a + jnp.minimum(f, 1), 0)) for a in range(3)]
        + [block(lambda f, a=a: (a, 0)) for a in range(3)] * 2
        + [everywhere] * len(earlier),
        out_specs=[
            pl.BlockSpec((1, 3, part, tokens), lambda f: (f, 0, 0, 0)),
            pl.BlockSpec((tokens, model), lambda f: (0, 0)),
        ],
        out_shape=[
            jax.ShapeDtypeStruct((4, 3, part, tokens), bf16),
            jax.ShapeDtypeStruct((tokens, model), dtype),
        ],
        scratch_shapes=[pltpu.VMEM((tokens, model), f32)],
        compiler_params=big,
        cost_estimate=cost(16),
        name="feed",
    )(x, grad, *([own] * 3), *([far] * 3), *([far_other] * 3), *earlier)


def half_grads(act_ref, near_ref, x_ref, xn_ref, g_ref, gn_ref, result_ref):
    a = pl.program_id(0)

    @pl.when(a < 2)
    def _():
        result_ref[...] = dot(act_ref[0, 0], x_ref[...], NN) + dot(near_ref[0, 0], xn_ref[...], NN)

    @pl.when(a == 2)
    def _():
        result_ref[...] = dot(act_ref[0, 0], g_ref[...], NN) + dot(near_ref[0, 0], gn_ref[...], NN)


def other_grads_kernel(scalars, *refs):
    out_ref, result_ref = refs[-2:]
    half_grads(*refs[:6], result_ref)
    out_ref[...] = result_ref[...].astype(bf16)


def far_grads_kernel(ranks, scalars, *refs):
    got_ref, out_refs, result_ref = refs[6], refs[7 : 7 + ranks], refs[-1]
    half_grads(*refs[:6], result_ref)
    rows = result_ref.shape[0] // ranks
    for e in range(ranks):
        at = slice(e * rows, (e + 1) * rows)
        out_refs[e][0] = (result_ref[at, :] + got_ref[at, :].astype(f32)).astype(bf16)


def own_grads_kernel(ranks, scalars, *refs):
    got_ref, out_ref, out_got_ref = refs[6:9]
    own_refs, result_ref = refs[9 : 9 + ranks], refs[-1]
    half_grads(*refs[:6], result_ref)
    i = pl.program_id(0)
    rows = result_ref.shape[0] // ranks
    result_ref[...] += got_ref[...].astype(f32)

    @pl.when(i == 0)
    def _():
        for e in range(ranks):
            number = scalars[1] ^ e
            both = out_ref[number].astype(f32) + out_got_ref[number].astype(f32)
            own_refs[e][3 * rows :, :] = both.astype(bf16)

    for a in range(3):

        @pl.when(i == a)
        def _(a=a):
            to = slice(a * rows, (a + 1) * rows)
            for e in range(ranks):
                if rows % 8 == 0:
                    at = pl.ds(pl.multiple_of((scalars[1] ^ e) * rows, 8), rows)
                    own_refs[e][to, :] = result_ref[at, :].astype(bf16)
                else:
                    for h in range(ranks):

                        @pl.when(scalars[1] ^ e == h)
                        def _(e=e, h=h):
                            own_refs[e][to, :] = result_ref[h * rows : (h + 1) * rows, :].astype(bf16)


def shard_grads(scalars, ranks, far, here, near, x, x_near, grad, grad_near, got=None):
    _, _, part, tokens = here.shape
    model = x.shape[1]
    if got is None:
        number = lambda c: 3 if far else 1 - c[0]
    else:
        number = lambda c: 2 if far else c[0]
    act = pl.BlockSpec((1, 1, part, tokens), lambda i, c: (number(c), i, 0, 0))
    in_specs = [act, act] + [spec_whole(x)] * 4
    args = [here, near, x, x_near, grad, grad_near]
    row_block = pl.BlockSpec((part, model), lambda i, c: (i, 0))
    rows = part // ranks
    if got is None:
        kernel, out_specs = other_grads_kernel, row_block
        out_shape = jax.ShapeDtypeStruct((3 * part, model), bf16)
    elif far:
        kernel = functools.partial(far_grads_kernel, ranks)
        in_specs.append(row_block)
        args += got
        out_specs = [pl.BlockSpec((1, rows, model), lambda i, c: (i, 0, 0))] * ranks
        out_shape = [jax.ShapeDtypeStruct((3, rows, model), bf16)] * ranks
    else:
        kernel = functools.partial(own_grads_kernel, ranks)
        in_specs += [row_block] + [spec_whole(g) for g in got[1:]]
        args += got
        wide = 3 * rows + got[1].shape[1]
        out_specs = [pl.BlockSpec((wide, model), lambda i, c: (0, 0))] * ranks
        out_shape = [jax.ShapeDtypeStruct((wide, model), bf16)] * ranks
    spec = pltpu.PrefetchScalarGridSpec(
        num_scalar_prefetch=1,
        grid=(3,),
        in_specs=in_specs,
        out_specs=out_specs,
        scratch_shapes=[pltpu.VMEM((part, model), f32)],
    )
    return pl.pallas_call(
        kernel,
        grid_spec=spec,
        out_shape=out_shape,
        compiler_params=big,
        cost_estimate=cost(8),
        name=("far" if far else "own") + ("_other" if got is None else "_sum"),
    )(scalars, *args)


def others_kernel(scalars, act_ref, near_ref, x_ref, xn_ref, g_ref, gn_ref, *refs):
    own_ref, far_ref, far_other_ref, far_out, own_out, out_ref, out_near_ref, sum_ref = refs
    i = pl.program_id(0)
    for a in range(6):

        @pl.when(i == a)
        def _(a=a):
            first, second = (x_ref, xn_ref) if a % 3 < 2 else (g_ref, gn_ref)
            target = far_out if a < 3 else own_out
            target[...] = (
                dot(act_ref[0, 0], first[...], NN) + dot(near_ref[0, 0], second[...], NN)
            ).astype(bf16)

    @pl.when(i == 5)
    def _():
        sum_ref[...] = jnp.zeros_like(sum_ref)

    for condition, ref in (((i == 6) | (i == 7), own_ref), (i == 8, far_ref), (i == 9, far_other_ref)):

        @pl.when(condition)
        def _(ref=ref):
            sum_ref[0] += dot(act_ref[0, 0], ref[...], TN)
            sum_ref[1] += dot(near_ref[0, 0], ref[...], TN)

    @pl.when(i == 9)
    def _():
        out_ref[...] = sum_ref[0]
        out_near_ref[...] = sum_ref[1].astype(bf16)


def others(scalars, here, near, x, x_near, grad, grad_near, own, far, far_other):
    _, _, part, tokens = here.shape
    model = x.shape[1]

    def act_at(i, c):
        number = jnp.where(i < 3, 3, jnp.where(i < 6, 1 - c[0], i - 6))
        return (number, jnp.where(i < 6, i % 3, 2), 0, 0)

    act = pl.BlockSpec((1, 1, part, tokens), act_at)
    row = lambda at: pl.BlockSpec((part, model), at)
    spec = pltpu.PrefetchScalarGridSpec(
        num_scalar_prefetch=1,
        grid=(10,),
        in_specs=[act, act]
        + [spec_whole(x)] * 4
        + [row(lambda i, c: (4 + jnp.clip(i - 6, 0, 1), 0))]
        + [row(lambda i, c: (2, 0))] * 2,
        out_specs=[
            row(lambda i, c: (jnp.minimum(i, 2), 0)),
            row(lambda i, c: (jnp.clip(i - 3, 0, 2), 0)),
            spec_whole(x),
            spec_whole(x),
        ],
        scratch_shapes=[pltpu.VMEM((2, tokens, model), f32)],
    )
    half = jax.ShapeDtypeStruct((3 * part, model), bf16)
    return pl.pallas_call(
        others_kernel,
        grid_spec=spec,
        out_shape=[half, half]
        + [jax.ShapeDtypeStruct((tokens, model), f32), jax.ShapeDtypeStruct((tokens, model), bf16)],
        compiler_params=big,
        cost_estimate=cost(19),
        name="others",
    )(scalars, here, near, x, x_near, grad, grad_near, own, far, far_other)


def regroup_kernel(ranks, rank_ref, *refs):
    out_ref = refs[-1]
    rows = out_ref.shape[2]
    e = pl.program_id(0)
    for k in range(ranks):

        @pl.when(e == k)
        def _(k=k):
            low, high = refs[2 * k], refs[2 * k + 1]
            cut = low.shape[0]
            for a in range(3):
                first, last = a * rows, (a + 1) * rows
                if last <= cut:
                    out_ref[a, 0] = low[first:last, :]
                elif first >= cut:
                    out_ref[a, 0] = high[first - cut : last - cut, :]
                else:
                    out_ref[a, 0, : cut - first] = low[first:, :]
                    out_ref[a, 0, cut - first :] = high[: last - cut, :]


def regroup(rank, pieces, rows, earlier=()):
    ranks = len(pieces)
    flat, specs = [], []
    for low, high in pieces:
        for x, at, size in (low, high):
            flat.append(x)
            specs.append(pl.BlockSpec((size, x.shape[1]), lambda e, r, at=at: (at, 0)))
    model = flat[0].shape[1]
    spec = pltpu.PrefetchScalarGridSpec(
        num_scalar_prefetch=1,
        grid=(ranks,),
        in_specs=specs + [everywhere] * len(earlier),
        out_specs=pl.BlockSpec((3, 1, rows, model), lambda e, r: (0, r[0] ^ e, 0, 0)),
    )
    return pl.pallas_call(
        functools.partial(regroup_kernel, ranks),
        grid_spec=spec,
        out_shape=jax.ShapeDtypeStruct((3, ranks, rows, model), bf16),
        compiler_params=big,
        cost_estimate=cost(2),
        name="regroup",
    )(rank[None], *flat, *earlier)


def unproject_kernel(counts, cuts, rank_ref, *refs):
    total = sum(counts)
    parts, w_ref, p_ref = refs[:total], refs[total], refs[total + 1]
    pieces = sum(len(c) for c in cuts)
    outs, gain_ref, rows_ref = refs[-2 - pieces : -2], refs[-2], refs[-1]
    i = pl.program_id(0)
    load_rows(parts, counts, i, rows_ref)
    x = rows_ref[...].astype(f32)
    grad = dot(p_ref[...], w_ref[...], NT)
    at = 0
    for k, sizes in enumerate(cuts):
        mine = outs[at : at + len(sizes)]
        at += len(sizes)

        @pl.when(i == k)
        def _(mine=mine):
            row = 0
            for ref in mine:
                ref[...] = grad[row : row + ref.shape[0]].astype(bf16)
                row += ref.shape[0]

    @pl.when(i == 0)
    def _():
        gain_ref[...] = jnp.zeros_like(gain_ref)

    gain_ref[...] += jnp.sum(grad * (x * rms_scale(x)), axis=0, keepdims=True)


def unproject(rank, parts, base, cuts, weights, grads, earlier=()):
    counts = tuple(len(p) for p in parts)
    flat = [x for p in parts for x in p]
    chunk, model = sum(x.shape[0] for x in parts[0]), flat[0].shape[1]
    block = lambda n: pl.BlockSpec((chunk, n), lambda i, r: (r[0] ^ (base + i), 0))
    sizes = [n for c in cuts for n in c]
    spec = pltpu.PrefetchScalarGridSpec(
        num_scalar_prefetch=1,
        grid=(len(parts),),
        in_specs=[spec_whole(x) for x in flat]
        + [spec_whole(weights)]
        + [block(grads.shape[1])]
        + [everywhere] * len(earlier),
        out_specs=[pl.BlockSpec((n, model), lambda i, r: (0, 0)) for n in sizes]
        + [pl.BlockSpec((1, model), lambda i, r: (0, 0))],
        scratch_shapes=[pltpu.VMEM((chunk, model), bf16)],
    )
    out = pl.pallas_call(
        functools.partial(unproject_kernel, counts, cuts),
        grid_spec=spec,
        out_shape=[jax.ShapeDtypeStruct((n, model), bf16) for n in sizes]
        + [jax.ShapeDtypeStruct((1, model), f32)],
        compiler_params=big,
        cost_estimate=cost(3.5 * len(parts)),
        name="unproject",
    )(rank[None], *flat, weights, grads, *earlier)
    return out[:-1], out[-1]


def state_kernel(back_ref, terms_ref, hidden_ref, grad_ref, gain_ref, w_ref, state_ref, low_ref, mixed_ref, sum_ref):
    hidden, gain = hidden_ref[...], gain_ref[...]
    grad = back_ref[...].astype(f32) + terms_ref[...]
    scale = rms_scale(hidden)
    state = grad_ref[...].astype(f32) + norm_back(hidden, scale, gain, grad)
    low = state.astype(bf16)
    state_ref[...] = state
    low_ref[...] = low
    for h in range(mixed_ref.shape[0]):
        mixed_ref[h] = dot(low, w_ref[h], NT).astype(bf16)

    @pl.when(pl.program_id(0) == 0)
    def _():
        sum_ref[...] = jnp.zeros_like(sum_ref)

    sum_ref[...] += jnp.sum(grad * hidden * scale, axis=0, keepdims=True)


def state_back(back, terms, hidden, grad, gain, weights):
    tokens, model = back.shape
    ranks, width, _ = weights.shape
    size = 128 if tokens % 128 == 0 else tokens
    row = pl.BlockSpec((size, model), lambda i: (i, 0))
    return pl.pallas_call(
        state_kernel,
        grid=(tokens // size,),
        in_specs=[row, row, row, row, spec_whole(gain), spec_whole(weights)],
        out_specs=[
            row,
            row,
            pl.BlockSpec((ranks, size, width), lambda i: (0, i, 0)),
            pl.BlockSpec((1, model), lambda i: (0, 0)),
        ],
        out_shape=[
            jax.ShapeDtypeStruct((tokens, model), f32),
            jax.ShapeDtypeStruct((tokens, model), bf16),
            jax.ShapeDtypeStruct((ranks, tokens, width), bf16),
            jax.ShapeDtypeStruct((1, model), f32),
        ],
        compiler_params=big,
        cost_estimate=cost(6),
        name="state_back",
    )(back, terms, hidden, grad, gain, weights)


def on_device(
    tokens,
    first_values,
    segment_ids,
    positions,
    attn_gain,
    w_query,
    w_key,
    w_value,
    w_out,
    mlp_gain,
    w_gate,
    w_up,
    w_down,
    out_grad,
):
    core, rank = lax.axis_index("dp"), lax.axis_index("head")
    ranks = lax.axis_size("head")
    chunk, width = tokens.shape[0], w_query.shape[1]
    model = tokens.shape[2]
    length, ff = segment_ids.shape[0], w_gate.shape[1]
    block = min(512, length)
    tokens, firsts, out_grad = tokens[:, 0], first_values[:, 0], out_grad[:, 0]
    places = positions[:, 0]
    start = jnp.arange(length, dtype=jnp.int32) - places

    row_parts = spread_relay(tokens, "head")

    part = ff // 2
    rows = part // ranks
    stack = jnp.concatenate([w_gate.T, w_up.T, w_down])
    cut_stack = stack.reshape(3, 2 * ranks, rows, model)
    far_piece = swap(
        lax.dynamic_index_in_dim(cut_stack, core * ranks + rank, 1, False), "mlp", 2
    ).reshape(3 * rows, model)
    out_grad_near = swap(out_grad, "mlp", 1)
    half_out = width // 2
    far_piece = after(far_piece, *row_parts[-1])
    bundle = jnp.concatenate([far_piece, block_of(w_out, core, half_out)])
    bundles = spread(bundle, "head")

    lanes = min(128, width)
    w_project = jnp.concatenate(
        [
            w[:, g * lanes : (g + 1) * lanes]
            for g in range(width // lanes)
            for w in (w_query, w_key, w_value)
        ],
        axis=1,
    )
    lane = jnp.arange(lanes)
    freq = theta_base ** (-(lane % (HEAD_DIM // 2)).astype(f32) * 2.0 / HEAD_DIM)
    angles = places.astype(f32)[:, None] * freq
    cosine = jnp.cos(angles)
    sine = jnp.sin(angles) * jnp.where(lane % HEAD_DIM < HEAD_DIM // 2, -1.0, 1.0)
    heads_args = (w_project, attn_gain[None], cosine, sine, firsts)
    soon = 3 if ranks == 4 else ranks
    *projected, norms = project(rank, row_parts[:soon], 0, *heads_args)
    if soon < ranks:
        *projected, more = project(rank, row_parts[soon:], soon, *heads_args, projected)
        norms = norms + more
    gathered, queries, keys, values = projected
    groups = width // lanes
    mixed, log_total, mixed_here = [], [], []
    for g in range(groups):
        one_mixed, one_total = attend_forward2(
            queries, keys, values, start, min(1024, length), g, tuple(mixed[-1:])
        )
        mixed.append(one_mixed)
        log_total.append(one_total)
        mixed_here.append(
            lax.all_to_all(one_mixed, "head", 0, 0, tiled=True).reshape(ranks, chunk, lanes)
        )

    far_half, out_half = assemble(rank, bundles, rows, (mixed_here[0], mixed[-1]))
    far_half = far_half.reshape(3 * part, model)
    far_other, out_other = swap(far_half, "dp", 1), swap(out_half, "dp", 1)
    first = core == 0
    out_all = jnp.concatenate(
        [jnp.where(first, out_half, out_other), jnp.where(first, out_other, out_half)], axis=1
    )

    residual = tokens.astype(f32)
    hidden_state = residual + sum(
        jnp.einsum("htk,hkd->td", m, out_all[:, g * lanes : (g + 1) * lanes], preferred_element_type=f32)
        for g, m in enumerate(mixed_here)
    )
    mlp_scale = rms_scale(hidden_state)
    mlp_input = (hidden_state * mlp_scale * mlp_gain).astype(bf16)
    mlp_input_near = swap(mlp_input, "mlp", 1)

    acts, terms = feed(mlp_input, out_grad, stack, far_half, far_other, f32)
    acts_near, terms_near = feed(
        mlp_input_near, out_grad_near, stack, far_half, far_other, bf16, (terms,)
    )
    terms_back = swap(terms_near, "mlp", 1)
    scalars = jnp.stack([core, rank]).astype(jnp.int32)
    tokens_two = (acts, acts_near, mlp_input, mlp_input_near, out_grad, out_grad_near)
    far_other_grads, own_other_grads, down_here, down_near = others(
        scalars, *tokens_two, stack, far_half, far_other
    )
    terms_back = after(terms_back, down_near)
    far_half_got = swap(after(far_other_grads, terms_back), "dp", 1)
    own_half_got = swap(after(own_other_grads, far_half_got), "dp", 1)
    state_grad, state_grad_low, mixed_grad, mlp_gain_grad = state_back(
        terms_back, terms, hidden_state, out_grad, mlp_gain[None], out_all
    )
    mlp_gain_grad = mlp_gain_grad[0]
    mixed_grad_rows = lax.all_to_all(mixed_grad, "head", 0, 0, tiled=True).reshape(length, width)

    low_grad = after(state_grad_low, mixed_grad)
    out_grads = [
        jnp.einsum("htk,td->hkd", m, low_grad, preferred_element_type=f32).astype(bf16)
        for m in mixed_here
    ]
    out_grads = jnp.concatenate(out_grads, axis=1).reshape(ranks, 2, half_out, model)
    out_got = swap(lax.dynamic_index_in_dim(out_grads, 1 - core, 1, False), "dp", 1)
    out_own = lax.dynamic_index_in_dim(out_grads, core, 1, False)
    far_half_got = after(far_half_got, mixed_grad)
    far_chip = shard_grads(scalars, ranks, True, *tokens_two, [far_half_got])
    far_got = [swap(f, "head", e) for e, f in enumerate(far_chip) if e]
    own_half_got = after(own_half_got, far_chip[0])
    own_chip = shard_grads(scalars, ranks, False, *tokens_two, [own_half_got, out_own, out_got])
    mixed_grad_rows = after(mixed_grad_rows, own_chip[0])

    down_back = swap(after(down_near, mixed_grad_rows), "mlp", 1)
    back_args = (queries, keys, values, mixed_grad_rows, start, cosine, sine, block)
    grads = attend_backward(*back_args, 0, mixed[0], log_total[0])
    far_got = [after(f, grads[0]) for f in far_got]
    far_sum = add_low(far_chip[0], *far_got)
    far_here = swap(far_sum, "mlp", 2)
    own_chip = [own_chip[0]] + [after(f, far_sum) for f in own_chip[1:]]
    own_got = [swap(f, "head", e) for e, f in enumerate(own_chip) if e]
    for g in range(1, width // lanes):
        grads = attend_backward(
            *back_args, g, mixed[g], log_total[g], grads, (far_sum, down_back, *own_chip[1:])
        )
    proj_grad, first_values_grad = grads
    cut = cut_of(chunk)
    half_proj = model // 2
    proj_wgrad = dot(gathered, proj_grad, TN).astype(bf16)
    proj_got = swap(block_of(proj_wgrad, 1 - core, half_proj), "dp", 1)
    if ranks == 4:
        (low, high), gain_last = unproject(
            rank, row_parts[3:], 3, ((cut, chunk - cut),), w_project, proj_grad, (proj_wgrad,)
        )
        for_two, for_one = swap(low, "head", 1), swap(high, "head", 2)
        own_got = [after(f, low) for f in own_got]
    else:
        own_got = [after(f, proj_grad) for f in own_got]
    own_all = (own_chip[0], *own_got)
    piece_sum = add_low(*(f[: 3 * rows] for f in own_all), far_here.reshape(3 * rows, model))
    out_sum = add_low(*(f[3 * rows :] for f in own_all))
    proj_mine = add_low(block_of(proj_wgrad, core, half_proj), proj_got)
    both_mine = jnp.concatenate([proj_mine, out_sum.reshape(half_proj, -1)], axis=1)
    line, count = lax.axis_index("mlp"), lax.axis_size("mlp")

    def line_sum(x):
        size = x.shape[0] // count
        return collect([block_of(x, line ^ e, size) for e in range(count)], "mlp").astype(bf16)

    if ranks == 4:
        cut_p = cut_of(3 * rows)
        cut_q = 3 * rows - cut_p
        low_p, high_p = piece_sum[:cut_p], piece_sum[cut_p:]
        low_x, high_y = swap(low_p, "head", 1), swap(high_p, "head", 2)
        low_yy = swap(jnp.concatenate([low_p, low_x]), "head", 2)
        high_xx = swap(jnp.concatenate([high_p, high_y]), "head", 1)
        (own, one, two), gain_rest = unproject(
            rank,
            row_parts[:3],
            0,
            ((chunk,),) * 3,
            w_project,
            proj_grad,
            (piece_sum, both_mine),
        )
        attn_gain_grad = gain_last + gain_rest
        one = after(one.at[cut:].set(add_low(one[cut:], for_one)), low_yy, high_xx)
        two = after(two.at[:cut].set(add_low(two[:cut], for_two)), low_yy, high_xx)
        one_got, two_got = swap(one, "head", 1), swap(two, "head", 2)
        half_sum = regroup(
            rank,
            [
                ((low_p, 0, cut_p), (high_p, 0, cut_q)),
                ((low_x, 0, cut_p), (high_xx, 0, cut_q)),
                ((low_yy, 0, cut_p), (high_y, 0, cut_q)),
                ((low_yy, 1, cut_p), (high_xx, 1, cut_q)),
            ],
            rows,
        )
        line_piece = after(line_sum(both_mine), one, two, half_sum)
        attn_normed_grad = own.astype(f32) + one_got.astype(f32) + two_got.astype(f32)
        ended = (one_got, two_got)
    else:
        parts, attn_gain_grad = unproject(
            rank, row_parts, 0, ((chunk,),) * ranks, w_project, proj_grad
        )
        half_sum = jnp.zeros((3, ranks, rows, model), bf16)
        for e, piece in enumerate(spread(piece_sum, "head")):
            piece = piece.reshape(3, 1, rows, model)
            half_sum = lax.dynamic_update_slice_in_dim(half_sum, piece, rank ^ e, 1)
        attn_normed_grad = collect(parts, "head")
        ended = (attn_normed_grad,)
        line_piece = line_sum(both_mine)
    half_sum = half_sum.reshape(3, part, model)

    norm_row = jnp.zeros((model,), f32).at[:2].set(jnp.sum(norms[:2], axis=1))
    if count == 4:
        line_one = swap(line_piece, "mlp", 1)
        line_two = swap(jnp.concatenate([line_piece, line_one]), "mlp", 2)
        size = line_piece.shape[0]
        line_got = [line_piece, line_one, line_two[:size], line_two[size:]]
    else:
        line_got = spread(line_piece, "mlp")
    small = jnp.stack([attn_gain_grad[0], mlp_gain_grad, norm_row])
    small = sum_over_all(after(small, line_got[1]))
    output = (hidden_state + after(down_back, line_piece).astype(f32) + down_here).astype(bf16)

    half_sum = after(half_sum, line_piece)
    other_sum = swap(half_sum, "dp", 1)
    ff_grads = jnp.concatenate(
        [jnp.where(first, half_sum, other_sum), jnp.where(first, other_sum, half_sum)], axis=1
    ).astype(f32)
    gate_wgrad, up_wgrad, down_wgrad = ff_grads[0].T, ff_grads[1].T, ff_grads[2]
    input_grad = (
        state_grad + norm_back(residual, rms_scale(residual), attn_gain, attn_normed_grad)
    ).astype(bf16)

    line_got = [after(line_got[0], output, input_grad, down_wgrad, small)] + line_got[1:]
    both_half = in_order(line_got, line)
    both_other = swap(both_half, "dp", 1)
    proj_sum = both_cores(both_half[:, : 3 * width], both_other[:, : 3 * width], core).astype(f32)
    query_wgrad, key_wgrad, value_wgrad = (
        jnp.concatenate(
            [proj_sum[:, (3 * g + k) * lanes : (3 * g + k + 1) * lanes] for g in range(width // lanes)],
            axis=1,
        )
        for k in range(3)
    )
    out_wgrad = both_cores(
        both_half[:, 3 * width :].reshape(half_out, model),
        both_other[:, 3 * width :].reshape(half_out, model),
        core,
    ).astype(f32)

    devices = lax.axis_size("dp") * ranks * count
    value_norms = small[2, :2] / (length * (width // HEAD_DIM) * devices)
    return (
        output[:, None],
        input_grad[:, None],
        first_values_grad[:, None],
        small[0],
        query_wgrad,
        key_wgrad,
        value_wgrad,
        out_wgrad,
        small[1],
        gate_wgrad,
        up_wgrad,
        down_wgrad,
        value_norms,
    )


def solution(mesh):
    placed = (
        P("head", ("dp", "mlp"), None),
        P(None, ("dp", "mlp"), "head"),
        P(None, ("dp", "mlp")),
        P(None, ("dp", "mlp")),
        P(),
        P(None, "head"),
        P(None, "head"),
        P(None, "head"),
        P("head", None),
        P(),
        P(None, "mlp"),
        P(None, "mlp"),
        P("mlp", None),
        P("head", ("dp", "mlp"), None),
    )
    return jax.shard_map(
        on_device,
        mesh=mesh,
        in_specs=placed,
        out_specs=(
            P("head", ("dp", "mlp"), None),
            P("head", ("dp", "mlp"), None),
            P(None, ("dp", "mlp"), "head"),
            P(),
            P(None, "head"),
            P(None, "head"),
            P(None, "head"),
            P("head", None),
            P(),
            P(None, "mlp"),
            P(None, "mlp"),
            P("mlp", None),
            P(),
        ),
        check_vma=False,
    )
```

```python
import functools

import jax
import jax.numpy as jnp
from jax import lax
from jax.experimental import pallas as pl
from jax.experimental.pallas import tpu as pltpu
from jax.sharding import PartitionSpec as P

HEAD_DIM = 64
epsilon = 1e-06
theta_base = 10000.0
blend_weight = 0.5
masked_score = -1e30
NT=(((1,),(1,)),((),()))
NN=(((1,),(0,)),((),()))
TN=(((0,),(0,)),((),()))
def dot(a,b,dims): return lax.dot_general(a,b,dims,preferred_element_type=jnp.float32)

def head_lanes(lanes):
    return lanes//HEAD_DIM

def only_head(x,number,lanes,other=0.0):
    if lanes==HEAD_DIM: return x
    lane=lax.broadcasted_iota(jnp.int32,x.shape,1)
    return jnp.where(lane//HEAD_DIM==number,x,jnp.asarray(other,x.dtype))

def fwd2_kernel(block,firsts,lasts,q_ref,k_ref,v_ref,start_ref,*rest):
    o_ref,lse_ref,vt_ref=rest[-3:]
    i=pl.program_id(1)
    length,lanes=k_ref.shape
    heads=lanes//HEAD_DIM
    @pl.when(i==0)
    def _():
        for r in range(length//block):
            rows=pl.ds(r*block,block)
            t=jnp.transpose(v_ref[rows,:])
            for n in range(heads):
                vt_ref[n,0:HEAD_DIM,rows]=t[n*HEAD_DIM:(n+1)*HEAD_DIM]
                vt_ref[n,HEAD_DIM:,rows]=jnp.ones((16,block),jnp.bfloat16)
    q=q_ref[...]*jnp.asarray(HEAD_DIM**-0.5,q_ref.dtype)
    qs=[only_head(q,n,lanes) for n in range(heads)]
    part=256 if block%256==0 else block
    def update(masked,at,size,first,carry):
        rows=pl.ds(pl.multiple_of(at,part),size)
        k=k_ref[rows,:]
        ss=[dot(k,x[first:],NT) for x in qs]
        if masked:
            shape=ss[0].shape
            key=at+lax.broadcasted_iota(jnp.int32,shape,0)
            query=i*block+first+lax.broadcasted_iota(jnp.int32,shape,1)
            allowed=(key<=query)&(key>=start_ref[:,first:])
            ss=[jnp.where(allowed,s,masked_score) for s in ss]
        ms=[jnp.maximum(carry[n][0],jnp.max(ss[n],axis=0,keepdims=True)) for n in range(heads)]
        ps=[jnp.exp(ss[n]-ms[n]).astype(jnp.bfloat16) for n in range(heads)]
        return tuple((ms[n],carry[n][1]*jnp.exp(carry[n][0]-ms[n])+dot(vt_ref[n,:,rows],ps[n],NN)) for n in range(heads))
    def step(masked,j,carry):
        return update(masked,j*block,block,0,carry)
    carry=tuple((jnp.full((1,block),masked_score,jnp.float32),jnp.zeros((HEAD_DIM+16,block),jnp.float32)) for _ in range(heads))
    a=firsts[i]//block
    b=jnp.clip((lasts[i]+block-1)//block,a,i)
    carry=lax.fori_loop(a,b,functools.partial(step,True),carry)
    carry=lax.fori_loop(b,i,functools.partial(step,False),carry)
    for at in range(0,block,part):
        late=update(True,i*block+at,part,at,tuple((m[:,at:],x[:,at:]) for m,x in carry))
        if at: late=tuple(tuple(jnp.concatenate([x[:,:at],y],axis=1) for x,y in zip(c,l)) for c,l in zip(carry,late))
        carry=late
    outs=[]
    for n in range(heads):
        m,acc=carry[n]
        l=acc[HEAD_DIM:HEAD_DIM+1]
        outs.append(acc[:HEAD_DIM]/l)
        lse_ref[0,n:n+1,:]=m+jnp.log(l)
    o=outs[0] if heads==1 else jnp.concatenate(outs,axis=0)
    o_ref[...]=jnp.transpose(o).astype(o_ref.dtype)

def attend_forward2(q,k,v,start,block,group,earlier=()):
    length,width=q.shape
    lanes=min(128,width); nq=length//block
    firsts=start[::block]; lasts=start[block-1::block]
    spec=pltpu.PrefetchScalarGridSpec(num_scalar_prefetch=2,grid=(1,nq),
        in_specs=[pl.BlockSpec((block,lanes),lambda g,i,*_:(i,group)),
                  pl.BlockSpec((length,lanes),lambda g,i,*_:(0,group)),
                  pl.BlockSpec((length,lanes),lambda g,i,*_:(0,group)),
                  pl.BlockSpec((1,block),lambda g,i,*_:(0,i))]+[pl.BlockSpec(memory_space=pl.ANY)]*len(earlier),
        out_specs=[pl.BlockSpec((block,lanes),lambda g,i,*_:(i,g)),
                   pl.BlockSpec((1,8,block),lambda g,i,*_:(g,0,i))],
        scratch_shapes=[pltpu.VMEM((lanes//HEAD_DIM,HEAD_DIM+16,length),jnp.bfloat16)])
    return pl.pallas_call(functools.partial(fwd2_kernel,block),grid_spec=spec,
        out_shape=[jax.ShapeDtypeStruct((length,lanes),jnp.bfloat16),jax.ShapeDtypeStruct((1,8,length),jnp.float32)],
        compiler_params=pltpu.CompilerParams(vmem_limit_bytes=60*1024*1024),
        cost_estimate=pl.CostEstimate(flops=29*length*length*lanes,bytes_accessed=8*length*lanes,transcendentals=0),
        name="attend_forward")(firsts,lasts,q,k,v,start[None,:],*earlier)

def backward_kernel(block,full_end,some_end,q_ref,k_ref,v_ref,d_ref,o_ref,lse_ref,start_ref,cos_ref,sin_ref,*rest):
    p_ref,first_ref,dq_ref,delta_ref=rest[-4:]
    j=pl.program_id(1)
    length,lanes=q_ref.shape
    heads=lanes//HEAD_DIM
    @pl.when(j==0)
    def _():
        dq_ref[...]=jnp.zeros_like(dq_ref)
        for i in range(length//block):
            rows=pl.ds(i*block,block)
            prod=jnp.transpose(d_ref[rows,:].astype(jnp.float32)*o_ref[rows,:].astype(jnp.float32))
            for n in range(heads):
                delta_ref[n:n+1,rows]=jnp.sum(prod[n*HEAD_DIM:(n+1)*HEAD_DIM],axis=0,keepdims=True)
    k=k_ref[...]; v=v_ref[...]
    scale=HEAD_DIM**-0.5
    kl=[only_head(k,n,lanes) for n in range(heads)]
    ks=[x*jnp.asarray(scale,k.dtype) for x in kl]
    vs=[only_head(v,n,lanes) for n in range(heads)]
    part=256 if block%256==0 else block
    def terms(masked,keys,at,size):
        rows=pl.ds(pl.multiple_of(at,part),size)
        q=q_ref[rows,:]; d=d_ref[rows,:]
        ss=[dot(x[keys],q,NT) for x in ks]
        dps=[dot(x[keys],d,NT) for x in vs]
        if masked:
            shape=ss[0].shape
            key=j*block+keys.start+lax.broadcasted_iota(jnp.int32,shape,0)
            query=at+lax.broadcasted_iota(jnp.int32,shape,1)
            allowed=(key<=query)&(key>=start_ref[0:1,rows])
            ss=[jnp.where(allowed,s,masked_score) for s in ss]
        ps=[jnp.exp(ss[n]-lse_ref[0,n:n+1,rows]) for n in range(heads)]
        dss=[(ps[n]*(dps[n]-delta_ref[n:n+1,rows])).astype(jnp.bfloat16) for n in range(heads)]
        pv=[dot(p.astype(jnp.bfloat16),d,NN) for p in ps]
        pk=[dot(x,q,NN) for x in dss]
        dq_ref[rows,:]+=sum(dot(dss[n],ks[n][keys],TN) for n in range(heads))
        if heads==2:
            lane=lax.broadcasted_iota(jnp.int32,pv[0].shape,1)<HEAD_DIM
            return jnp.where(lane,pk[0],pk[1]),jnp.where(lane,pv[0],pv[1])
        return pk[0],pv[0]
    def step(masked,i,carry):
        dk,dv=terms(masked,slice(0,block),i*block,block)
        return carry[0]+dk,carry[1]+dv
    pieces=[terms(True,slice(at,at+part),j*block+at,block-at) for at in range(0,block,part)]
    carry=tuple(jnp.concatenate(x,axis=0) if len(x)>1 else x[0] for x in zip(*pieces))
    carry=lax.fori_loop(j+1,full_end[j],functools.partial(step,False),carry)
    dk,dv=lax.fori_loop(full_end[j],some_end[j],functools.partial(step,True),carry)
    here=pl.ds(pl.multiple_of(j*block,block),block)
    p_ref[here,lanes:2*lanes]=turned(dk*scale,cos_ref[here,:],-sin_ref[here,:]).astype(jnp.bfloat16)
    blend=dv.astype(jnp.bfloat16).astype(jnp.float32)
    p_ref[here,2*lanes:]=(blend_weight*blend).astype(jnp.bfloat16)
    first_ref[...]=((1.0-blend_weight)*blend).astype(jnp.bfloat16)
    @pl.when(j==pl.num_programs(1)-1)
    def _():
        for i in range(length//block):
            rows=pl.ds(i*block,block)
            p_ref[rows,:lanes]=turned(dq_ref[rows,:],cos_ref[rows,:],-sin_ref[rows,:]).astype(jnp.bfloat16)

def attend_backward(q,k,v,d,start,cosine,sine,block,group,o,lse,before=(),earlier=()):
    length,width=q.shape
    lanes=cosine.shape[1]; n=length//block
    lasts=start[block-1::block]
    edge=jnp.arange(n,dtype=jnp.int32)
    full_end=jnp.maximum(edge+1,jnp.sum((lasts[None,:]<=edge[:,None]*block).astype(jnp.int32),axis=1))
    reach=jnp.sum((start[None,:]<=edge[:,None]*block+block-1).astype(jnp.int32),axis=1)
    some_end=jnp.maximum(full_end,(reach+block-1)//block)
    whole=pl.BlockSpec((length,lanes),lambda g,j,*_:(0,group))
    part=pl.BlockSpec((block,lanes),lambda g,j,*_:(j,group))
    table=pl.BlockSpec((length,lanes),lambda g,j,*_:(0,0))
    more=list(earlier)+list(before)
    spec=pltpu.PrefetchScalarGridSpec(num_scalar_prefetch=2,grid=(1,n),
        in_specs=[whole,part,part,whole,table,pl.BlockSpec((1,8,length),lambda g,j,*_:(0,0,0)),pl.BlockSpec((1,length),lambda g,j,*_:(0,0)),table,table]+[pl.BlockSpec(memory_space=pl.ANY)]*len(more),
        out_specs=[pl.BlockSpec((length,3*lanes),lambda g,j,*_:(0,group)),part],
        scratch_shapes=[pltpu.VMEM((length,lanes),jnp.float32),pltpu.VMEM((8,length),jnp.float32)])
    return pl.pallas_call(functools.partial(backward_kernel,block),grid_spec=spec,
        out_shape=[jax.ShapeDtypeStruct((length,3*width),jnp.bfloat16),jax.ShapeDtypeStruct((length,width),jnp.bfloat16)],
        input_output_aliases={11+len(earlier)+k:k for k in range(len(before))},
        compiler_params=pltpu.CompilerParams(vmem_limit_bytes=56*1024*1024),
        cost_estimate=pl.CostEstimate(flops=52*length*length*lanes,bytes_accessed=22*length*lanes,transcendentals=0),
        name="attend_backward")(full_end,some_end,q,k,v,d,o,lse,start[None,:],cosine,sine,*more)


f32 = jnp.float32
bf16 = jnp.bfloat16
everywhere = pl.BlockSpec(memory_space=pl.ANY)


def swap(x, axis, mask):
    return lax.ppermute(x, axis, [(i, i ^ mask) for i in range(lax.axis_size(axis))])


def cut_of(rows):
    half = rows // 2
    return half - half % 8 if half >= 8 else half


def after(x, *earlier):
    def kernel(*refs):
        pass

    return pl.pallas_call(
        kernel,
        in_specs=[everywhere] * (1 + len(earlier)),
        out_specs=everywhere,
        out_shape=jax.ShapeDtypeStruct(x.shape, x.dtype),
        input_output_aliases={0: 0},
        name="after",
    )(x, *earlier)


def spread_relay(x, axis):
    count = lax.axis_size(axis)
    if count != 4:
        return [[x]] + [[swap(x, axis, e)] for e in range(1, count)]
    cut = cut_of(x.shape[0])
    one, two = swap(x, axis, 1), swap(x, axis, 2)
    return [[x], [one], [two], [swap(two[:cut], axis, 1), swap(one[cut:], axis, 2)]]


def spread(x, axis):
    return [x] + [swap(x, axis, e) for e in range(1, lax.axis_size(axis))]


def add_low(*terms):
    return sum(t.astype(f32) for t in terms).astype(bf16)


def collect(parts, axis):
    return sum((swap(p, axis, e) if e else p).astype(f32) for e, p in enumerate(parts))


def in_order(parts, rank):
    rows = parts[0].shape[0]
    whole = jnp.zeros((len(parts) * rows,) + parts[0].shape[1:], parts[0].dtype)
    for e, part in enumerate(parts):
        whole = lax.dynamic_update_slice_in_dim(whole, part, (rank ^ e) * rows, 0)
    return whole


def block_of(x, number, rows):
    return lax.dynamic_slice_in_dim(x, number * rows, rows, 0)


def both_cores(own, other, core):
    first = core == 0
    return jnp.concatenate([jnp.where(first, own, other), jnp.where(first, other, own)])


def sum_over_all(x):
    for axis in ("mlp", "dp", "head"):
        count = lax.axis_size(axis)
        if count == 4:
            x = (x + swap(x, axis, 1)) + (swap(x, axis, 2) + swap(x, axis, 3))
            continue
        mask = 1
        while mask < count:
            x = x + swap(x, axis, mask)
            mask *= 2
    return x


def rms_scale(rows):
    return lax.rsqrt(jnp.mean(rows * rows, axis=-1, keepdims=True) + epsilon)


def norm_back(rows, scale, gain, grad):
    weighted = grad * gain
    return scale * weighted - rows * scale * scale * scale * jnp.mean(
        weighted * rows, axis=-1, keepdims=True
    )


def turned(x, cosine, sine):
    half = HEAD_DIM // 2
    if x.shape[1] == HEAD_DIM:
        other = jnp.concatenate([x[:, half:], x[:, :half]], axis=1)
    else:
        lanes = x.shape[1]
        lane = lax.broadcasted_iota(jnp.int32, x.shape, 1)
        other = jnp.where(
            lane % HEAD_DIM < half, pltpu.roll(x, lanes - half, 1), pltpu.roll(x, half, 1)
        )
    return x * cosine + other * sine


def load_rows(refs, counts, number, target):
    at = 0
    for k, pieces in enumerate(counts):
        mine = refs[at : at + pieces]
        at += pieces

        @pl.when(number == k)
        def _(mine=mine):
            row = 0
            for ref in mine:
                target[row : row + ref.shape[0], :] = ref[...]
                row += ref.shape[0]


def project_kernel(counts, rank_ref, *refs):
    total = sum(counts)
    parts, (w_ref, gain_ref, cos_ref, sin_ref, first_ref) = refs[:total], refs[total : total + 5]
    a_ref, q_ref, k_ref, v_ref, norm_ref, rows_ref = refs[-6:]
    i = pl.program_id(0)
    load_rows(parts, counts, i, rows_ref)
    x = rows_ref[...].astype(f32)
    a = (x * rms_scale(x) * gain_ref[...]).astype(bf16)
    a_ref[...] = a
    width = q_ref.shape[1]
    lanes = cos_ref.shape[1]
    cosine, sine = cos_ref[...], sin_ref[...]
    joined = dot(a, w_ref[...], NN)
    of = lax.broadcasted_iota(jnp.int32, (lanes, 128), 0) // HEAD_DIM
    one_hot = (of == lax.broadcasted_iota(jnp.int32, (lanes, 128), 1)).astype(f32)

    def norms(value):
        squares = lax.dot_general(
            value * value, one_hot, NN, precision=lax.Precision.HIGHEST, preferred_element_type=f32
        )
        return jnp.sum(jnp.sqrt(jnp.maximum(squares, 0.0)), axis=0, keepdims=True)

    @pl.when(i == 0)
    def _():
        norm_ref[...] = jnp.zeros_like(norm_ref)

    for g in range(width // lanes):
        at = slice(g * lanes, (g + 1) * lanes)
        query, key, value = (
            joined[:, (3 * g + k) * lanes : (3 * g + k + 1) * lanes] for k in range(3)
        )
        q_ref[:, at] = turned(query, cosine, sine).astype(bf16)
        k_ref[:, at] = turned(key, cosine, sine).astype(bf16)
        first = first_ref[:, at].astype(f32)
        blended = blend_weight * value + (1.0 - blend_weight) * first
        v_ref[:, at] = blended.astype(bf16)
        norm_ref[0:1, :] += norms(first)
        norm_ref[1:2, :] += norms(blended)


def spec_whole(x):
    return pl.BlockSpec(x.shape, lambda *_: (0,) * x.ndim)


def cost(us):
    return pl.CostEstimate(flops=int(us * 1.1e9), bytes_accessed=int(us * 1e5), transcendentals=0)


big = pltpu.CompilerParams(vmem_limit_bytes=56 * 1024 * 1024)


def project(rank, parts, base, weights, gain, cosine, sine, firsts, before=()):
    counts = tuple(len(p) for p in parts)
    flat = [x for p in parts for x in p]
    chunk = sum(x.shape[0] for x in parts[0])
    length, width = firsts.shape
    model, lanes = flat[0].shape[1], cosine.shape[1]
    there = lambda i, r: (r[0] ^ (base + i), 0)
    block = lambda n: pl.BlockSpec((chunk, n), there)
    spec = pltpu.PrefetchScalarGridSpec(
        num_scalar_prefetch=1,
        grid=(len(parts),),
        in_specs=[spec_whole(x) for x in flat]
        + [spec_whole(weights), spec_whole(gain), block(lanes), block(lanes), block(width)]
        + [everywhere] * len(before),
        out_specs=[block(model), block(width), block(width), block(width)]
        + [pl.BlockSpec((8, 128), lambda i, r: (0, 0))],
        scratch_shapes=[pltpu.VMEM((chunk, model), bf16)],
    )
    low = jax.ShapeDtypeStruct((length, width), bf16)
    return pl.pallas_call(
        functools.partial(project_kernel, counts),
        grid_spec=spec,
        out_shape=[jax.ShapeDtypeStruct((length, model), bf16), low, low, low]
        + [jax.ShapeDtypeStruct((8, 128), f32)],
        input_output_aliases={len(flat) + 6 + k: k for k in range(len(before))},
        compiler_params=big,
        cost_estimate=cost(4.5 * len(parts)),
        name="project",
    )(rank[None], *flat, weights, gain, cosine, sine, firsts, *before)


def assemble_kernel(ranks, rank_ref, *refs):
    far_ref, out_ref = refs[-2:]
    rows = far_ref.shape[2]
    e = pl.program_id(0)
    for k in range(ranks):

        @pl.when(e == k)
        def _(ref=refs[k]):
            for a in range(3):
                far_ref[a, 0] = ref[a * rows : (a + 1) * rows, :]
            out_ref[0] = ref[3 * rows :, :]


def assemble(rank, bundles, rows, earlier):
    ranks = len(bundles)
    wide, model = bundles[0].shape
    spec = pltpu.PrefetchScalarGridSpec(
        num_scalar_prefetch=1,
        grid=(ranks,),
        in_specs=[spec_whole(b) for b in bundles] + [everywhere] * len(earlier),
        out_specs=[
            pl.BlockSpec((3, 1, rows, model), lambda e, r: (0, e, 0, 0)),
            pl.BlockSpec((1, wide - 3 * rows, model), lambda e, r: (r[0] ^ e, 0, 0)),
        ],
    )
    return pl.pallas_call(
        functools.partial(assemble_kernel, ranks),
        grid_spec=spec,
        out_shape=[
            jax.ShapeDtypeStruct((3, ranks, rows, model), bf16),
            jax.ShapeDtypeStruct((ranks, wide - 3 * rows, model), bf16),
        ],
        compiler_params=big,
        cost_estimate=cost(3),
        name="assemble",
    )(rank[None], *bundles, *earlier)


def feed_kernel(x_ref, g_ref, *refs):
    sources, (act_ref, in_ref, sum_ref) = (refs[0:3], refs[3:6], refs[6:9]), refs[-3:]
    f = pl.program_id(0)
    steps = pl.num_programs(0)

    @pl.when(f == 0)
    def _():
        sum_ref[...] = jnp.zeros_like(sum_ref)

    def work(gate_w, up_w, down_w):
        x, g = x_ref[...], g_ref[...]
        gate, up = dot(gate_w[...], x, NT), dot(up_w[...], x, NT)
        hidden_grad = dot(down_w[...], g, NT)
        sigma = 1.0 / (1.0 + jnp.exp(-gate))
        gate_sigma = gate * sigma
        hidden = (gate_sigma * up).astype(bf16)
        gate_grad = (hidden_grad * up * (sigma + gate_sigma * (1.0 - sigma))).astype(bf16)
        up_grad = (hidden_grad * gate_sigma).astype(bf16)
        act_ref[0, 0], act_ref[0, 1], act_ref[0, 2] = gate_grad, up_grad, hidden
        sum_ref[...] += dot(gate_grad, gate_w[...], TN) + dot(up_grad, up_w[...], TN)

    for k, condition in enumerate((f < 2, f == 2, f == 3)):

        @pl.when(condition)
        def _(k=k):
            work(*sources[k])

    @pl.when(f == steps - 1)
    def _():
        in_ref[...] = sum_ref[...].astype(in_ref.dtype)


def feed(x, grad, own, far, far_other, dtype, earlier=()):
    tokens, model = x.shape
    part = own.shape[0] // 6
    block = lambda at: pl.BlockSpec((part, model), at)
    return pl.pallas_call(
        feed_kernel,
        grid=(4,),
        in_specs=[spec_whole(x), spec_whole(grad)]
        + [block(lambda f, a=a: (2 * a + jnp.minimum(f, 1), 0)) for a in range(3)]
        + [block(lambda f, a=a: (a, 0)) for a in range(3)] * 2
        + [everywhere] * len(earlier),
        out_specs=[
            pl.BlockSpec((1, 3, part, tokens), lambda f: (f, 0, 0, 0)),
            pl.BlockSpec((tokens, model), lambda f: (0, 0)),
        ],
        out_shape=[
            jax.ShapeDtypeStruct((4, 3, part, tokens), bf16),
            jax.ShapeDtypeStruct((tokens, model), dtype),
        ],
        scratch_shapes=[pltpu.VMEM((tokens, model), f32)],
        compiler_params=big,
        cost_estimate=cost(16),
        name="feed",
    )(x, grad, *([own] * 3), *([far] * 3), *([far_other] * 3), *earlier)


def half_grads(act_ref, near_ref, x_ref, xn_ref, g_ref, gn_ref, result_ref):
    a = pl.program_id(0)

    @pl.when(a < 2)
    def _():
        result_ref[...] = dot(act_ref[0, 0], x_ref[...], NN) + dot(near_ref[0, 0], xn_ref[...], NN)

    @pl.when(a == 2)
    def _():
        result_ref[...] = dot(act_ref[0, 0], g_ref[...], NN) + dot(near_ref[0, 0], gn_ref[...], NN)


def other_grads_kernel(scalars, *refs):
    out_ref, result_ref = refs[-2:]
    half_grads(*refs[:6], result_ref)
    out_ref[...] = result_ref[...].astype(bf16)


def far_grads_kernel(ranks, scalars, *refs):
    got_ref, out_refs, result_ref = refs[6], refs[7 : 7 + ranks], refs[-1]
    half_grads(*refs[:6], result_ref)
    rows = result_ref.shape[0] // ranks
    for e in range(ranks):
        at = slice(e * rows, (e + 1) * rows)
        out_refs[e][0] = (result_ref[at, :] + got_ref[at, :].astype(f32)).astype(bf16)


def own_grads_kernel(ranks, scalars, *refs):
    got_ref, out_ref, out_got_ref = refs[6:9]
    own_refs, result_ref = refs[9 : 9 + ranks], refs[-1]
    half_grads(*refs[:6], result_ref)
    i = pl.program_id(0)
    rows = result_ref.shape[0] // ranks
    result_ref[...] += got_ref[...].astype(f32)

    @pl.when(i == 0)
    def _():
        for e in range(ranks):
            number = scalars[1] ^ e
            both = out_ref[number].astype(f32) + out_got_ref[number].astype(f32)
            own_refs[e][3 * rows :, :] = both.astype(bf16)

    for a in range(3):

        @pl.when(i == a)
        def _(a=a):
            to = slice(a * rows, (a + 1) * rows)
            for e in range(ranks):
                if rows % 8 == 0:
                    at = pl.ds(pl.multiple_of((scalars[1] ^ e) * rows, 8), rows)
                    own_refs[e][to, :] = result_ref[at, :].astype(bf16)
                else:
                    for h in range(ranks):

                        @pl.when(scalars[1] ^ e == h)
                        def _(e=e, h=h):
                            own_refs[e][to, :] = result_ref[h * rows : (h + 1) * rows, :].astype(bf16)


def shard_grads(scalars, ranks, far, here, near, x, x_near, grad, grad_near, got=None):
    _, _, part, tokens = here.shape
    model = x.shape[1]
    if got is None:
        number = lambda c: 3 if far else 1 - c[0]
    else:
        number = lambda c: 2 if far else c[0]
    act = pl.BlockSpec((1, 1, part, tokens), lambda i, c: (number(c), i, 0, 0))
    in_specs = [act, act] + [spec_whole(x)] * 4
    args = [here, near, x, x_near, grad, grad_near]
    row_block = pl.BlockSpec((part, model), lambda i, c: (i, 0))
    rows = part // ranks
    if got is None:
        kernel, out_specs = other_grads_kernel, row_block
        out_shape = jax.ShapeDtypeStruct((3 * part, model), bf16)
    elif far:
        kernel = functools.partial(far_grads_kernel, ranks)
        in_specs.append(row_block)
        args += got
        out_specs = [pl.BlockSpec((1, rows, model), lambda i, c: (i, 0, 0))] * ranks
        out_shape = [jax.ShapeDtypeStruct((3, rows, model), bf16)] * ranks
    else:
        kernel = functools.partial(own_grads_kernel, ranks)
        in_specs += [row_block] + [spec_whole(g) for g in got[1:]]
        args += got
        wide = 3 * rows + got[1].shape[1]
        out_specs = [pl.BlockSpec((wide, model), lambda i, c: (0, 0))] * ranks
        out_shape = [jax.ShapeDtypeStruct((wide, model), bf16)] * ranks
    spec = pltpu.PrefetchScalarGridSpec(
        num_scalar_prefetch=1,
        grid=(3,),
        in_specs=in_specs,
        out_specs=out_specs,
        scratch_shapes=[pltpu.VMEM((part, model), f32)],
    )
    return pl.pallas_call(
        kernel,
        grid_spec=spec,
        out_shape=out_shape,
        compiler_params=big,
        cost_estimate=cost(8),
        name=("far" if far else "own") + ("_other" if got is None else "_sum"),
    )(scalars, *args)


def others_kernel(scalars, act_ref, near_ref, x_ref, xn_ref, g_ref, gn_ref, *refs):
    own_ref, far_ref, far_other_ref, far_out, own_out, out_ref, out_near_ref, sum_ref = refs
    i = pl.program_id(0)
    for a in range(6):

        @pl.when(i == a)
        def _(a=a):
            first, second = (x_ref, xn_ref) if a % 3 < 2 else (g_ref, gn_ref)
            target = far_out if a < 3 else own_out
            target[...] = (
                dot(act_ref[0, 0], first[...], NN) + dot(near_ref[0, 0], second[...], NN)
            ).astype(bf16)

    @pl.when(i == 5)
    def _():
        sum_ref[...] = jnp.zeros_like(sum_ref)

    for condition, ref in (((i == 6) | (i == 7), own_ref), (i == 8, far_ref), (i == 9, far_other_ref)):

        @pl.when(condition)
        def _(ref=ref):
            sum_ref[0] += dot(act_ref[0, 0], ref[...], TN)
            sum_ref[1] += dot(near_ref[0, 0], ref[...], TN)

    @pl.when(i == 9)
    def _():
        out_ref[...] = sum_ref[0]
        out_near_ref[...] = sum_ref[1].astype(bf16)


def others(scalars, here, near, x, x_near, grad, grad_near, own, far, far_other):
    _, _, part, tokens = here.shape
    model = x.shape[1]

    def act_at(i, c):
        number = jnp.where(i < 3, 3, jnp.where(i < 6, 1 - c[0], i - 6))
        return (number, jnp.where(i < 6, i % 3, 2), 0, 0)

    act = pl.BlockSpec((1, 1, part, tokens), act_at)
    row = lambda at: pl.BlockSpec((part, model), at)
    spec = pltpu.PrefetchScalarGridSpec(
        num_scalar_prefetch=1,
        grid=(10,),
        in_specs=[act, act]
        + [spec_whole(x)] * 4
        + [row(lambda i, c: (4 + jnp.clip(i - 6, 0, 1), 0))]
        + [row(lambda i, c: (2, 0))] * 2,
        out_specs=[
            row(lambda i, c: (jnp.minimum(i, 2), 0)),
            row(lambda i, c: (jnp.clip(i - 3, 0, 2), 0)),
            spec_whole(x),
            spec_whole(x),
        ],
        scratch_shapes=[pltpu.VMEM((2, tokens, model), f32)],
    )
    half = jax.ShapeDtypeStruct((3 * part, model), bf16)
    return pl.pallas_call(
        others_kernel,
        grid_spec=spec,
        out_shape=[half, half]
        + [jax.ShapeDtypeStruct((tokens, model), f32), jax.ShapeDtypeStruct((tokens, model), bf16)],
        compiler_params=big,
        cost_estimate=cost(19),
        name="others",
    )(scalars, here, near, x, x_near, grad, grad_near, own, far, far_other)


def regroup_kernel(ranks, rank_ref, *refs):
    out_ref = refs[-1]
    rows = out_ref.shape[2]
    e = pl.program_id(0)
    for k in range(ranks):

        @pl.when(e == k)
        def _(k=k):
            low, high = refs[2 * k], refs[2 * k + 1]
            cut = low.shape[0]
            for a in range(3):
                first, last = a * rows, (a + 1) * rows
                if last <= cut:
                    out_ref[a, 0] = low[first:last, :]
                elif first >= cut:
                    out_ref[a, 0] = high[first - cut : last - cut, :]
                else:
                    out_ref[a, 0, : cut - first] = low[first:, :]
                    out_ref[a, 0, cut - first :] = high[: last - cut, :]


def regroup(rank, pieces, rows, earlier=()):
    ranks = len(pieces)
    flat, specs = [], []
    for low, high in pieces:
        for x, at, size in (low, high):
            flat.append(x)
            specs.append(pl.BlockSpec((size, x.shape[1]), lambda e, r, at=at: (at, 0)))
    model = flat[0].shape[1]
    spec = pltpu.PrefetchScalarGridSpec(
        num_scalar_prefetch=1,
        grid=(ranks,),
        in_specs=specs + [everywhere] * len(earlier),
        out_specs=pl.BlockSpec((3, 1, rows, model), lambda e, r: (0, r[0] ^ e, 0, 0)),
    )
    return pl.pallas_call(
        functools.partial(regroup_kernel, ranks),
        grid_spec=spec,
        out_shape=jax.ShapeDtypeStruct((3, ranks, rows, model), bf16),
        compiler_params=big,
        cost_estimate=cost(2),
        name="regroup",
    )(rank[None], *flat, *earlier)


def unproject_kernel(counts, cuts, rank_ref, *refs):
    total = sum(counts)
    parts, w_ref, p_ref = refs[:total], refs[total], refs[total + 1]
    pieces = sum(len(c) for c in cuts)
    outs, gain_ref, rows_ref = refs[-2 - pieces : -2], refs[-2], refs[-1]
    i = pl.program_id(0)
    load_rows(parts, counts, i, rows_ref)
    x = rows_ref[...].astype(f32)
    grad = dot(p_ref[...], w_ref[...], NT)
    at = 0
    for k, sizes in enumerate(cuts):
        mine = outs[at : at + len(sizes)]
        at += len(sizes)

        @pl.when(i == k)
        def _(mine=mine):
            row = 0
            for ref in mine:
                ref[...] = grad[row : row + ref.shape[0]].astype(bf16)
                row += ref.shape[0]

    @pl.when(i == 0)
    def _():
        gain_ref[...] = jnp.zeros_like(gain_ref)

    gain_ref[...] += jnp.sum(grad * (x * rms_scale(x)), axis=0, keepdims=True)


def unproject(rank, parts, base, cuts, weights, grads, earlier=()):
    counts = tuple(len(p) for p in parts)
    flat = [x for p in parts for x in p]
    chunk, model = sum(x.shape[0] for x in parts[0]), flat[0].shape[1]
    block = lambda n: pl.BlockSpec((chunk, n), lambda i, r: (r[0] ^ (base + i), 0))
    sizes = [n for c in cuts for n in c]
    spec = pltpu.PrefetchScalarGridSpec(
        num_scalar_prefetch=1,
        grid=(len(parts),),
        in_specs=[spec_whole(x) for x in flat]
        + [spec_whole(weights)]
        + [block(grads.shape[1])]
        + [everywhere] * len(earlier),
        out_specs=[pl.BlockSpec((n, model), lambda i, r: (0, 0)) for n in sizes]
        + [pl.BlockSpec((1, model), lambda i, r: (0, 0))],
        scratch_shapes=[pltpu.VMEM((chunk, model), bf16)],
    )
    out = pl.pallas_call(
        functools.partial(unproject_kernel, counts, cuts),
        grid_spec=spec,
        out_shape=[jax.ShapeDtypeStruct((n, model), bf16) for n in sizes]
        + [jax.ShapeDtypeStruct((1, model), f32)],
        compiler_params=big,
        cost_estimate=cost(3.5 * len(parts)),
        name="unproject",
    )(rank[None], *flat, weights, grads, *earlier)
    return out[:-1], out[-1]


def state_kernel(back_ref, terms_ref, hidden_ref, grad_ref, gain_ref, w_ref, state_ref, low_ref, mixed_ref, sum_ref):
    hidden, gain = hidden_ref[...], gain_ref[...]
    grad = back_ref[...].astype(f32) + terms_ref[...]
    scale = rms_scale(hidden)
    state = grad_ref[...].astype(f32) + norm_back(hidden, scale, gain, grad)
    low = state.astype(bf16)
    state_ref[...] = state
    low_ref[...] = low
    for h in range(mixed_ref.shape[0]):
        mixed_ref[h] = dot(low, w_ref[h], NT).astype(bf16)

    @pl.when(pl.program_id(0) == 0)
    def _():
        sum_ref[...] = jnp.zeros_like(sum_ref)

    sum_ref[...] += jnp.sum(grad * hidden * scale, axis=0, keepdims=True)


def state_back(back, terms, hidden, grad, gain, weights):
    tokens, model = back.shape
    ranks, width, _ = weights.shape
    size = 128 if tokens % 128 == 0 else tokens
    row = pl.BlockSpec((size, model), lambda i: (i, 0))
    return pl.pallas_call(
        state_kernel,
        grid=(tokens // size,),
        in_specs=[row, row, row, row, spec_whole(gain), spec_whole(weights)],
        out_specs=[
            row,
            row,
            pl.BlockSpec((ranks, size, width), lambda i: (0, i, 0)),
            pl.BlockSpec((1, model), lambda i: (0, 0)),
        ],
        out_shape=[
            jax.ShapeDtypeStruct((tokens, model), f32),
            jax.ShapeDtypeStruct((tokens, model), bf16),
            jax.ShapeDtypeStruct((ranks, tokens, width), bf16),
            jax.ShapeDtypeStruct((1, model), f32),
        ],
        compiler_params=big,
        cost_estimate=cost(6),
        name="state_back",
    )(back, terms, hidden, grad, gain, weights)


def on_device(
    tokens,
    first_values,
    segment_ids,
    positions,
    attn_gain,
    w_query,
    w_key,
    w_value,
    w_out,
    mlp_gain,
    w_gate,
    w_up,
    w_down,
    out_grad,
):
    core, rank = lax.axis_index("dp"), lax.axis_index("head")
    ranks = lax.axis_size("head")
    chunk, width = tokens.shape[0], w_query.shape[1]
    model = tokens.shape[2]
    length, ff = segment_ids.shape[0], w_gate.shape[1]
    block = min(512, length)
    tokens, firsts, out_grad = tokens[:, 0], first_values[:, 0], out_grad[:, 0]
    places = positions[:, 0]
    start = jnp.arange(length, dtype=jnp.int32) - places

    row_parts = spread_relay(tokens, "head")

    part = ff // 2
    rows = part // ranks
    stack = jnp.concatenate([w_gate.T, w_up.T, w_down])
    cut_stack = stack.reshape(3, 2 * ranks, rows, model)
    far_piece = swap(
        lax.dynamic_index_in_dim(cut_stack, core * ranks + rank, 1, False), "mlp", 2
    ).reshape(3 * rows, model)
    out_grad_near = swap(out_grad, "mlp", 1)
    half_out = width // 2
    far_piece = after(far_piece, *row_parts[-1])
    bundle = jnp.concatenate([far_piece, block_of(w_out, core, half_out)])
    bundles = spread(bundle, "head")

    lanes = min(128, width)
    w_project = jnp.concatenate(
        [
            w[:, g * lanes : (g + 1) * lanes]
            for g in range(width // lanes)
            for w in (w_query, w_key, w_value)
        ],
        axis=1,
    )
    lane = jnp.arange(lanes)
    freq = theta_base ** (-(lane % (HEAD_DIM // 2)).astype(f32) * 2.0 / HEAD_DIM)
    angles = places.astype(f32)[:, None] * freq
    cosine = jnp.cos(angles)
    sine = jnp.sin(angles) * jnp.where(lane % HEAD_DIM < HEAD_DIM // 2, -1.0, 1.0)
    heads_args = (w_project, attn_gain[None], cosine, sine, firsts)
    soon = 3 if ranks == 4 else ranks
    *projected, norms = project(rank, row_parts[:soon], 0, *heads_args)
    if soon < ranks:
        *projected, more = project(rank, row_parts[soon:], soon, *heads_args, projected)
        norms = norms + more
    gathered, queries, keys, values = projected
    groups = width // lanes
    mixed, log_total, mixed_here = [], [], []
    for g in range(groups):
        one_mixed, one_total = attend_forward2(
            queries, keys, values, start, min(1024, length), g, tuple(mixed[-1:])
        )
        mixed.append(one_mixed)
        log_total.append(one_total)
        mixed_here.append(
            lax.all_to_all(one_mixed, "head", 0, 0, tiled=True).reshape(ranks, chunk, lanes)
        )

    far_half, out_half = assemble(rank, bundles, rows, (mixed_here[0], mixed[-1]))
    far_half = far_half.reshape(3 * part, model)
    far_other, out_other = swap(far_half, "dp", 1), swap(out_half, "dp", 1)
    first = core == 0
    out_all = jnp.concatenate(
        [jnp.where(first, out_half, out_other), jnp.where(first, out_other, out_half)], axis=1
    )

    residual = tokens.astype(f32)
    hidden_state = residual + sum(
        jnp.einsum("htk,hkd->td", m, out_all[:, g * lanes : (g + 1) * lanes], preferred_element_type=f32)
        for g, m in enumerate(mixed_here)
    )
    mlp_scale = rms_scale(hidden_state)
    mlp_input = (hidden_state * mlp_scale * mlp_gain).astype(bf16)
    mlp_input_near = swap(mlp_input, "mlp", 1)

    acts, terms = feed(mlp_input, out_grad, stack, far_half, far_other, f32)
    acts_near, terms_near = feed(
        mlp_input_near, out_grad_near, stack, far_half, far_other, bf16, (terms,)
    )
    terms_back = swap(terms_near, "mlp", 1)
    scalars = jnp.stack([core, rank]).astype(jnp.int32)
    tokens_two = (acts, acts_near, mlp_input, mlp_input_near, out_grad, out_grad_near)
    far_other_grads, own_other_grads, down_here, down_near = others(
        scalars, *tokens_two, stack, far_half, far_other
    )
    terms_back = after(terms_back, down_near)
    far_half_got = swap(after(far_other_grads, terms_back), "dp", 1)
    own_half_got = swap(after(own_other_grads, far_half_got), "dp", 1)
    state_grad, state_grad_low, mixed_grad, mlp_gain_grad = state_back(
        terms_back, terms, hidden_state, out_grad, mlp_gain[None], out_all
    )
    mlp_gain_grad = mlp_gain_grad[0]
    mixed_grad_rows = lax.all_to_all(mixed_grad, "head", 0, 0, tiled=True).reshape(length, width)

    low_grad = after(state_grad_low, mixed_grad)
    out_grads = [
        jnp.einsum("htk,td->hkd", m, low_grad, preferred_element_type=f32).astype(bf16)
        for m in mixed_here
    ]
    out_grads = jnp.concatenate(out_grads, axis=1).reshape(ranks, 2, half_out, model)
    out_got = swap(lax.dynamic_index_in_dim(out_grads, 1 - core, 1, False), "dp", 1)
    out_own = lax.dynamic_index_in_dim(out_grads, core, 1, False)
    far_half_got = after(far_half_got, mixed_grad)
    far_chip = shard_grads(scalars, ranks, True, *tokens_two, [far_half_got])
    far_got = [swap(f, "head", e) for e, f in enumerate(far_chip) if e]
    mixed_grad_rows = after(mixed_grad_rows, far_chip[0])

    back_args = (queries, keys, values, mixed_grad_rows, start, cosine, sine, block)
    grads = attend_backward(*back_args, 0, mixed[0], log_total[0])
    own_half_got = after(own_half_got, grads[0])
    own_chip = shard_grads(scalars, ranks, False, *tokens_two, [own_half_got, out_own, out_got])
    far_got = [after(f, own_chip[0]) for f in far_got]
    far_sum = add_low(far_chip[0], *far_got)
    far_here = swap(far_sum, "mlp", 2)
    own_chip = [own_chip[0]] + [after(f, far_sum) for f in own_chip[1:]]
    own_got = [swap(f, "head", e) for e, f in enumerate(own_chip) if e]
    down_back = swap(after(down_near, own_chip[0]), "mlp", 1)
    for g in range(1, width // lanes):
        grads = attend_backward(
            *back_args, g, mixed[g], log_total[g], grads, (far_sum, *own_chip[1:])
        )
    proj_grad, first_values_grad = grads
    cut = cut_of(chunk)
    half_proj = model // 2
    proj_wgrad = dot(gathered, proj_grad, TN).astype(bf16)
    if ranks == 4:
        (low, high), gain_last = unproject(
            rank, row_parts[3:], 3, ((cut, chunk - cut),), w_project, proj_grad, (proj_wgrad, down_back)
        )
        for_two, for_one = swap(low, "head", 1), swap(high, "head", 2)
        own_got = [after(f, low) for f in own_got]
    else:
        own_got = [after(f, proj_grad) for f in own_got]
    own_all = (own_chip[0], *own_got)
    piece_sum = add_low(*(f[: 3 * rows] for f in own_all), far_here.reshape(3 * rows, model))
    out_sum = add_low(*(f[3 * rows :] for f in own_all))
    proj_got = swap(after(block_of(proj_wgrad, 1 - core, half_proj), own_got[-1]), "dp", 1)
    proj_mine = add_low(block_of(proj_wgrad, core, half_proj), proj_got)
    both_mine = jnp.concatenate([proj_mine, out_sum.reshape(half_proj, -1)], axis=1)
    line, count = lax.axis_index("mlp"), lax.axis_size("mlp")

    def line_sum(x):
        size = x.shape[0] // count
        return collect([block_of(x, line ^ e, size) for e in range(count)], "mlp").astype(bf16)

    if ranks == 4:
        cut_p = cut_of(3 * rows)
        cut_q = 3 * rows - cut_p
        (own, one, two), gain_rest = unproject(
            rank,
            row_parts[:3],
            0,
            ((chunk,),) * 3,
            w_project,
            proj_grad,
            (both_mine,),
        )
        attn_gain_grad = gain_last + gain_rest
        piece_sum = after(piece_sum, own)
        low_p, high_p = piece_sum[:cut_p], piece_sum[cut_p:]
        low_x, high_y = swap(low_p, "head", 1), swap(high_p, "head", 2)
        low_yy = swap(jnp.concatenate([low_p, low_x]), "head", 2)
        high_xx = swap(jnp.concatenate([high_p, high_y]), "head", 1)
        one = one.at[cut:].set(add_low(one[cut:], for_one))
        two = two.at[:cut].set(add_low(two[:cut], for_two))
        one_got, two_got = swap(one, "head", 1), swap(two, "head", 2)
        half_sum = regroup(
            rank,
            [
                ((low_p, 0, cut_p), (high_p, 0, cut_q)),
                ((low_x, 0, cut_p), (high_xx, 0, cut_q)),
                ((low_yy, 0, cut_p), (high_y, 0, cut_q)),
                ((low_yy, 1, cut_p), (high_xx, 1, cut_q)),
            ],
            rows,
        )
        line_piece = after(line_sum(both_mine), one, two)
        attn_normed_grad = own.astype(f32) + one_got.astype(f32) + two_got.astype(f32)
        ended = (one_got, two_got)
    else:
        parts, attn_gain_grad = unproject(
            rank, row_parts, 0, ((chunk,),) * ranks, w_project, proj_grad
        )
        half_sum = jnp.zeros((3, ranks, rows, model), bf16)
        for e, piece in enumerate(spread(piece_sum, "head")):
            piece = piece.reshape(3, 1, rows, model)
            half_sum = lax.dynamic_update_slice_in_dim(half_sum, piece, rank ^ e, 1)
        attn_normed_grad = collect(parts, "head")
        ended = (attn_normed_grad,)
        line_piece = line_sum(both_mine)
    half_sum = half_sum.reshape(3, part, model)

    norm_row = jnp.zeros((model,), f32).at[:2].set(jnp.sum(norms[:2], axis=1))
    if count == 4:
        line_one = swap(line_piece, "mlp", 1)
        line_two = swap(jnp.concatenate([line_piece, line_one]), "mlp", 2)
        size = line_piece.shape[0]
        line_got = [line_piece, line_one, line_two[:size], line_two[size:]]
    else:
        line_got = spread(line_piece, "mlp")
    small = jnp.stack([attn_gain_grad[0], mlp_gain_grad, norm_row])
    small = sum_over_all(after(small, line_got[1]))
    output = (hidden_state + after(down_back, line_piece).astype(f32) + down_here).astype(bf16)

    half_sum = after(half_sum, line_piece)
    other_sum = swap(half_sum, "dp", 1)
    ff_grads = jnp.concatenate(
        [jnp.where(first, half_sum, other_sum), jnp.where(first, other_sum, half_sum)], axis=1
    ).astype(f32)
    gate_wgrad, up_wgrad, down_wgrad = ff_grads[0].T, ff_grads[1].T, ff_grads[2]
    input_grad = (
        state_grad + norm_back(residual, rms_scale(residual), attn_gain, attn_normed_grad)
    ).astype(bf16)

    line_got = [after(line_got[0], output, input_grad, down_wgrad, small)] + line_got[1:]
    both_half = in_order(line_got, line)
    both_other = swap(both_half, "dp", 1)
    proj_sum = both_cores(both_half[:, : 3 * width], both_other[:, : 3 * width], core).astype(f32)
    query_wgrad, key_wgrad, value_wgrad = (
        jnp.concatenate(
            [proj_sum[:, (3 * g + k) * lanes : (3 * g + k + 1) * lanes] for g in range(width // lanes)],
            axis=1,
        )
        for k in range(3)
    )
    out_wgrad = both_cores(
        both_half[:, 3 * width :].reshape(half_out, model),
        both_other[:, 3 * width :].reshape(half_out, model),
        core,
    ).astype(f32)

    devices = lax.axis_size("dp") * ranks * count
    value_norms = small[2, :2] / (length * (width // HEAD_DIM) * devices)
    return (
        output[:, None],
        input_grad[:, None],
        first_values_grad[:, None],
        small[0],
        query_wgrad,
        key_wgrad,
        value_wgrad,
        out_wgrad,
        small[1],
        gate_wgrad,
        up_wgrad,
        down_wgrad,
        value_norms,
    )


def solution(mesh):
    placed = (
        P("head", ("dp", "mlp"), None),
        P(None, ("dp", "mlp"), "head"),
        P(None, ("dp", "mlp")),
        P(None, ("dp", "mlp")),
        P(),
        P(None, "head"),
        P(None, "head"),
        P(None, "head"),
        P("head", None),
        P(),
        P(None, "mlp"),
        P(None, "mlp"),
        P("mlp", None),
        P("head", ("dp", "mlp"), None),
    )
    return jax.shard_map(
        on_device,
        mesh=mesh,
        in_specs=placed,
        out_specs=(
            P("head", ("dp", "mlp"), None),
            P("head", ("dp", "mlp"), None),
            P(None, ("dp", "mlp"), "head"),
            P(),
            P(None, "head"),
            P(None, "head"),
            P(None, "head"),
            P("head", None),
            P(),
            P(None, "mlp"),
            P(None, "mlp"),
            P("mlp", None),
            P(),
        ),
        check_vma=False,
    )
```

```python
import functools

import jax
import jax.numpy as jnp
from jax import lax
from jax.experimental import pallas as pl
from jax.experimental.pallas import tpu as pltpu
from jax.sharding import PartitionSpec as P

HEAD_DIM = 64
epsilon = 1e-06
theta_base = 10000.0
blend_weight = 0.5
masked_score = -1e30
NT=(((1,),(1,)),((),()))
NN=(((1,),(0,)),((),()))
TN=(((0,),(0,)),((),()))
def dot(a,b,dims): return lax.dot_general(a,b,dims,preferred_element_type=jnp.float32)

def head_lanes(lanes):
    return lanes//HEAD_DIM

def only_head(x,number,lanes,other=0.0):
    if lanes==HEAD_DIM: return x
    lane=lax.broadcasted_iota(jnp.int32,x.shape,1)
    return jnp.where(lane//HEAD_DIM==number,x,jnp.asarray(other,x.dtype))

def fwd2_kernel(block,firsts,lasts,q_ref,k_ref,v_ref,start_ref,*rest):
    o_ref,lse_ref,vt_ref=rest[-3:]
    i=pl.program_id(1)
    length,lanes=k_ref.shape
    heads=lanes//HEAD_DIM
    @pl.when(i==0)
    def _():
        for r in range(length//block):
            rows=pl.ds(r*block,block)
            t=jnp.transpose(v_ref[rows,:])
            for n in range(heads):
                vt_ref[n,0:HEAD_DIM,rows]=t[n*HEAD_DIM:(n+1)*HEAD_DIM]
                vt_ref[n,HEAD_DIM:,rows]=jnp.ones((16,block),jnp.bfloat16)
    q=q_ref[...]*jnp.asarray(HEAD_DIM**-0.5,q_ref.dtype)
    qs=[only_head(q,n,lanes) for n in range(heads)]
    part=256 if block%256==0 else block
    def update(masked,at,size,first,carry):
        rows=pl.ds(pl.multiple_of(at,part),size)
        k=k_ref[rows,:]
        ss=[dot(k,x[first:],NT) for x in qs]
        if masked:
            shape=ss[0].shape
            key=at+lax.broadcasted_iota(jnp.int32,shape,0)
            query=i*block+first+lax.broadcasted_iota(jnp.int32,shape,1)
            allowed=(key<=query)&(key>=start_ref[:,first:])
            ss=[jnp.where(allowed,s,masked_score) for s in ss]
        ms=[jnp.maximum(carry[n][0],jnp.max(ss[n],axis=0,keepdims=True)) for n in range(heads)]
        ps=[jnp.exp(ss[n]-ms[n]).astype(jnp.bfloat16) for n in range(heads)]
        return tuple((ms[n],carry[n][1]*jnp.exp(carry[n][0]-ms[n])+dot(vt_ref[n,:,rows],ps[n],NN)) for n in range(heads))
    def step(masked,j,carry):
        return update(masked,j*block,block,0,carry)
    carry=tuple((jnp.full((1,block),masked_score,jnp.float32),jnp.zeros((HEAD_DIM+16,block),jnp.float32)) for _ in range(heads))
    a=firsts[i]//block
    b=jnp.clip((lasts[i]+block-1)//block,a,i)
    carry=lax.fori_loop(a,b,functools.partial(step,True),carry)
    carry=lax.fori_loop(b,i,functools.partial(step,False),carry)
    for at in range(0,block,part):
        late=update(True,i*block+at,part,at,tuple((m[:,at:],x[:,at:]) for m,x in carry))
        if at: late=tuple(tuple(jnp.concatenate([x[:,:at],y],axis=1) for x,y in zip(c,l)) for c,l in zip(carry,late))
        carry=late
    outs=[]
    for n in range(heads):
        m,acc=carry[n]
        l=acc[HEAD_DIM:HEAD_DIM+1]
        outs.append(acc[:HEAD_DIM]/l)
        lse_ref[0,n:n+1,:]=m+jnp.log(l)
    o=outs[0] if heads==1 else jnp.concatenate(outs,axis=0)
    o_ref[...]=jnp.transpose(o).astype(o_ref.dtype)

def attend_forward2(q,k,v,start,block,group,earlier=()):
    length,width=q.shape
    lanes=min(128,width); nq=length//block
    firsts=start[::block]; lasts=start[block-1::block]
    spec=pltpu.PrefetchScalarGridSpec(num_scalar_prefetch=2,grid=(1,nq),
        in_specs=[pl.BlockSpec((block,lanes),lambda g,i,*_:(i,group)),
                  pl.BlockSpec((length,lanes),lambda g,i,*_:(0,group)),
                  pl.BlockSpec((length,lanes),lambda g,i,*_:(0,group)),
                  pl.BlockSpec((1,block),lambda g,i,*_:(0,i))]+[pl.BlockSpec(memory_space=pl.ANY)]*len(earlier),
        out_specs=[pl.BlockSpec((block,lanes),lambda g,i,*_:(i,g)),
                   pl.BlockSpec((1,8,block),lambda g,i,*_:(g,0,i))],
        scratch_shapes=[pltpu.VMEM((lanes//HEAD_DIM,HEAD_DIM+16,length),jnp.bfloat16)])
    return pl.pallas_call(functools.partial(fwd2_kernel,block),grid_spec=spec,
        out_shape=[jax.ShapeDtypeStruct((length,lanes),jnp.bfloat16),jax.ShapeDtypeStruct((1,8,length),jnp.float32)],
        compiler_params=pltpu.CompilerParams(vmem_limit_bytes=60*1024*1024),
        cost_estimate=pl.CostEstimate(flops=29*length*length*lanes,bytes_accessed=8*length*lanes,transcendentals=0),
        name="attend_forward")(firsts,lasts,q,k,v,start[None,:],*earlier)

def backward_kernel(block,full_end,some_end,q_ref,k_ref,v_ref,d_ref,o_ref,lse_ref,start_ref,cos_ref,sin_ref,*rest):
    p_ref,first_ref,dq_ref,delta_ref=rest[-4:]
    j=pl.program_id(1)
    length,lanes=q_ref.shape
    heads=lanes//HEAD_DIM
    @pl.when(j==0)
    def _():
        dq_ref[...]=jnp.zeros_like(dq_ref)
        for i in range(length//block):
            rows=pl.ds(i*block,block)
            prod=jnp.transpose(d_ref[rows,:].astype(jnp.float32)*o_ref[rows,:].astype(jnp.float32))
            for n in range(heads):
                delta_ref[n:n+1,rows]=jnp.sum(prod[n*HEAD_DIM:(n+1)*HEAD_DIM],axis=0,keepdims=True)
    k=k_ref[...]; v=v_ref[...]
    scale=HEAD_DIM**-0.5
    kl=[only_head(k,n,lanes) for n in range(heads)]
    ks=[x*jnp.asarray(scale,k.dtype) for x in kl]
    vs=[only_head(v,n,lanes) for n in range(heads)]
    part=256 if block%256==0 else block
    def terms(masked,keys,at,size):
        rows=pl.ds(pl.multiple_of(at,part),size)
        q=q_ref[rows,:]; d=d_ref[rows,:]
        ss=[dot(x[keys],q,NT) for x in ks]
        dps=[dot(x[keys],d,NT) for x in vs]
        if masked:
            shape=ss[0].shape
            key=j*block+keys.start+lax.broadcasted_iota(jnp.int32,shape,0)
            query=at+lax.broadcasted_iota(jnp.int32,shape,1)
            allowed=(key<=query)&(key>=start_ref[0:1,rows])
            ss=[jnp.where(allowed,s,masked_score) for s in ss]
        ps=[jnp.exp(ss[n]-lse_ref[0,n:n+1,rows]) for n in range(heads)]
        dss=[(ps[n]*(dps[n]-delta_ref[n:n+1,rows])).astype(jnp.bfloat16) for n in range(heads)]
        pv=[dot(p.astype(jnp.bfloat16),d,NN) for p in ps]
        pk=[dot(x,q,NN) for x in dss]
        dq_ref[rows,:]+=sum(dot(dss[n],ks[n][keys],TN) for n in range(heads))
        if heads==2:
            lane=lax.broadcasted_iota(jnp.int32,pv[0].shape,1)<HEAD_DIM
            return jnp.where(lane,pk[0],pk[1]),jnp.where(lane,pv[0],pv[1])
        return pk[0],pv[0]
    def step(masked,i,carry):
        dk,dv=terms(masked,slice(0,block),i*block,block)
        return carry[0]+dk,carry[1]+dv
    pieces=[terms(True,slice(at,at+part),j*block+at,block-at) for at in range(0,block,part)]
    carry=tuple(jnp.concatenate(x,axis=0) if len(x)>1 else x[0] for x in zip(*pieces))
    carry=lax.fori_loop(j+1,full_end[j],functools.partial(step,False),carry)
    dk,dv=lax.fori_loop(full_end[j],some_end[j],functools.partial(step,True),carry)
    here=pl.ds(pl.multiple_of(j*block,block),block)
    cosine,sine=cos_ref[here,:],-sin_ref[here,:]
    p_ref[:,:lanes]=turned(dq_ref[here,:],cosine,sine).astype(jnp.bfloat16)
    p_ref[:,lanes:2*lanes]=turned(dk*scale,cosine,sine).astype(jnp.bfloat16)
    blend=dv.astype(jnp.bfloat16).astype(jnp.float32)
    p_ref[:,2*lanes:]=(blend_weight*blend).astype(jnp.bfloat16)
    first_ref[...]=((1.0-blend_weight)*blend).astype(jnp.bfloat16)

def attend_backward(q,k,v,d,start,cosine,sine,block,group,o,lse,before=(),earlier=()):
    length,width=q.shape
    lanes=cosine.shape[1]; n=length//block
    lasts=start[block-1::block]
    edge=jnp.arange(n,dtype=jnp.int32)
    full_end=jnp.maximum(edge+1,jnp.sum((lasts[None,:]<=edge[:,None]*block).astype(jnp.int32),axis=1))
    reach=jnp.sum((start[None,:]<=edge[:,None]*block+block-1).astype(jnp.int32),axis=1)
    some_end=jnp.maximum(full_end,(reach+block-1)//block)
    whole=pl.BlockSpec((length,lanes),lambda g,j,*_:(0,group))
    part=pl.BlockSpec((block,lanes),lambda g,j,*_:(j,group))
    table=pl.BlockSpec((length,lanes),lambda g,j,*_:(0,0))
    more=list(earlier)+list(before)
    spec=pltpu.PrefetchScalarGridSpec(num_scalar_prefetch=2,grid=(1,n),
        in_specs=[whole,part,part,whole,table,pl.BlockSpec((1,8,length),lambda g,j,*_:(0,0,0)),pl.BlockSpec((1,length),lambda g,j,*_:(0,0)),table,table]+[pl.BlockSpec(memory_space=pl.ANY)]*len(more),
        out_specs=[pl.BlockSpec((block,3*lanes),lambda g,j,*_:(j,group)),part],
        scratch_shapes=[pltpu.VMEM((length,lanes),jnp.float32),pltpu.VMEM((8,length),jnp.float32)])
    return pl.pallas_call(functools.partial(backward_kernel,block),grid_spec=spec,
        out_shape=[jax.ShapeDtypeStruct((length,3*width),jnp.bfloat16),jax.ShapeDtypeStruct((length,width),jnp.bfloat16)],
        input_output_aliases={11+len(earlier)+k:k for k in range(len(before))},
        compiler_params=pltpu.CompilerParams(vmem_limit_bytes=56*1024*1024),
        cost_estimate=pl.CostEstimate(flops=52*length*length*lanes,bytes_accessed=22*length*lanes,transcendentals=0),
        name="attend_backward")(full_end,some_end,q,k,v,d,o,lse,start[None,:],cosine,sine,*more)


f32 = jnp.float32
bf16 = jnp.bfloat16
everywhere = pl.BlockSpec(memory_space=pl.ANY)


def swap(x, axis, mask):
    return lax.ppermute(x, axis, [(i, i ^ mask) for i in range(lax.axis_size(axis))])


def cut_of(rows):
    half = rows // 2
    return half - half % 8 if half >= 8 else half


def after(x, *earlier):
    def kernel(*refs):
        pass

    return pl.pallas_call(
        kernel,
        in_specs=[everywhere] * (1 + len(earlier)),
        out_specs=everywhere,
        out_shape=jax.ShapeDtypeStruct(x.shape, x.dtype),
        input_output_aliases={0: 0},
        name="after",
    )(x, *earlier)


def spread_relay(x, axis):
    count = lax.axis_size(axis)
    if count != 4:
        return [[x]] + [[swap(x, axis, e)] for e in range(1, count)]
    cut = cut_of(x.shape[0])
    one, two = swap(x, axis, 1), swap(x, axis, 2)
    return [[x], [one], [two], [swap(two[:cut], axis, 1), swap(one[cut:], axis, 2)]]


def spread(x, axis):
    return [x] + [swap(x, axis, e) for e in range(1, lax.axis_size(axis))]


def add_low(*terms):
    return sum(t.astype(f32) for t in terms).astype(bf16)


def collect(parts, axis):
    return sum((swap(p, axis, e) if e else p).astype(f32) for e, p in enumerate(parts))


def in_order(parts, rank):
    rows = parts[0].shape[0]
    whole = jnp.zeros((len(parts) * rows,) + parts[0].shape[1:], parts[0].dtype)
    for e, part in enumerate(parts):
        whole = lax.dynamic_update_slice_in_dim(whole, part, (rank ^ e) * rows, 0)
    return whole


def block_of(x, number, rows):
    return lax.dynamic_slice_in_dim(x, number * rows, rows, 0)


def both_cores(own, other, core):
    first = core == 0
    return jnp.concatenate([jnp.where(first, own, other), jnp.where(first, other, own)])


def sum_over_all(x):
    for axis in ("mlp", "dp", "head"):
        count = lax.axis_size(axis)
        if count == 4:
            x = (x + swap(x, axis, 1)) + (swap(x, axis, 2) + swap(x, axis, 3))
            continue
        mask = 1
        while mask < count:
            x = x + swap(x, axis, mask)
            mask *= 2
    return x


def rms_scale(rows):
    return lax.rsqrt(jnp.mean(rows * rows, axis=-1, keepdims=True) + epsilon)


def norm_back(rows, scale, gain, grad):
    weighted = grad * gain
    return scale * weighted - rows * scale * scale * scale * jnp.mean(
        weighted * rows, axis=-1, keepdims=True
    )


def turned(x, cosine, sine):
    half = HEAD_DIM // 2
    if x.shape[1] == HEAD_DIM:
        other = jnp.concatenate([x[:, half:], x[:, :half]], axis=1)
    else:
        lanes = x.shape[1]
        lane = lax.broadcasted_iota(jnp.int32, x.shape, 1)
        other = jnp.where(
            lane % HEAD_DIM < half, pltpu.roll(x, lanes - half, 1), pltpu.roll(x, half, 1)
        )
    return x * cosine + other * sine


def load_rows(refs, counts, number, target):
    at = 0
    for k, pieces in enumerate(counts):
        mine = refs[at : at + pieces]
        at += pieces

        @pl.when(number == k)
        def _(mine=mine):
            row = 0
            for ref in mine:
                target[row : row + ref.shape[0], :] = ref[...]
                row += ref.shape[0]


def project_kernel(counts, rank_ref, *refs):
    total = sum(counts)
    parts, (w_ref, gain_ref, cos_ref, sin_ref, first_ref) = refs[:total], refs[total : total + 5]
    a_ref, q_ref, k_ref, v_ref, norm_ref, rows_ref = refs[-6:]
    i = pl.program_id(0)
    load_rows(parts, counts, i, rows_ref)
    x = rows_ref[...].astype(f32)
    a = (x * rms_scale(x) * gain_ref[...]).astype(bf16)
    a_ref[...] = a
    width = q_ref.shape[1]
    lanes = cos_ref.shape[1]
    cosine, sine = cos_ref[...], sin_ref[...]
    joined = dot(a, w_ref[...], NN)
    of = lax.broadcasted_iota(jnp.int32, (lanes, 128), 0) // HEAD_DIM
    one_hot = (of == lax.broadcasted_iota(jnp.int32, (lanes, 128), 1)).astype(bf16)

    def norms(value):
        wide = value * value
        high = wide.astype(bf16)
        low = (wide - high.astype(f32)).astype(bf16)
        squares = dot(high, one_hot, NN) + dot(low, one_hot, NN)
        return jnp.sum(jnp.sqrt(jnp.maximum(squares, 0.0)), axis=0, keepdims=True)

    @pl.when(i == 0)
    def _():
        norm_ref[...] = jnp.zeros_like(norm_ref)

    for g in range(width // lanes):
        at = slice(g * lanes, (g + 1) * lanes)
        query, key, value = (
            joined[:, (3 * g + k) * lanes : (3 * g + k + 1) * lanes] for k in range(3)
        )
        q_ref[:, at] = turned(query, cosine, sine).astype(bf16)
        k_ref[:, at] = turned(key, cosine, sine).astype(bf16)
        first = first_ref[:, at].astype(f32)
        blended = blend_weight * value + (1.0 - blend_weight) * first
        v_ref[:, at] = blended.astype(bf16)
        norm_ref[0:1, :] += norms(first)
        norm_ref[1:2, :] += norms(blended)


def spec_whole(x):
    return pl.BlockSpec(x.shape, lambda *_: (0,) * x.ndim)


def cost(us):
    return pl.CostEstimate(flops=int(us * 1.1e9), bytes_accessed=int(us * 1e5), transcendentals=0)


big = pltpu.CompilerParams(vmem_limit_bytes=56 * 1024 * 1024)


def project(rank, parts, base, weights, gain, cosine, sine, firsts, before=()):
    counts = tuple(len(p) for p in parts)
    flat = [x for p in parts for x in p]
    chunk = sum(x.shape[0] for x in parts[0])
    length, width = firsts.shape
    model, lanes = flat[0].shape[1], cosine.shape[1]
    there = lambda i, r: (r[0] ^ (base + i), 0)
    block = lambda n: pl.BlockSpec((chunk, n), there)
    spec = pltpu.PrefetchScalarGridSpec(
        num_scalar_prefetch=1,
        grid=(len(parts),),
        in_specs=[spec_whole(x) for x in flat]
        + [spec_whole(weights), spec_whole(gain), block(lanes), block(lanes), block(width)]
        + [everywhere] * len(before),
        out_specs=[block(model), block(width), block(width), block(width)]
        + [pl.BlockSpec((8, 128), lambda i, r: (0, 0))],
        scratch_shapes=[pltpu.VMEM((chunk, model), bf16)],
    )
    low = jax.ShapeDtypeStruct((length, width), bf16)
    return pl.pallas_call(
        functools.partial(project_kernel, counts),
        grid_spec=spec,
        out_shape=[jax.ShapeDtypeStruct((length, model), bf16), low, low, low]
        + [jax.ShapeDtypeStruct((8, 128), f32)],
        input_output_aliases={len(flat) + 6 + k: k for k in range(len(before))},
        compiler_params=big,
        cost_estimate=cost(4.5 * len(parts)),
        name="project",
    )(rank[None], *flat, weights, gain, cosine, sine, firsts, *before)


def assemble_kernel(ranks, rank_ref, *refs):
    far_ref, out_ref = refs[-2:]
    rows = far_ref.shape[2]
    e = pl.program_id(0)
    for k in range(ranks):

        @pl.when(e == k)
        def _(ref=refs[k]):
            for a in range(3):
                far_ref[a, 0] = ref[a * rows : (a + 1) * rows, :]
            out_ref[0] = ref[3 * rows :, :]


def assemble(rank, bundles, rows, earlier):
    ranks = len(bundles)
    wide, model = bundles[0].shape
    spec = pltpu.PrefetchScalarGridSpec(
        num_scalar_prefetch=1,
        grid=(ranks,),
        in_specs=[spec_whole(b) for b in bundles] + [everywhere] * len(earlier),
        out_specs=[
            pl.BlockSpec((3, 1, rows, model), lambda e, r: (0, e, 0, 0)),
            pl.BlockSpec((1, wide - 3 * rows, model), lambda e, r: (r[0] ^ e, 0, 0)),
        ],
    )
    return pl.pallas_call(
        functools.partial(assemble_kernel, ranks),
        grid_spec=spec,
        out_shape=[
            jax.ShapeDtypeStruct((3, ranks, rows, model), bf16),
            jax.ShapeDtypeStruct((ranks, wide - 3 * rows, model), bf16),
        ],
        compiler_params=big,
        cost_estimate=cost(3),
        name="assemble",
    )(rank[None], *bundles, *earlier)


def feed_kernel(x_ref, g_ref, *refs):
    sources, (act_ref, in_ref, sum_ref) = (refs[0:3], refs[3:6], refs[6:9]), refs[-3:]
    f = pl.program_id(0)
    steps = pl.num_programs(0)

    @pl.when(f == 0)
    def _():
        sum_ref[...] = jnp.zeros_like(sum_ref)

    def work(gate_w, up_w, down_w):
        x, g = x_ref[...], g_ref[...]
        gate, up = dot(gate_w[...], x, NT), dot(up_w[...], x, NT)
        hidden_grad = dot(down_w[...], g, NT)
        sigma = 1.0 / (1.0 + jnp.exp(-gate))
        gate_sigma = gate * sigma
        hidden = (gate_sigma * up).astype(bf16)
        gate_grad = (hidden_grad * up * (sigma + gate_sigma * (1.0 - sigma))).astype(bf16)
        up_grad = (hidden_grad * gate_sigma).astype(bf16)
        act_ref[0, 0], act_ref[0, 1], act_ref[0, 2] = gate_grad, up_grad, hidden
        sum_ref[...] += dot(gate_grad, gate_w[...], TN) + dot(up_grad, up_w[...], TN)

    for k, condition in enumerate((f < 2, f == 2, f == 3)):

        @pl.when(condition)
        def _(k=k):
            work(*sources[k])

    @pl.when(f == steps - 1)
    def _():
        in_ref[...] = sum_ref[...].astype(in_ref.dtype)


def feed(x, grad, own, far, far_other, dtype, earlier=()):
    tokens, model = x.shape
    part = own.shape[0] // 6
    block = lambda at: pl.BlockSpec((part, model), at)
    return pl.pallas_call(
        feed_kernel,
        grid=(4,),
        in_specs=[spec_whole(x), spec_whole(grad)]
        + [block(lambda f, a=a: (2 * a + jnp.minimum(f, 1), 0)) for a in range(3)]
        + [block(lambda f, a=a: (a, 0)) for a in range(3)] * 2
        + [everywhere] * len(earlier),
        out_specs=[
            pl.BlockSpec((1, 3, part, tokens), lambda f: (f, 0, 0, 0)),
            pl.BlockSpec((tokens, model), lambda f: (0, 0)),
        ],
        out_shape=[
            jax.ShapeDtypeStruct((4, 3, part, tokens), bf16),
            jax.ShapeDtypeStruct((tokens, model), dtype),
        ],
        scratch_shapes=[pltpu.VMEM((tokens, model), f32)],
        compiler_params=big,
        cost_estimate=cost(16),
        name="feed",
    )(x, grad, *([own] * 3), *([far] * 3), *([far_other] * 3), *earlier)


def half_grads(act_ref, near_ref, x_ref, xn_ref, g_ref, gn_ref, result_ref):
    a = pl.program_id(0)

    @pl.when(a < 2)
    def _():
        result_ref[...] = dot(act_ref[0, 0], x_ref[...], NN) + dot(near_ref[0, 0], xn_ref[...], NN)

    @pl.when(a == 2)
    def _():
        result_ref[...] = dot(act_ref[0, 0], g_ref[...], NN) + dot(near_ref[0, 0], gn_ref[...], NN)


def other_grads_kernel(scalars, *refs):
    out_ref, result_ref = refs[-2:]
    half_grads(*refs[:6], result_ref)
    out_ref[...] = result_ref[...].astype(bf16)


def far_grads_kernel(ranks, scalars, *refs):
    got_ref, out_refs, result_ref = refs[6], refs[7 : 7 + ranks], refs[-1]
    half_grads(*refs[:6], result_ref)
    rows = result_ref.shape[0] // ranks
    for e in range(ranks):
        at = slice(e * rows, (e + 1) * rows)
        out_refs[e][0] = (result_ref[at, :] + got_ref[at, :].astype(f32)).astype(bf16)


def own_grads_kernel(ranks, scalars, *refs):
    got_ref, out_ref, out_got_ref = refs[6:9]
    own_refs, result_ref = refs[9 : 9 + ranks], refs[-1]
    half_grads(*refs[:6], result_ref)
    i = pl.program_id(0)
    rows = result_ref.shape[0] // ranks
    result_ref[...] += got_ref[...].astype(f32)

    @pl.when(i == 0)
    def _():
        for e in range(ranks):
            number = scalars[1] ^ e
            both = out_ref[number].astype(f32) + out_got_ref[number].astype(f32)
            own_refs[e][3 * rows :, :] = both.astype(bf16)

    for a in range(3):

        @pl.when(i == a)
        def _(a=a):
            to = slice(a * rows, (a + 1) * rows)
            for e in range(ranks):
                if rows % 8 == 0:
                    at = pl.ds(pl.multiple_of((scalars[1] ^ e) * rows, 8), rows)
                    own_refs[e][to, :] = result_ref[at, :].astype(bf16)
                else:
                    for h in range(ranks):

                        @pl.when(scalars[1] ^ e == h)
                        def _(e=e, h=h):
                            own_refs[e][to, :] = result_ref[h * rows : (h + 1) * rows, :].astype(bf16)


def shard_grads(scalars, ranks, far, here, near, x, x_near, grad, grad_near, got=None):
    _, _, part, tokens = here.shape
    model = x.shape[1]
    if got is None:
        number = lambda c: 3 if far else 1 - c[0]
    else:
        number = lambda c: 2 if far else c[0]
    act = pl.BlockSpec((1, 1, part, tokens), lambda i, c: (number(c), i, 0, 0))
    in_specs = [act, act] + [spec_whole(x)] * 4
    args = [here, near, x, x_near, grad, grad_near]
    row_block = pl.BlockSpec((part, model), lambda i, c: (i, 0))
    rows = part // ranks
    if got is None:
        kernel, out_specs = other_grads_kernel, row_block
        out_shape = jax.ShapeDtypeStruct((3 * part, model), bf16)
    elif far:
        kernel = functools.partial(far_grads_kernel, ranks)
        in_specs.append(row_block)
        args += got
        out_specs = [pl.BlockSpec((1, rows, model), lambda i, c: (i, 0, 0))] * ranks
        out_shape = [jax.ShapeDtypeStruct((3, rows, model), bf16)] * ranks
    else:
        kernel = functools.partial(own_grads_kernel, ranks)
        in_specs += [row_block] + [spec_whole(g) for g in got[1:]]
        args += got
        wide = 3 * rows + got[1].shape[1]
        out_specs = [pl.BlockSpec((wide, model), lambda i, c: (0, 0))] * ranks
        out_shape = [jax.ShapeDtypeStruct((wide, model), bf16)] * ranks
    spec = pltpu.PrefetchScalarGridSpec(
        num_scalar_prefetch=1,
        grid=(3,),
        in_specs=in_specs,
        out_specs=out_specs,
        scratch_shapes=[pltpu.VMEM((part, model), f32)],
    )
    return pl.pallas_call(
        kernel,
        grid_spec=spec,
        out_shape=out_shape,
        compiler_params=big,
        cost_estimate=cost(8),
        name=("far" if far else "own") + ("_other" if got is None else "_sum"),
    )(scalars, *args)


def others_kernel(scalars, act_ref, near_ref, x_ref, xn_ref, g_ref, gn_ref, *refs):
    own_ref, far_ref, far_other_ref, far_out, own_out, out_ref, out_near_ref, sum_ref = refs
    i = pl.program_id(0)
    for a in range(6):

        @pl.when(i == a)
        def _(a=a):
            first, second = (x_ref, xn_ref) if a % 3 < 2 else (g_ref, gn_ref)
            target = far_out if a < 3 else own_out
            target[...] = (
                dot(act_ref[0, 0], first[...], NN) + dot(near_ref[0, 0], second[...], NN)
            ).astype(bf16)

    @pl.when(i == 5)
    def _():
        sum_ref[...] = jnp.zeros_like(sum_ref)

    for condition, ref in (((i == 6) | (i == 7), own_ref), (i == 8, far_ref), (i == 9, far_other_ref)):

        @pl.when(condition)
        def _(ref=ref):
            sum_ref[0] += dot(act_ref[0, 0], ref[...], TN)
            sum_ref[1] += dot(near_ref[0, 0], ref[...], TN)

    @pl.when(i == 9)
    def _():
        out_ref[...] = sum_ref[0]
        out_near_ref[...] = sum_ref[1].astype(bf16)


def others(scalars, here, near, x, x_near, grad, grad_near, own, far, far_other):
    _, _, part, tokens = here.shape
    model = x.shape[1]

    def act_at(i, c):
        number = jnp.where(i < 3, 3, jnp.where(i < 6, 1 - c[0], i - 6))
        return (number, jnp.where(i < 6, i % 3, 2), 0, 0)

    act = pl.BlockSpec((1, 1, part, tokens), act_at)
    row = lambda at: pl.BlockSpec((part, model), at)
    spec = pltpu.PrefetchScalarGridSpec(
        num_scalar_prefetch=1,
        grid=(10,),
        in_specs=[act, act]
        + [spec_whole(x)] * 4
        + [row(lambda i, c: (4 + jnp.clip(i - 6, 0, 1), 0))]
        + [row(lambda i, c: (2, 0))] * 2,
        out_specs=[
            row(lambda i, c: (jnp.minimum(i, 2), 0)),
            row(lambda i, c: (jnp.clip(i - 3, 0, 2), 0)),
            spec_whole(x),
            spec_whole(x),
        ],
        scratch_shapes=[pltpu.VMEM((2, tokens, model), f32)],
    )
    half = jax.ShapeDtypeStruct((3 * part, model), bf16)
    return pl.pallas_call(
        others_kernel,
        grid_spec=spec,
        out_shape=[half, half]
        + [jax.ShapeDtypeStruct((tokens, model), f32), jax.ShapeDtypeStruct((tokens, model), bf16)],
        compiler_params=big,
        cost_estimate=cost(19),
        name="others",
    )(scalars, here, near, x, x_near, grad, grad_near, own, far, far_other)


def regroup_kernel(ranks, rank_ref, *refs):
    out_ref = refs[-1]
    rows = out_ref.shape[2]
    e = pl.program_id(0)
    for k in range(ranks):

        @pl.when(e == k)
        def _(k=k):
            low, high = refs[2 * k], refs[2 * k + 1]
            cut = low.shape[0]
            for a in range(3):
                first, last = a * rows, (a + 1) * rows
                if last <= cut:
                    out_ref[a, 0] = low[first:last, :]
                elif first >= cut:
                    out_ref[a, 0] = high[first - cut : last - cut, :]
                else:
                    out_ref[a, 0, : cut - first] = low[first:, :]
                    out_ref[a, 0, cut - first :] = high[: last - cut, :]


def regroup(rank, pieces, rows, earlier=()):
    ranks = len(pieces)
    flat, specs = [], []
    for low, high in pieces:
        for x, at, size in (low, high):
            flat.append(x)
            specs.append(pl.BlockSpec((size, x.shape[1]), lambda e, r, at=at: (at, 0)))
    model = flat[0].shape[1]
    spec = pltpu.PrefetchScalarGridSpec(
        num_scalar_prefetch=1,
        grid=(ranks,),
        in_specs=specs + [everywhere] * len(earlier),
        out_specs=pl.BlockSpec((3, 1, rows, model), lambda e, r: (0, r[0] ^ e, 0, 0)),
    )
    return pl.pallas_call(
        functools.partial(regroup_kernel, ranks),
        grid_spec=spec,
        out_shape=jax.ShapeDtypeStruct((3, ranks, rows, model), bf16),
        compiler_params=big,
        cost_estimate=cost(2),
        name="regroup",
    )(rank[None], *flat, *earlier)


def unproject_kernel(counts, cuts, rank_ref, *refs):
    total = sum(counts)
    parts, w_ref, p_ref = refs[:total], refs[total], refs[total + 1]
    pieces = sum(len(c) for c in cuts)
    outs, gain_ref, rows_ref = refs[-2 - pieces : -2], refs[-2], refs[-1]
    i = pl.program_id(0)
    load_rows(parts, counts, i, rows_ref)
    x = rows_ref[...].astype(f32)
    grad = dot(p_ref[...], w_ref[...], NT)
    at = 0
    for k, sizes in enumerate(cuts):
        mine = outs[at : at + len(sizes)]
        at += len(sizes)

        @pl.when(i == k)
        def _(mine=mine):
            row = 0
            for ref in mine:
                ref[...] = grad[row : row + ref.shape[0]].astype(bf16)
                row += ref.shape[0]

    @pl.when(i == 0)
    def _():
        gain_ref[...] = jnp.zeros_like(gain_ref)

    gain_ref[...] += jnp.sum(grad * (x * rms_scale(x)), axis=0, keepdims=True)


def unproject(rank, parts, base, cuts, weights, grads, earlier=()):
    counts = tuple(len(p) for p in parts)
    flat = [x for p in parts for x in p]
    chunk, model = sum(x.shape[0] for x in parts[0]), flat[0].shape[1]
    block = lambda n: pl.BlockSpec((chunk, n), lambda i, r: (r[0] ^ (base + i), 0))
    sizes = [n for c in cuts for n in c]
    spec = pltpu.PrefetchScalarGridSpec(
        num_scalar_prefetch=1,
        grid=(len(parts),),
        in_specs=[spec_whole(x) for x in flat]
        + [spec_whole(weights)]
        + [block(grads.shape[1])]
        + [everywhere] * len(earlier),
        out_specs=[pl.BlockSpec((n, model), lambda i, r: (0, 0)) for n in sizes]
        + [pl.BlockSpec((1, model), lambda i, r: (0, 0))],
        scratch_shapes=[pltpu.VMEM((chunk, model), bf16)],
    )
    out = pl.pallas_call(
        functools.partial(unproject_kernel, counts, cuts),
        grid_spec=spec,
        out_shape=[jax.ShapeDtypeStruct((n, model), bf16) for n in sizes]
        + [jax.ShapeDtypeStruct((1, model), f32)],
        compiler_params=big,
        cost_estimate=cost(3.5 * len(parts)),
        name="unproject",
    )(rank[None], *flat, weights, grads, *earlier)
    return out[:-1], out[-1]


def state_kernel(back_ref, terms_ref, hidden_ref, grad_ref, gain_ref, w_ref, state_ref, low_ref, mixed_ref, sum_ref):
    hidden, gain = hidden_ref[...], gain_ref[...]
    grad = back_ref[...].astype(f32) + terms_ref[...]
    scale = rms_scale(hidden)
    state = grad_ref[...].astype(f32) + norm_back(hidden, scale, gain, grad)
    low = state.astype(bf16)
    state_ref[...] = state
    low_ref[...] = low
    for h in range(mixed_ref.shape[0]):
        mixed_ref[h] = dot(low, w_ref[h], NT).astype(bf16)

    @pl.when(pl.program_id(0) == 0)
    def _():
        sum_ref[...] = jnp.zeros_like(sum_ref)

    sum_ref[...] += jnp.sum(grad * hidden * scale, axis=0, keepdims=True)


def state_back(back, terms, hidden, grad, gain, weights):
    tokens, model = back.shape
    ranks, width, _ = weights.shape
    size = 128 if tokens % 128 == 0 else tokens
    row = pl.BlockSpec((size, model), lambda i: (i, 0))
    return pl.pallas_call(
        state_kernel,
        grid=(tokens // size,),
        in_specs=[row, row, row, row, spec_whole(gain), spec_whole(weights)],
        out_specs=[
            row,
            row,
            pl.BlockSpec((ranks, size, width), lambda i: (0, i, 0)),
            pl.BlockSpec((1, model), lambda i: (0, 0)),
        ],
        out_shape=[
            jax.ShapeDtypeStruct((tokens, model), f32),
            jax.ShapeDtypeStruct((tokens, model), bf16),
            jax.ShapeDtypeStruct((ranks, tokens, width), bf16),
            jax.ShapeDtypeStruct((1, model), f32),
        ],
        compiler_params=big,
        cost_estimate=cost(6),
        name="state_back",
    )(back, terms, hidden, grad, gain, weights)


def on_device(
    tokens,
    first_values,
    segment_ids,
    positions,
    attn_gain,
    w_query,
    w_key,
    w_value,
    w_out,
    mlp_gain,
    w_gate,
    w_up,
    w_down,
    out_grad,
):
    core, rank = lax.axis_index("dp"), lax.axis_index("head")
    ranks = lax.axis_size("head")
    chunk, width = tokens.shape[0], w_query.shape[1]
    model = tokens.shape[2]
    length, ff = segment_ids.shape[0], w_gate.shape[1]
    block = min(512, length)
    tokens, firsts, out_grad = tokens[:, 0], first_values[:, 0], out_grad[:, 0]
    places = positions[:, 0]
    start = jnp.arange(length, dtype=jnp.int32) - places

    row_parts = spread_relay(tokens, "head")

    part = ff // 2
    rows = part // ranks
    stack = jnp.concatenate([w_gate.T, w_up.T, w_down])
    cut_stack = stack.reshape(3, 2 * ranks, rows, model)
    far_piece = swap(
        lax.dynamic_index_in_dim(cut_stack, core * ranks + rank, 1, False), "mlp", 2
    ).reshape(3 * rows, model)
    out_grad_near = swap(out_grad, "mlp", 1)
    half_out = width // 2
    far_piece = after(far_piece, *row_parts[-1])
    bundle = jnp.concatenate([far_piece, block_of(w_out, core, half_out)])
    bundles = spread(bundle, "head")

    lanes = min(128, width)
    w_project = jnp.concatenate(
        [
            w[:, g * lanes : (g + 1) * lanes]
            for g in range(width // lanes)
            for w in (w_query, w_key, w_value)
        ],
        axis=1,
    )
    lane = jnp.arange(lanes)
    freq = theta_base ** (-(lane % (HEAD_DIM // 2)).astype(f32) * 2.0 / HEAD_DIM)
    angles = places.astype(f32)[:, None] * freq
    cosine = jnp.cos(angles)
    sine = jnp.sin(angles) * jnp.where(lane % HEAD_DIM < HEAD_DIM // 2, -1.0, 1.0)
    heads_args = (w_project, attn_gain[None], cosine, sine, firsts)
    soon = 3 if ranks == 4 else ranks
    *projected, norms = project(rank, row_parts[:soon], 0, *heads_args)
    if soon < ranks:
        *projected, more = project(rank, row_parts[soon:], soon, *heads_args, projected)
        norms = norms + more
    gathered, queries, keys, values = projected
    groups = width // lanes
    mixed, log_total, mixed_here = [], [], []
    for g in range(groups):
        one_mixed, one_total = attend_forward2(
            queries, keys, values, start, min(1024, length), g, tuple(mixed[-1:])
        )
        mixed.append(one_mixed)
        log_total.append(one_total)
        mixed_here.append(
            lax.all_to_all(one_mixed, "head", 0, 0, tiled=True).reshape(ranks, chunk, lanes)
        )

    far_half, out_half = assemble(rank, bundles, rows, (mixed_here[0], mixed[-1]))
    far_half = far_half.reshape(3 * part, model)
    far_other, out_other = swap(far_half, "dp", 1), swap(out_half, "dp", 1)
    first = core == 0
    out_all = jnp.concatenate(
        [jnp.where(first, out_half, out_other), jnp.where(first, out_other, out_half)], axis=1
    )

    residual = tokens.astype(f32)
    hidden_state = residual + sum(
        jnp.einsum("htk,hkd->td", m, out_all[:, g * lanes : (g + 1) * lanes], preferred_element_type=f32)
        for g, m in enumerate(mixed_here)
    )
    mlp_scale = rms_scale(hidden_state)
    mlp_input = (hidden_state * mlp_scale * mlp_gain).astype(bf16)
    mlp_input_near = swap(mlp_input, "mlp", 1)

    acts, terms = feed(mlp_input, out_grad, stack, far_half, far_other, f32)
    acts_near, terms_near = feed(
        mlp_input_near, out_grad_near, stack, far_half, far_other, bf16, (terms,)
    )
    terms_back = swap(terms_near, "mlp", 1)
    scalars = jnp.stack([core, rank]).astype(jnp.int32)
    tokens_two = (acts, acts_near, mlp_input, mlp_input_near, out_grad, out_grad_near)
    far_other_grads, own_other_grads, down_here, down_near = others(
        scalars, *tokens_two, stack, far_half, far_other
    )
    terms_back = after(terms_back, down_near)
    far_half_got = swap(after(far_other_grads, terms_back), "dp", 1)
    own_half_got = swap(after(own_other_grads, far_half_got), "dp", 1)
    state_grad, state_grad_low, mixed_grad, mlp_gain_grad = state_back(
        terms_back, terms, hidden_state, out_grad, mlp_gain[None], out_all
    )
    mlp_gain_grad = mlp_gain_grad[0]
    mixed_grad_rows = lax.all_to_all(mixed_grad, "head", 0, 0, tiled=True).reshape(length, width)

    low_grad = after(state_grad_low, mixed_grad)
    out_grads = [
        jnp.einsum("htk,td->hkd", m, low_grad, preferred_element_type=f32).astype(bf16)
        for m in mixed_here
    ]
    out_grads = jnp.concatenate(out_grads, axis=1).reshape(ranks, 2, half_out, model)
    out_got = swap(lax.dynamic_index_in_dim(out_grads, 1 - core, 1, False), "dp", 1)
    out_own = lax.dynamic_index_in_dim(out_grads, core, 1, False)
    far_half_got = after(far_half_got, mixed_grad)
    far_chip = shard_grads(scalars, ranks, True, *tokens_two, [far_half_got])
    far_got = [swap(f, "head", e) for e, f in enumerate(far_chip) if e]
    mixed_grad_rows = after(mixed_grad_rows, far_chip[0])

    back_args = (queries, keys, values, mixed_grad_rows, start, cosine, sine, block)
    grads = attend_backward(*back_args, 0, mixed[0], log_total[0])
    own_half_got = after(own_half_got, grads[0])
    own_chip = shard_grads(scalars, ranks, False, *tokens_two, [own_half_got, out_own, out_got])
    far_got = [after(f, own_chip[0]) for f in far_got]
    far_sum = add_low(far_chip[0], *far_got)
    far_here = swap(far_sum, "mlp", 2)
    own_chip = [own_chip[0]] + [after(f, far_sum) for f in own_chip[1:]]
    own_got = [swap(f, "head", e) for e, f in enumerate(own_chip) if e]
    down_back = swap(after(down_near, own_chip[0]), "mlp", 1)
    for g in range(1, width // lanes):
        grads = attend_backward(
            *back_args, g, mixed[g], log_total[g], grads, (far_sum, *own_chip[1:])
        )
    proj_grad, first_values_grad = grads
    cut = cut_of(chunk)
    half_proj = model // 2
    proj_wgrad = dot(gathered, proj_grad, TN).astype(bf16)
    if ranks == 4:
        (low, high), gain_last = unproject(
            rank, row_parts[3:], 3, ((cut, chunk - cut),), w_project, proj_grad, (proj_wgrad, down_back)
        )
        for_two, for_one = swap(low, "head", 1), swap(high, "head", 2)
        own_got = [after(f, low) for f in own_got]
    else:
        own_got = [after(f, proj_grad) for f in own_got]
    own_all = (own_chip[0], *own_got)
    piece_sum = add_low(*(f[: 3 * rows] for f in own_all), far_here.reshape(3 * rows, model))
    out_sum = add_low(*(f[3 * rows :] for f in own_all))
    proj_got = swap(after(block_of(proj_wgrad, 1 - core, half_proj), own_got[-1]), "dp", 1)
    proj_mine = add_low(block_of(proj_wgrad, core, half_proj), proj_got)
    both_mine = jnp.concatenate([proj_mine, out_sum.reshape(half_proj, -1)], axis=1)
    line, count = lax.axis_index("mlp"), lax.axis_size("mlp")

    def line_sum(x):
        size = x.shape[0] // count
        return collect([block_of(x, line ^ e, size) for e in range(count)], "mlp").astype(bf16)

    if ranks == 4:
        cut_p = cut_of(3 * rows)
        cut_q = 3 * rows - cut_p
        (own, one, two), gain_rest = unproject(
            rank,
            row_parts[:3],
            0,
            ((chunk,),) * 3,
            w_project,
            proj_grad,
            (both_mine,),
        )
        attn_gain_grad = gain_last + gain_rest
        piece_sum = after(piece_sum, own)
        low_p, high_p = piece_sum[:cut_p], piece_sum[cut_p:]
        low_x, high_y = swap(low_p, "head", 1), swap(high_p, "head", 2)
        low_yy = swap(jnp.concatenate([low_p, low_x]), "head", 2)
        high_xx = swap(jnp.concatenate([high_p, high_y]), "head", 1)
        one = one.at[cut:].set(add_low(one[cut:], for_one))
        two = two.at[:cut].set(add_low(two[:cut], for_two))
        one_got, two_got = swap(one, "head", 1), swap(two, "head", 2)
        half_sum = regroup(
            rank,
            [
                ((low_p, 0, cut_p), (high_p, 0, cut_q)),
                ((low_x, 0, cut_p), (high_xx, 0, cut_q)),
                ((low_yy, 0, cut_p), (high_y, 0, cut_q)),
                ((low_yy, 1, cut_p), (high_xx, 1, cut_q)),
            ],
            rows,
        )
        line_piece = after(line_sum(both_mine), one, two)
        attn_normed_grad = own.astype(f32) + one_got.astype(f32) + two_got.astype(f32)
        ended = (one_got, two_got)
    else:
        parts, attn_gain_grad = unproject(
            rank, row_parts, 0, ((chunk,),) * ranks, w_project, proj_grad
        )
        half_sum = jnp.zeros((3, ranks, rows, model), bf16)
        for e, piece in enumerate(spread(piece_sum, "head")):
            piece = piece.reshape(3, 1, rows, model)
            half_sum = lax.dynamic_update_slice_in_dim(half_sum, piece, rank ^ e, 1)
        attn_normed_grad = collect(parts, "head")
        ended = (attn_normed_grad,)
        line_piece = line_sum(both_mine)
    half_sum = half_sum.reshape(3, part, model)

    norm_row = jnp.zeros((model,), f32).at[:2].set(jnp.sum(norms[:2], axis=1))
    if count == 4:
        line_one = swap(line_piece, "mlp", 1)
        line_two = swap(jnp.concatenate([line_piece, line_one]), "mlp", 2)
        size = line_piece.shape[0]
        line_got = [line_piece, line_one, line_two[:size], line_two[size:]]
    else:
        line_got = spread(line_piece, "mlp")
    small = jnp.stack([attn_gain_grad[0], mlp_gain_grad, norm_row])
    small = sum_over_all(after(small, line_got[1]))
    output = (hidden_state + after(down_back, line_piece).astype(f32) + down_here).astype(bf16)

    half_sum = after(half_sum, line_piece)
    other_sum = swap(half_sum, "dp", 1)
    ff_grads = jnp.concatenate(
        [jnp.where(first, half_sum, other_sum), jnp.where(first, other_sum, half_sum)], axis=1
    ).astype(f32)
    gate_wgrad, up_wgrad, down_wgrad = ff_grads[0].T, ff_grads[1].T, ff_grads[2]
    input_grad = (
        state_grad + norm_back(residual, rms_scale(residual), attn_gain, attn_normed_grad)
    ).astype(bf16)

    line_got = [after(line_got[0], output, input_grad, down_wgrad, small)] + line_got[1:]
    both_half = in_order(line_got, line)
    both_other = swap(both_half, "dp", 1)
    proj_sum = both_cores(both_half[:, : 3 * width], both_other[:, : 3 * width], core).astype(f32)
    query_wgrad, key_wgrad, value_wgrad = (
        jnp.concatenate(
            [proj_sum[:, (3 * g + k) * lanes : (3 * g + k + 1) * lanes] for g in range(width // lanes)],
            axis=1,
        )
        for k in range(3)
    )
    out_wgrad = both_cores(
        both_half[:, 3 * width :].reshape(half_out, model),
        both_other[:, 3 * width :].reshape(half_out, model),
        core,
    ).astype(f32)

    devices = lax.axis_size("dp") * ranks * count
    value_norms = small[2, :2] / (length * (width // HEAD_DIM) * devices)
    return (
        output[:, None],
        input_grad[:, None],
        first_values_grad[:, None],
        small[0],
        query_wgrad,
        key_wgrad,
        value_wgrad,
        out_wgrad,
        small[1],
        gate_wgrad,
        up_wgrad,
        down_wgrad,
        value_norms,
    )


def solution(mesh):
    placed = (
        P("head", ("dp", "mlp"), None),
        P(None, ("dp", "mlp"), "head"),
        P(None, ("dp", "mlp")),
        P(None, ("dp", "mlp")),
        P(),
        P(None, "head"),
        P(None, "head"),
        P(None, "head"),
        P("head", None),
        P(),
        P(None, "mlp"),
        P(None, "mlp"),
        P("mlp", None),
        P("head", ("dp", "mlp"), None),
    )
    return jax.shard_map(
        on_device,
        mesh=mesh,
        in_specs=placed,
        out_specs=(
            P("head", ("dp", "mlp"), None),
            P("head", ("dp", "mlp"), None),
            P(None, ("dp", "mlp"), "head"),
            P(),
            P(None, "head"),
            P(None, "head"),
            P(None, "head"),
            P("head", None),
            P(),
            P(None, "mlp"),
            P(None, "mlp"),
            P("mlp", None),
            P(),
        ),
        check_vma=False,
    )
```

```python
import functools

import jax
import jax.numpy as jnp
from jax import lax
from jax.experimental import pallas as pl
from jax.experimental.pallas import tpu as pltpu
from jax.sharding import PartitionSpec as P

HEAD_DIM = 64
epsilon = 1e-06
theta_base = 10000.0
blend_weight = 0.5
masked_score = -1e30
NT=(((1,),(1,)),((),()))
NN=(((1,),(0,)),((),()))
TN=(((0,),(0,)),((),()))
def dot(a,b,dims): return lax.dot_general(a,b,dims,preferred_element_type=jnp.float32)

def head_lanes(lanes):
    return lanes//HEAD_DIM

def only_head(x,number,lanes,other=0.0):
    if lanes==HEAD_DIM: return x
    lane=lax.broadcasted_iota(jnp.int32,x.shape,1)
    return jnp.where(lane//HEAD_DIM==number,x,jnp.asarray(other,x.dtype))

def fwd2_kernel(block,firsts,lasts,q_ref,k_ref,v_ref,start_ref,*rest):
    o_ref,lse_ref,vt_ref=rest[-3:]
    i=pl.program_id(1)
    length,lanes=k_ref.shape
    heads=lanes//HEAD_DIM
    @pl.when(i==0)
    def _():
        for r in range(length//block):
            rows=pl.ds(r*block,block)
            t=jnp.transpose(v_ref[rows,:])
            for n in range(heads):
                vt_ref[n,0:HEAD_DIM,rows]=t[n*HEAD_DIM:(n+1)*HEAD_DIM]
                vt_ref[n,HEAD_DIM:,rows]=jnp.ones((16,block),jnp.bfloat16)
    q=q_ref[...]*jnp.asarray(HEAD_DIM**-0.5,q_ref.dtype)
    qs=[only_head(q,n,lanes) for n in range(heads)]
    part=256 if block%256==0 else block
    def update(masked,at,size,first,carry):
        rows=pl.ds(pl.multiple_of(at,part),size)
        k=k_ref[rows,:]
        ss=[dot(k,x[first:],NT) for x in qs]
        if masked:
            shape=ss[0].shape
            key=at+lax.broadcasted_iota(jnp.int32,shape,0)
            query=i*block+first+lax.broadcasted_iota(jnp.int32,shape,1)
            allowed=(key<=query)&(key>=start_ref[:,first:])
            ss=[jnp.where(allowed,s,masked_score) for s in ss]
        ms=[jnp.maximum(carry[n][0],jnp.max(ss[n],axis=0,keepdims=True)) for n in range(heads)]
        ps=[jnp.exp(ss[n]-ms[n]).astype(jnp.bfloat16) for n in range(heads)]
        return tuple((ms[n],carry[n][1]*jnp.exp(carry[n][0]-ms[n])+dot(vt_ref[n,:,rows],ps[n],NN)) for n in range(heads))
    def step(masked,j,carry):
        return update(masked,j*block,block,0,carry)
    carry=tuple((jnp.full((1,block),masked_score,jnp.float32),jnp.zeros((HEAD_DIM+16,block),jnp.float32)) for _ in range(heads))
    a=firsts[i]//block
    b=jnp.clip((lasts[i]+block-1)//block,a,i)
    carry=lax.fori_loop(a,b,functools.partial(step,True),carry)
    carry=lax.fori_loop(b,i,functools.partial(step,False),carry)
    for at in range(0,block,part):
        late=update(True,i*block+at,part,at,tuple((m[:,at:],x[:,at:]) for m,x in carry))
        if at: late=tuple(tuple(jnp.concatenate([x[:,:at],y],axis=1) for x,y in zip(c,l)) for c,l in zip(carry,late))
        carry=late
    outs=[]
    for n in range(heads):
        m,acc=carry[n]
        l=acc[HEAD_DIM:HEAD_DIM+1]
        outs.append(acc[:HEAD_DIM]/l)
        lse_ref[0,n:n+1,:]=m+jnp.log(l)
    o=outs[0] if heads==1 else jnp.concatenate(outs,axis=0)
    o_ref[...]=jnp.transpose(o).astype(o_ref.dtype)

def attend_forward2(q,k,v,start,block,group,earlier=()):
    length,width=q.shape
    lanes=min(128,width); nq=length//block
    firsts=start[::block]; lasts=start[block-1::block]
    spec=pltpu.PrefetchScalarGridSpec(num_scalar_prefetch=2,grid=(1,nq),
        in_specs=[pl.BlockSpec((block,lanes),lambda g,i,*_:(i,group)),
                  pl.BlockSpec((length,lanes),lambda g,i,*_:(0,group)),
                  pl.BlockSpec((length,lanes),lambda g,i,*_:(0,group)),
                  pl.BlockSpec((1,block),lambda g,i,*_:(0,i))]+[pl.BlockSpec(memory_space=pl.ANY)]*len(earlier),
        out_specs=[pl.BlockSpec((block,lanes),lambda g,i,*_:(i,g)),
                   pl.BlockSpec((1,8,block),lambda g,i,*_:(g,0,i))],
        scratch_shapes=[pltpu.VMEM((lanes//HEAD_DIM,HEAD_DIM+16,length),jnp.bfloat16)])
    return pl.pallas_call(functools.partial(fwd2_kernel,block),grid_spec=spec,
        out_shape=[jax.ShapeDtypeStruct((length,lanes),jnp.bfloat16),jax.ShapeDtypeStruct((1,8,length),jnp.float32)],
        compiler_params=pltpu.CompilerParams(vmem_limit_bytes=60*1024*1024),
        cost_estimate=pl.CostEstimate(flops=29*length*length*lanes,bytes_accessed=8*length*lanes,transcendentals=0),
        name="attend_forward")(firsts,lasts,q,k,v,start[None,:],*earlier)

def backward_kernel(block,full_end,some_end,q_ref,k_ref,v_ref,d_ref,o_ref,lse_ref,start_ref,cos_ref,sin_ref,*rest):
    p_ref,first_ref,dq_ref,delta_ref=rest[-4:]
    j=pl.program_id(1)
    length,lanes=q_ref.shape
    heads=lanes//HEAD_DIM
    @pl.when(j==0)
    def _():
        dq_ref[...]=jnp.zeros_like(dq_ref)
        for i in range(length//block):
            rows=pl.ds(i*block,block)
            prod=jnp.transpose(d_ref[rows,:].astype(jnp.float32)*o_ref[rows,:].astype(jnp.float32))
            for n in range(heads):
                delta_ref[n:n+1,rows]=jnp.sum(prod[n*HEAD_DIM:(n+1)*HEAD_DIM],axis=0,keepdims=True)
    k=k_ref[...]; v=v_ref[...]
    scale=HEAD_DIM**-0.5
    kl=[only_head(k,n,lanes) for n in range(heads)]
    ks=[x*jnp.asarray(scale,k.dtype) for x in kl]
    vs=[only_head(v,n,lanes) for n in range(heads)]
    part=256 if block%256==0 else block
    def terms(masked,keys,at,size):
        rows=pl.ds(pl.multiple_of(at,part),size)
        q=q_ref[rows,:]; d=d_ref[rows,:]
        ss=[dot(x[keys],q,NT) for x in ks]
        dps=[dot(x[keys],d,NT) for x in vs]
        if masked:
            shape=ss[0].shape
            key=j*block+keys.start+lax.broadcasted_iota(jnp.int32,shape,0)
            query=at+lax.broadcasted_iota(jnp.int32,shape,1)
            allowed=(key<=query)&(key>=start_ref[0:1,rows])
            ss=[jnp.where(allowed,s,masked_score) for s in ss]
        ps=[jnp.exp(ss[n]-lse_ref[0,n:n+1,rows]) for n in range(heads)]
        dss=[(ps[n]*(dps[n]-delta_ref[n:n+1,rows])).astype(jnp.bfloat16) for n in range(heads)]
        pv=[dot(p.astype(jnp.bfloat16),d,NN) for p in ps]
        pk=[dot(x,q,NN) for x in dss]
        dq_ref[rows,:]+=sum(dot(dss[n],ks[n][keys],TN) for n in range(heads))
        if heads==2:
            lane=lax.broadcasted_iota(jnp.int32,pv[0].shape,1)<HEAD_DIM
            return jnp.where(lane,pk[0],pk[1]),jnp.where(lane,pv[0],pv[1])
        return pk[0],pv[0]
    def step(masked,i,carry):
        dk,dv=terms(masked,slice(0,block),i*block,block)
        return carry[0]+dk,carry[1]+dv
    pieces=[terms(True,slice(at,at+part),j*block+at,block-at) for at in range(0,block,part)]
    carry=tuple(jnp.concatenate(x,axis=0) if len(x)>1 else x[0] for x in zip(*pieces))
    carry=lax.fori_loop(j+1,full_end[j],functools.partial(step,False),carry)
    dk,dv=lax.fori_loop(full_end[j],some_end[j],functools.partial(step,True),carry)
    here=pl.ds(pl.multiple_of(j*block,block),block)
    cosine,sine=cos_ref[here,:],-sin_ref[here,:]
    p_ref[:,:lanes]=turned(dq_ref[here,:],cosine,sine).astype(jnp.bfloat16)
    p_ref[:,lanes:2*lanes]=turned(dk*scale,cosine,sine).astype(jnp.bfloat16)
    blend=dv.astype(jnp.bfloat16).astype(jnp.float32)
    p_ref[:,2*lanes:]=(blend_weight*blend).astype(jnp.bfloat16)
    first_ref[...]=((1.0-blend_weight)*blend).astype(jnp.bfloat16)

def attend_backward(q,k,v,d,start,cosine,sine,block,group,o,lse,before=(),earlier=()):
    length,width=q.shape
    lanes=cosine.shape[1]; n=length//block
    lasts=start[block-1::block]
    edge=jnp.arange(n,dtype=jnp.int32)
    full_end=jnp.maximum(edge+1,jnp.sum((lasts[None,:]<=edge[:,None]*block).astype(jnp.int32),axis=1))
    reach=jnp.sum((start[None,:]<=edge[:,None]*block+block-1).astype(jnp.int32),axis=1)
    some_end=jnp.maximum(full_end,(reach+block-1)//block)
    whole=pl.BlockSpec((length,lanes),lambda g,j,*_:(0,group))
    part=pl.BlockSpec((block,lanes),lambda g,j,*_:(j,group))
    table=pl.BlockSpec((length,lanes),lambda g,j,*_:(0,0))
    more=list(earlier)+list(before)
    spec=pltpu.PrefetchScalarGridSpec(num_scalar_prefetch=2,grid=(1,n),
        in_specs=[whole,part,part,whole,table,pl.BlockSpec((1,8,length),lambda g,j,*_:(0,0,0)),pl.BlockSpec((1,length),lambda g,j,*_:(0,0)),table,table]+[pl.BlockSpec(memory_space=pl.ANY)]*len(more),
        out_specs=[pl.BlockSpec((block,3*lanes),lambda g,j,*_:(j,group)),part],
        scratch_shapes=[pltpu.VMEM((length,lanes),jnp.float32),pltpu.VMEM((8,length),jnp.float32)])
    return pl.pallas_call(functools.partial(backward_kernel,block),grid_spec=spec,
        out_shape=[jax.ShapeDtypeStruct((length,3*width),jnp.bfloat16),jax.ShapeDtypeStruct((length,width),jnp.bfloat16)],
        input_output_aliases={11+len(earlier)+k:k for k in range(len(before))},
        compiler_params=pltpu.CompilerParams(vmem_limit_bytes=56*1024*1024),
        cost_estimate=pl.CostEstimate(flops=52*length*length*lanes,bytes_accessed=22*length*lanes,transcendentals=0),
        name="attend_backward")(full_end,some_end,q,k,v,d,o,lse,start[None,:],cosine,sine,*more)


f32 = jnp.float32
bf16 = jnp.bfloat16
everywhere = pl.BlockSpec(memory_space=pl.ANY)


def swap(x, axis, mask):
    return lax.ppermute(x, axis, [(i, i ^ mask) for i in range(lax.axis_size(axis))])


def cut_of(rows):
    half = rows // 2
    return half - half % 8 if half >= 8 else half


def after(x, *earlier):
    def kernel(*refs):
        pass

    return pl.pallas_call(
        kernel,
        in_specs=[everywhere] * (1 + len(earlier)),
        out_specs=everywhere,
        out_shape=jax.ShapeDtypeStruct(x.shape, x.dtype),
        input_output_aliases={0: 0},
        name="after",
    )(x, *earlier)


def spread_relay(x, axis):
    count = lax.axis_size(axis)
    if count != 4:
        return [[x]] + [[swap(x, axis, e)] for e in range(1, count)]
    cut = cut_of(x.shape[0])
    one, two = swap(x, axis, 1), swap(x, axis, 2)
    return [[x], [one], [two], [swap(two[:cut], axis, 1), swap(one[cut:], axis, 2)]]


def spread(x, axis):
    return [x] + [swap(x, axis, e) for e in range(1, lax.axis_size(axis))]


def add_low(*terms):
    return sum(t.astype(f32) for t in terms).astype(bf16)


def collect(parts, axis):
    return sum((swap(p, axis, e) if e else p).astype(f32) for e, p in enumerate(parts))


def in_order(parts, rank):
    rows = parts[0].shape[0]
    whole = jnp.zeros((len(parts) * rows,) + parts[0].shape[1:], parts[0].dtype)
    for e, part in enumerate(parts):
        whole = lax.dynamic_update_slice_in_dim(whole, part, (rank ^ e) * rows, 0)
    return whole


def block_of(x, number, rows):
    return lax.dynamic_slice_in_dim(x, number * rows, rows, 0)


def both_cores(own, other, core):
    first = core == 0
    return jnp.concatenate([jnp.where(first, own, other), jnp.where(first, other, own)])


def sum_over_all(x):
    for axis in ("mlp", "dp", "head"):
        count = lax.axis_size(axis)
        if count == 4:
            x = (x + swap(x, axis, 1)) + (swap(x, axis, 2) + swap(x, axis, 3))
            continue
        mask = 1
        while mask < count:
            x = x + swap(x, axis, mask)
            mask *= 2
    return x


def rms_scale(rows):
    return lax.rsqrt(jnp.mean(rows * rows, axis=-1, keepdims=True) + epsilon)


def norm_back(rows, scale, gain, grad):
    weighted = grad * gain
    return scale * weighted - rows * scale * scale * scale * jnp.mean(
        weighted * rows, axis=-1, keepdims=True
    )


def turned(x, cosine, sine):
    half = HEAD_DIM // 2
    if x.shape[1] == HEAD_DIM:
        other = jnp.concatenate([x[:, half:], x[:, :half]], axis=1)
    else:
        lanes = x.shape[1]
        lane = lax.broadcasted_iota(jnp.int32, x.shape, 1)
        other = jnp.where(
            lane % HEAD_DIM < half, pltpu.roll(x, lanes - half, 1), pltpu.roll(x, half, 1)
        )
    return x * cosine + other * sine


def load_rows(refs, counts, number, target):
    at = 0
    for k, pieces in enumerate(counts):
        mine = refs[at : at + pieces]
        at += pieces

        @pl.when(number == k)
        def _(mine=mine):
            row = 0
            for ref in mine:
                target[row : row + ref.shape[0], :] = ref[...]
                row += ref.shape[0]


def project_kernel(counts, rank_ref, *refs):
    total = sum(counts)
    parts, (w_ref, gain_ref, cos_ref, sin_ref, first_ref) = refs[:total], refs[total : total + 5]
    a_ref, q_ref, k_ref, v_ref, norm_ref, rows_ref = refs[-6:]
    i = pl.program_id(0)
    load_rows(parts, counts, i, rows_ref)
    x = rows_ref[...].astype(f32)
    a = (x * rms_scale(x) * gain_ref[...]).astype(bf16)
    a_ref[...] = a
    width = q_ref.shape[1]
    lanes = cos_ref.shape[1]
    cosine, sine = cos_ref[...], sin_ref[...]
    joined = dot(a, w_ref[...], NN)
    of = lax.broadcasted_iota(jnp.int32, (lanes, 128), 0) // HEAD_DIM
    one_hot = (of == lax.broadcasted_iota(jnp.int32, (lanes, 128), 1)).astype(bf16)

    def norms(value):
        wide = value * value
        high = wide.astype(bf16)
        low = (wide - high.astype(f32)).astype(bf16)
        squares = dot(high, one_hot, NN) + dot(low, one_hot, NN)
        return jnp.sum(jnp.sqrt(jnp.maximum(squares, 0.0)), axis=0, keepdims=True)

    @pl.when(i == 0)
    def _():
        norm_ref[...] = jnp.zeros_like(norm_ref)

    for g in range(width // lanes):
        at = slice(g * lanes, (g + 1) * lanes)
        query, key, value = (
            joined[:, (3 * g + k) * lanes : (3 * g + k + 1) * lanes] for k in range(3)
        )
        q_ref[:, at] = turned(query, cosine, sine).astype(bf16)
        k_ref[:, at] = turned(key, cosine, sine).astype(bf16)
        first = first_ref[:, at].astype(f32)
        blended = blend_weight * value + (1.0 - blend_weight) * first
        v_ref[:, at] = blended.astype(bf16)
        norm_ref[0:1, :] += norms(first)
        norm_ref[1:2, :] += norms(blended)


def spec_whole(x):
    return pl.BlockSpec(x.shape, lambda *_: (0,) * x.ndim)


def cost(us):
    return pl.CostEstimate(flops=int(us * 1.1e9), bytes_accessed=int(us * 1e5), transcendentals=0)


big = pltpu.CompilerParams(vmem_limit_bytes=56 * 1024 * 1024)


def project(rank, parts, base, weights, gain, cosine, sine, firsts, before=()):
    counts = tuple(len(p) for p in parts)
    flat = [x for p in parts for x in p]
    chunk = sum(x.shape[0] for x in parts[0])
    length, width = firsts.shape
    model, lanes = flat[0].shape[1], cosine.shape[1]
    there = lambda i, r: (r[0] ^ (base + i), 0)
    block = lambda n: pl.BlockSpec((chunk, n), there)
    spec = pltpu.PrefetchScalarGridSpec(
        num_scalar_prefetch=1,
        grid=(len(parts),),
        in_specs=[spec_whole(x) for x in flat]
        + [spec_whole(weights), spec_whole(gain), block(lanes), block(lanes), block(width)]
        + [everywhere] * len(before),
        out_specs=[block(model), block(width), block(width), block(width)]
        + [pl.BlockSpec((8, 128), lambda i, r: (0, 0))],
        scratch_shapes=[pltpu.VMEM((chunk, model), bf16)],
    )
    low = jax.ShapeDtypeStruct((length, width), bf16)
    return pl.pallas_call(
        functools.partial(project_kernel, counts),
        grid_spec=spec,
        out_shape=[jax.ShapeDtypeStruct((length, model), bf16), low, low, low]
        + [jax.ShapeDtypeStruct((8, 128), f32)],
        input_output_aliases={len(flat) + 6 + k: k for k in range(len(before))},
        compiler_params=big,
        cost_estimate=cost(4.5 * len(parts)),
        name="project",
    )(rank[None], *flat, weights, gain, cosine, sine, firsts, *before)


def assemble_kernel(ranks, rank_ref, *refs):
    far_ref, out_ref = refs[-2:]
    rows = far_ref.shape[2]
    e = pl.program_id(0)
    for k in range(ranks):

        @pl.when(e == k)
        def _(ref=refs[k]):
            for a in range(3):
                far_ref[a, 0] = ref[a * rows : (a + 1) * rows, :]
            out_ref[0] = ref[3 * rows :, :]


def assemble(rank, bundles, rows, earlier):
    ranks = len(bundles)
    wide, model = bundles[0].shape
    spec = pltpu.PrefetchScalarGridSpec(
        num_scalar_prefetch=1,
        grid=(ranks,),
        in_specs=[spec_whole(b) for b in bundles] + [everywhere] * len(earlier),
        out_specs=[
            pl.BlockSpec((3, 1, rows, model), lambda e, r: (0, e, 0, 0)),
            pl.BlockSpec((1, wide - 3 * rows, model), lambda e, r: (r[0] ^ e, 0, 0)),
        ],
    )
    return pl.pallas_call(
        functools.partial(assemble_kernel, ranks),
        grid_spec=spec,
        out_shape=[
            jax.ShapeDtypeStruct((3, ranks, rows, model), bf16),
            jax.ShapeDtypeStruct((ranks, wide - 3 * rows, model), bf16),
        ],
        compiler_params=big,
        cost_estimate=cost(3),
        name="assemble",
    )(rank[None], *bundles, *earlier)


def feed_kernel(x_ref, g_ref, *refs):
    sources, (act_ref, in_ref, sum_ref) = (refs[0:3], refs[3:6], refs[6:9]), refs[-3:]
    f = pl.program_id(0)
    steps = pl.num_programs(0)

    def work(begin, gate_w, up_w, down_w):
        x, g = x_ref[...], g_ref[...]
        gate, up = dot(gate_w[...], x, NT), dot(up_w[...], x, NT)
        hidden_grad = dot(down_w[...], g, NT)
        sigma = 1.0 / (1.0 + jnp.exp(-gate))
        gate_sigma = gate * sigma
        hidden = (gate_sigma * up).astype(bf16)
        gate_grad = (hidden_grad * up * (sigma + gate_sigma * (1.0 - sigma))).astype(bf16)
        up_grad = (hidden_grad * gate_sigma).astype(bf16)
        act_ref[0, 0], act_ref[0, 1], act_ref[0, 2] = gate_grad, up_grad, hidden
        terms = dot(gate_grad, gate_w[...], TN) + dot(up_grad, up_w[...], TN)
        sum_ref[...] = terms if begin else sum_ref[...] + terms

    for number, condition in enumerate((f == 0, f == 1, f == 2, f == 3)):

        @pl.when(condition)
        def _(number=number):
            work(number == 0, *sources[max(number - 1, 0)])

    @pl.when(f == steps - 1)
    def _():
        in_ref[...] = sum_ref[...].astype(in_ref.dtype)


def feed(x, grad, own, far, far_other, dtype, earlier=()):
    tokens, model = x.shape
    part = own.shape[0] // 6
    block = lambda at: pl.BlockSpec((part, model), at)
    return pl.pallas_call(
        feed_kernel,
        grid=(4,),
        in_specs=[spec_whole(x), spec_whole(grad)]
        + [block(lambda f, a=a: (2 * a + jnp.minimum(f, 1), 0)) for a in range(3)]
        + [block(lambda f, a=a: (a, 0)) for a in range(3)] * 2
        + [everywhere] * len(earlier),
        out_specs=[
            pl.BlockSpec((1, 3, part, tokens), lambda f: (f, 0, 0, 0)),
            pl.BlockSpec((tokens, model), lambda f: (0, 0)),
        ],
        out_shape=[
            jax.ShapeDtypeStruct((4, 3, part, tokens), bf16),
            jax.ShapeDtypeStruct((tokens, model), dtype),
        ],
        scratch_shapes=[pltpu.VMEM((tokens, model), f32)],
        compiler_params=big,
        cost_estimate=cost(16),
        name="feed",
    )(x, grad, *([own] * 3), *([far] * 3), *([far_other] * 3), *earlier)


def half_grads(act_ref, near_ref, x_ref, xn_ref, g_ref, gn_ref, result_ref):
    a = pl.program_id(0)

    @pl.when(a < 2)
    def _():
        result_ref[...] = dot(act_ref[0, 0], x_ref[...], NN) + dot(near_ref[0, 0], xn_ref[...], NN)

    @pl.when(a == 2)
    def _():
        result_ref[...] = dot(act_ref[0, 0], g_ref[...], NN) + dot(near_ref[0, 0], gn_ref[...], NN)


def other_grads_kernel(scalars, *refs):
    out_ref, result_ref = refs[-2:]
    half_grads(*refs[:6], result_ref)
    out_ref[...] = result_ref[...].astype(bf16)


def far_grads_kernel(ranks, scalars, *refs):
    got_ref, out_refs, result_ref = refs[6], refs[7 : 7 + ranks], refs[-1]
    half_grads(*refs[:6], result_ref)
    rows = result_ref.shape[0] // ranks
    for e in range(ranks):
        at = slice(e * rows, (e + 1) * rows)
        out_refs[e][0] = (result_ref[at, :] + got_ref[at, :].astype(f32)).astype(bf16)


def own_grads_kernel(ranks, scalars, *refs):
    got_ref, out_ref, out_got_ref = refs[6:9]
    own_refs, result_ref = refs[9 : 9 + ranks], refs[-1]
    half_grads(*refs[:6], result_ref)
    i = pl.program_id(0)
    rows = result_ref.shape[0] // ranks
    result_ref[...] += got_ref[...].astype(f32)

    @pl.when(i == 0)
    def _():
        for e in range(ranks):
            number = scalars[1] ^ e
            both = out_ref[number].astype(f32) + out_got_ref[number].astype(f32)
            own_refs[e][3 * rows :, :] = both.astype(bf16)

    for a in range(3):

        @pl.when(i == a)
        def _(a=a):
            to = slice(a * rows, (a + 1) * rows)
            for e in range(ranks):
                if rows % 8 == 0:
                    at = pl.ds(pl.multiple_of((scalars[1] ^ e) * rows, 8), rows)
                    own_refs[e][to, :] = result_ref[at, :].astype(bf16)
                else:
                    for h in range(ranks):

                        @pl.when(scalars[1] ^ e == h)
                        def _(e=e, h=h):
                            own_refs[e][to, :] = result_ref[h * rows : (h + 1) * rows, :].astype(bf16)


def shard_grads(scalars, ranks, far, here, near, x, x_near, grad, grad_near, got=None):
    _, _, part, tokens = here.shape
    model = x.shape[1]
    if got is None:
        number = lambda c: 3 if far else 1 - c[0]
    else:
        number = lambda c: 2 if far else c[0]
    act = pl.BlockSpec((1, 1, part, tokens), lambda i, c: (number(c), i, 0, 0))
    in_specs = [act, act] + [spec_whole(x)] * 4
    args = [here, near, x, x_near, grad, grad_near]
    row_block = pl.BlockSpec((part, model), lambda i, c: (i, 0))
    rows = part // ranks
    if got is None:
        kernel, out_specs = other_grads_kernel, row_block
        out_shape = jax.ShapeDtypeStruct((3 * part, model), bf16)
    elif far:
        kernel = functools.partial(far_grads_kernel, ranks)
        in_specs.append(row_block)
        args += got
        out_specs = [pl.BlockSpec((1, rows, model), lambda i, c: (i, 0, 0))] * ranks
        out_shape = [jax.ShapeDtypeStruct((3, rows, model), bf16)] * ranks
    else:
        kernel = functools.partial(own_grads_kernel, ranks)
        in_specs += [row_block] + [spec_whole(g) for g in got[1:]]
        args += got
        wide = 3 * rows + got[1].shape[1]
        out_specs = [pl.BlockSpec((wide, model), lambda i, c: (0, 0))] * ranks
        out_shape = [jax.ShapeDtypeStruct((wide, model), bf16)] * ranks
    spec = pltpu.PrefetchScalarGridSpec(
        num_scalar_prefetch=1,
        grid=(3,),
        in_specs=in_specs,
        out_specs=out_specs,
        scratch_shapes=[pltpu.VMEM((part, model), f32)],
    )
    return pl.pallas_call(
        kernel,
        grid_spec=spec,
        out_shape=out_shape,
        compiler_params=big,
        cost_estimate=cost(8),
        name=("far" if far else "own") + ("_other" if got is None else "_sum"),
    )(scalars, *args)


def others_kernel(scalars, act_ref, near_ref, x_ref, xn_ref, g_ref, gn_ref, *refs):
    own_ref, far_ref, far_other_ref, far_out, own_out, out_ref, out_near_ref, sum_ref = refs
    i = pl.program_id(0)
    for a in range(6):

        @pl.when(i == a)
        def _(a=a):
            first, second = (x_ref, xn_ref) if a % 3 < 2 else (g_ref, gn_ref)
            target = far_out if a < 3 else own_out
            target[...] = (
                dot(act_ref[0, 0], first[...], NN) + dot(near_ref[0, 0], second[...], NN)
            ).astype(bf16)

    @pl.when(i == 5)
    def _():
        sum_ref[...] = jnp.zeros_like(sum_ref)

    for condition, ref in (((i == 6) | (i == 7), own_ref), (i == 8, far_ref), (i == 9, far_other_ref)):

        @pl.when(condition)
        def _(ref=ref):
            sum_ref[0] += dot(act_ref[0, 0], ref[...], TN)
            sum_ref[1] += dot(near_ref[0, 0], ref[...], TN)

    @pl.when(i == 9)
    def _():
        out_ref[...] = sum_ref[0]
        out_near_ref[...] = sum_ref[1].astype(bf16)


def others(scalars, here, near, x, x_near, grad, grad_near, own, far, far_other):
    _, _, part, tokens = here.shape
    model = x.shape[1]

    def act_at(i, c):
        number = jnp.where(i < 3, 3, jnp.where(i < 6, 1 - c[0], i - 6))
        return (number, jnp.where(i < 6, i % 3, 2), 0, 0)

    act = pl.BlockSpec((1, 1, part, tokens), act_at)
    row = lambda at: pl.BlockSpec((part, model), at)
    spec = pltpu.PrefetchScalarGridSpec(
        num_scalar_prefetch=1,
        grid=(10,),
        in_specs=[act, act]
        + [spec_whole(x)] * 4
        + [row(lambda i, c: (4 + jnp.clip(i - 6, 0, 1), 0))]
        + [row(lambda i, c: (2, 0))] * 2,
        out_specs=[
            row(lambda i, c: (jnp.minimum(i, 2), 0)),
            row(lambda i, c: (jnp.clip(i - 3, 0, 2), 0)),
            spec_whole(x),
            spec_whole(x),
        ],
        scratch_shapes=[pltpu.VMEM((2, tokens, model), f32)],
    )
    half = jax.ShapeDtypeStruct((3 * part, model), bf16)
    return pl.pallas_call(
        others_kernel,
        grid_spec=spec,
        out_shape=[half, half]
        + [jax.ShapeDtypeStruct((tokens, model), f32), jax.ShapeDtypeStruct((tokens, model), bf16)],
        compiler_params=big,
        cost_estimate=cost(19),
        name="others",
    )(scalars, here, near, x, x_near, grad, grad_near, own, far, far_other)


def regroup_kernel(ranks, rank_ref, *refs):
    out_ref = refs[-1]
    rows = out_ref.shape[2]
    e = pl.program_id(0)
    for k in range(ranks):

        @pl.when(e == k)
        def _(k=k):
            low, high = refs[2 * k], refs[2 * k + 1]
            cut = low.shape[0]
            for a in range(3):
                first, last = a * rows, (a + 1) * rows
                if last <= cut:
                    out_ref[a, 0] = low[first:last, :]
                elif first >= cut:
                    out_ref[a, 0] = high[first - cut : last - cut, :]
                else:
                    out_ref[a, 0, : cut - first] = low[first:, :]
                    out_ref[a, 0, cut - first :] = high[: last - cut, :]


def regroup(rank, pieces, rows, earlier=()):
    ranks = len(pieces)
    flat, specs = [], []
    for low, high in pieces:
        for x, at, size in (low, high):
            flat.append(x)
            specs.append(pl.BlockSpec((size, x.shape[1]), lambda e, r, at=at: (at, 0)))
    model = flat[0].shape[1]
    spec = pltpu.PrefetchScalarGridSpec(
        num_scalar_prefetch=1,
        grid=(ranks,),
        in_specs=specs + [everywhere] * len(earlier),
        out_specs=pl.BlockSpec((3, 1, rows, model), lambda e, r: (0, r[0] ^ e, 0, 0)),
    )
    return pl.pallas_call(
        functools.partial(regroup_kernel, ranks),
        grid_spec=spec,
        out_shape=jax.ShapeDtypeStruct((3, ranks, rows, model), bf16),
        compiler_params=big,
        cost_estimate=cost(2),
        name="regroup",
    )(rank[None], *flat, *earlier)


def unproject_kernel(counts, cuts, rank_ref, *refs):
    total = sum(counts)
    parts, w_ref, p_ref = refs[:total], refs[total], refs[total + 1]
    pieces = sum(len(c) for c in cuts)
    outs, gain_ref, rows_ref = refs[-2 - pieces : -2], refs[-2], refs[-1]
    i = pl.program_id(0)
    load_rows(parts, counts, i, rows_ref)
    x = rows_ref[...].astype(f32)
    grad = dot(p_ref[...], w_ref[...], NT)
    at = 0
    for k, sizes in enumerate(cuts):
        mine = outs[at : at + len(sizes)]
        at += len(sizes)

        @pl.when(i == k)
        def _(mine=mine):
            row = 0
            for ref in mine:
                ref[...] = grad[row : row + ref.shape[0]].astype(bf16)
                row += ref.shape[0]

    @pl.when(i == 0)
    def _():
        gain_ref[...] = jnp.zeros_like(gain_ref)

    gain_ref[...] += jnp.sum(grad * (x * rms_scale(x)), axis=0, keepdims=True)


def unproject(rank, parts, base, cuts, weights, grads, earlier=()):
    counts = tuple(len(p) for p in parts)
    flat = [x for p in parts for x in p]
    chunk, model = sum(x.shape[0] for x in parts[0]), flat[0].shape[1]
    block = lambda n: pl.BlockSpec((chunk, n), lambda i, r: (r[0] ^ (base + i), 0))
    sizes = [n for c in cuts for n in c]
    spec = pltpu.PrefetchScalarGridSpec(
        num_scalar_prefetch=1,
        grid=(len(parts),),
        in_specs=[spec_whole(x) for x in flat]
        + [spec_whole(weights)]
        + [block(grads.shape[1])]
        + [everywhere] * len(earlier),
        out_specs=[pl.BlockSpec((n, model), lambda i, r: (0, 0)) for n in sizes]
        + [pl.BlockSpec((1, model), lambda i, r: (0, 0))],
        scratch_shapes=[pltpu.VMEM((chunk, model), bf16)],
    )
    out = pl.pallas_call(
        functools.partial(unproject_kernel, counts, cuts),
        grid_spec=spec,
        out_shape=[jax.ShapeDtypeStruct((n, model), bf16) for n in sizes]
        + [jax.ShapeDtypeStruct((1, model), f32)],
        compiler_params=big,
        cost_estimate=cost(3.5 * len(parts)),
        name="unproject",
    )(rank[None], *flat, weights, grads, *earlier)
    return out[:-1], out[-1]


def state_kernel(back_ref, terms_ref, hidden_ref, grad_ref, gain_ref, w_ref, state_ref, low_ref, mixed_ref, sum_ref):
    hidden, gain = hidden_ref[...], gain_ref[...]
    grad = back_ref[...].astype(f32) + terms_ref[...]
    scale = rms_scale(hidden)
    state = grad_ref[...].astype(f32) + norm_back(hidden, scale, gain, grad)
    low = state.astype(bf16)
    state_ref[...] = state
    low_ref[...] = low
    for h in range(mixed_ref.shape[0]):
        mixed_ref[h] = dot(low, w_ref[h], NT).astype(bf16)

    @pl.when(pl.program_id(0) == 0)
    def _():
        sum_ref[...] = jnp.zeros_like(sum_ref)

    sum_ref[...] += jnp.sum(grad * hidden * scale, axis=0, keepdims=True)


def state_back(back, terms, hidden, grad, gain, weights):
    tokens, model = back.shape
    ranks, width, _ = weights.shape
    size = 128 if tokens % 128 == 0 else tokens
    row = pl.BlockSpec((size, model), lambda i: (i, 0))
    return pl.pallas_call(
        state_kernel,
        grid=(tokens // size,),
        in_specs=[row, row, row, row, spec_whole(gain), spec_whole(weights)],
        out_specs=[
            row,
            row,
            pl.BlockSpec((ranks, size, width), lambda i: (0, i, 0)),
            pl.BlockSpec((1, model), lambda i: (0, 0)),
        ],
        out_shape=[
            jax.ShapeDtypeStruct((tokens, model), f32),
            jax.ShapeDtypeStruct((tokens, model), bf16),
            jax.ShapeDtypeStruct((ranks, tokens, width), bf16),
            jax.ShapeDtypeStruct((1, model), f32),
        ],
        compiler_params=big,
        cost_estimate=cost(6),
        name="state_back",
    )(back, terms, hidden, grad, gain, weights)


def on_device(
    tokens,
    first_values,
    segment_ids,
    positions,
    attn_gain,
    w_query,
    w_key,
    w_value,
    w_out,
    mlp_gain,
    w_gate,
    w_up,
    w_down,
    out_grad,
):
    core, rank = lax.axis_index("dp"), lax.axis_index("head")
    ranks = lax.axis_size("head")
    chunk, width = tokens.shape[0], w_query.shape[1]
    model = tokens.shape[2]
    length, ff = segment_ids.shape[0], w_gate.shape[1]
    block = min(512, length)
    tokens, firsts, out_grad = tokens[:, 0], first_values[:, 0], out_grad[:, 0]
    places = positions[:, 0]
    start = jnp.arange(length, dtype=jnp.int32) - places

    row_parts = spread_relay(tokens, "head")

    part = ff // 2
    rows = part // ranks
    stack = jnp.concatenate([w_gate.T, w_up.T, w_down])
    cut_stack = stack.reshape(3, 2 * ranks, rows, model)
    far_piece = swap(
        lax.dynamic_index_in_dim(cut_stack, core * ranks + rank, 1, False), "mlp", 2
    ).reshape(3 * rows, model)
    out_grad_near = swap(out_grad, "mlp", 1)
    half_out = width // 2
    far_piece = after(far_piece, *row_parts[-1])
    bundle = jnp.concatenate([far_piece, block_of(w_out, core, half_out)])
    bundles = spread(bundle, "head")

    lanes = min(128, width)
    w_project = jnp.concatenate(
        [
            w[:, g * lanes : (g + 1) * lanes]
            for g in range(width // lanes)
            for w in (w_query, w_key, w_value)
        ],
        axis=1,
    )
    lane = jnp.arange(lanes)
    freq = theta_base ** (-(lane % (HEAD_DIM // 2)).astype(f32) * 2.0 / HEAD_DIM)
    angles = places.astype(f32)[:, None] * freq
    cosine = jnp.cos(angles)
    sine = jnp.sin(angles) * jnp.where(lane % HEAD_DIM < HEAD_DIM // 2, -1.0, 1.0)
    heads_args = (w_project, attn_gain[None], cosine, sine, firsts)
    soon = 3 if ranks == 4 else ranks
    *projected, norms = project(rank, row_parts[:soon], 0, *heads_args)
    if soon < ranks:
        *projected, more = project(rank, row_parts[soon:], soon, *heads_args, projected)
        norms = norms + more
    gathered, queries, keys, values = projected
    groups = width // lanes
    mixed, log_total, mixed_here = [], [], []
    for g in range(groups):
        one_mixed, one_total = attend_forward2(
            queries, keys, values, start, min(1024, length), g, tuple(mixed[-1:])
        )
        mixed.append(one_mixed)
        log_total.append(one_total)
        mixed_here.append(
            lax.all_to_all(one_mixed, "head", 0, 0, tiled=True).reshape(ranks, chunk, lanes)
        )

    far_half, out_half = assemble(rank, bundles, rows, (mixed_here[0], mixed[-1]))
    far_half = far_half.reshape(3 * part, model)
    far_other, out_other = swap(far_half, "dp", 1), swap(out_half, "dp", 1)
    first = core == 0
    out_all = jnp.concatenate(
        [jnp.where(first, out_half, out_other), jnp.where(first, out_other, out_half)], axis=1
    )

    residual = tokens.astype(f32)
    hidden_state = residual + sum(
        jnp.einsum("htk,hkd->td", m, out_all[:, g * lanes : (g + 1) * lanes], preferred_element_type=f32)
        for g, m in enumerate(mixed_here)
    )
    mlp_scale = rms_scale(hidden_state)
    mlp_input = (hidden_state * mlp_scale * mlp_gain).astype(bf16)
    mlp_input_near = swap(mlp_input, "mlp", 1)

    acts, terms = feed(mlp_input, out_grad, stack, far_half, far_other, f32)
    acts_near, terms_near = feed(
        mlp_input_near, out_grad_near, stack, far_half, far_other, bf16, (terms,)
    )
    terms_back = swap(terms_near, "mlp", 1)
    scalars = jnp.stack([core, rank]).astype(jnp.int32)
    tokens_two = (acts, acts_near, mlp_input, mlp_input_near, out_grad, out_grad_near)
    far_other_grads, own_other_grads, down_here, down_near = others(
        scalars, *tokens_two, stack, far_half, far_other
    )
    terms_back = after(terms_back, down_near)
    far_half_got = swap(after(far_other_grads, terms_back), "dp", 1)
    own_half_got = swap(after(own_other_grads, far_half_got), "dp", 1)
    state_grad, state_grad_low, mixed_grad, mlp_gain_grad = state_back(
        terms_back, terms, hidden_state, out_grad, mlp_gain[None], out_all
    )
    mlp_gain_grad = mlp_gain_grad[0]
    mixed_grad_rows = lax.all_to_all(mixed_grad, "head", 0, 0, tiled=True).reshape(length, width)

    low_grad = after(state_grad_low, mixed_grad)
    out_grads = [
        jnp.einsum("htk,td->hkd", m, low_grad, preferred_element_type=f32).astype(bf16)
        for m in mixed_here
    ]
    out_grads = jnp.concatenate(out_grads, axis=1).reshape(ranks, 2, half_out, model)
    out_got = swap(lax.dynamic_index_in_dim(out_grads, 1 - core, 1, False), "dp", 1)
    out_own = lax.dynamic_index_in_dim(out_grads, core, 1, False)
    far_half_got = after(far_half_got, mixed_grad)
    far_chip = shard_grads(scalars, ranks, True, *tokens_two, [far_half_got])
    far_got = [swap(f, "head", e) for e, f in enumerate(far_chip) if e]
    mixed_grad_rows = after(mixed_grad_rows, far_chip[0])

    back_args = (queries, keys, values, mixed_grad_rows, start, cosine, sine, block)
    grads = attend_backward(*back_args, 0, mixed[0], log_total[0])
    own_half_got = after(own_half_got, grads[0])
    own_chip = shard_grads(scalars, ranks, False, *tokens_two, [own_half_got, out_own, out_got])
    far_got = [after(f, own_chip[0]) for f in far_got]
    far_sum = add_low(far_chip[0], *far_got)
    far_here = swap(far_sum, "mlp", 2)
    own_chip = [own_chip[0]] + [after(f, far_sum) for f in own_chip[1:]]
    own_got = [swap(f, "head", e) for e, f in enumerate(own_chip) if e]
    down_back = swap(after(down_near, own_chip[0]), "mlp", 1)
    for g in range(1, width // lanes):
        grads = attend_backward(
            *back_args, g, mixed[g], log_total[g], grads, (far_sum, *own_chip[1:])
        )
    proj_grad, first_values_grad = grads
    cut = cut_of(chunk)
    half_proj = model // 2
    proj_wgrad = dot(gathered, proj_grad, TN).astype(bf16)
    if ranks == 4:
        (low, high), gain_last = unproject(
            rank, row_parts[3:], 3, ((cut, chunk - cut),), w_project, proj_grad, (proj_wgrad, down_back)
        )
        for_two, for_one = swap(low, "head", 1), swap(high, "head", 2)
        own_got = [after(f, low) for f in own_got]
    else:
        own_got = [after(f, proj_grad) for f in own_got]
    own_all = (own_chip[0], *own_got)
    piece_sum = add_low(*(f[: 3 * rows] for f in own_all), far_here.reshape(3 * rows, model))
    out_sum = add_low(*(f[3 * rows :] for f in own_all))
    proj_got = swap(after(block_of(proj_wgrad, 1 - core, half_proj), own_got[-1]), "dp", 1)
    proj_mine = add_low(block_of(proj_wgrad, core, half_proj), proj_got)
    both_mine = jnp.concatenate([proj_mine, out_sum.reshape(half_proj, -1)], axis=1)
    line, count = lax.axis_index("mlp"), lax.axis_size("mlp")

    def line_sum(x):
        size = x.shape[0] // count
        return collect([block_of(x, line ^ e, size) for e in range(count)], "mlp").astype(bf16)

    if ranks == 4:
        cut_p = cut_of(3 * rows)
        cut_q = 3 * rows - cut_p
        (own, one, two), gain_rest = unproject(
            rank,
            row_parts[:3],
            0,
            ((chunk,),) * 3,
            w_project,
            proj_grad,
            (both_mine,),
        )
        attn_gain_grad = gain_last + gain_rest
        piece_sum = after(piece_sum, own)
        low_p, high_p = piece_sum[:cut_p], piece_sum[cut_p:]
        low_x, high_y = swap(low_p, "head", 1), swap(high_p, "head", 2)
        low_yy = swap(jnp.concatenate([low_p, low_x]), "head", 2)
        high_xx = swap(jnp.concatenate([high_p, high_y]), "head", 1)
        one = one.at[cut:].set(add_low(one[cut:], for_one))
        two = two.at[:cut].set(add_low(two[:cut], for_two))
        one_got, two_got = swap(one, "head", 1), swap(two, "head", 2)
        half_sum = regroup(
            rank,
            [
                ((low_p, 0, cut_p), (high_p, 0, cut_q)),
                ((low_x, 0, cut_p), (high_xx, 0, cut_q)),
                ((low_yy, 0, cut_p), (high_y, 0, cut_q)),
                ((low_yy, 1, cut_p), (high_xx, 1, cut_q)),
            ],
            rows,
        )
        line_piece = after(line_sum(both_mine), one, two)
        attn_normed_grad = own.astype(f32) + one_got.astype(f32) + two_got.astype(f32)
        ended = (one_got, two_got)
    else:
        parts, attn_gain_grad = unproject(
            rank, row_parts, 0, ((chunk,),) * ranks, w_project, proj_grad
        )
        half_sum = jnp.zeros((3, ranks, rows, model), bf16)
        for e, piece in enumerate(spread(piece_sum, "head")):
            piece = piece.reshape(3, 1, rows, model)
            half_sum = lax.dynamic_update_slice_in_dim(half_sum, piece, rank ^ e, 1)
        attn_normed_grad = collect(parts, "head")
        ended = (attn_normed_grad,)
        line_piece = line_sum(both_mine)
    half_sum = half_sum.reshape(3, part, model)

    norm_row = jnp.zeros((model,), f32).at[:2].set(jnp.sum(norms[:2], axis=1))
    if count == 4:
        line_one = swap(line_piece, "mlp", 1)
        line_two = swap(jnp.concatenate([line_piece, line_one]), "mlp", 2)
        size = line_piece.shape[0]
        line_got = [line_piece, line_one, line_two[:size], line_two[size:]]
    else:
        line_got = spread(line_piece, "mlp")
    small = jnp.stack([attn_gain_grad[0], mlp_gain_grad, norm_row])
    small = sum_over_all(after(small, line_got[1]))
    output = (hidden_state + after(down_back, line_piece).astype(f32) + down_here).astype(bf16)

    half_sum = after(half_sum, line_piece)
    other_sum = swap(half_sum, "dp", 1)
    ff_grads = jnp.concatenate(
        [jnp.where(first, half_sum, other_sum), jnp.where(first, other_sum, half_sum)], axis=1
    ).astype(f32)
    gate_wgrad, up_wgrad, down_wgrad = ff_grads[0].T, ff_grads[1].T, ff_grads[2]
    input_grad = (
        state_grad + norm_back(residual, rms_scale(residual), attn_gain, attn_normed_grad)
    ).astype(bf16)

    line_got = [after(line_got[0], output, input_grad, down_wgrad, small)] + line_got[1:]
    both_half = in_order(line_got, line)
    both_other = swap(both_half, "dp", 1)
    proj_sum = both_cores(both_half[:, : 3 * width], both_other[:, : 3 * width], core).astype(f32)
    query_wgrad, key_wgrad, value_wgrad = (
        jnp.concatenate(
            [proj_sum[:, (3 * g + k) * lanes : (3 * g + k + 1) * lanes] for g in range(width // lanes)],
            axis=1,
        )
        for k in range(3)
    )
    out_wgrad = both_cores(
        both_half[:, 3 * width :].reshape(half_out, model),
        both_other[:, 3 * width :].reshape(half_out, model),
        core,
    ).astype(f32)

    devices = lax.axis_size("dp") * ranks * count
    value_norms = small[2, :2] / (length * (width // HEAD_DIM) * devices)
    return (
        output[:, None],
        input_grad[:, None],
        first_values_grad[:, None],
        small[0],
        query_wgrad,
        key_wgrad,
        value_wgrad,
        out_wgrad,
        small[1],
        gate_wgrad,
        up_wgrad,
        down_wgrad,
        value_norms,
    )


def solution(mesh):
    placed = (
        P("head", ("dp", "mlp"), None),
        P(None, ("dp", "mlp"), "head"),
        P(None, ("dp", "mlp")),
        P(None, ("dp", "mlp")),
        P(),
        P(None, "head"),
        P(None, "head"),
        P(None, "head"),
        P("head", None),
        P(),
        P(None, "mlp"),
        P(None, "mlp"),
        P("mlp", None),
        P("head", ("dp", "mlp"), None),
    )
    return jax.shard_map(
        on_device,
        mesh=mesh,
        in_specs=placed,
        out_specs=(
            P("head", ("dp", "mlp"), None),
            P("head", ("dp", "mlp"), None),
            P(None, ("dp", "mlp"), "head"),
            P(),
            P(None, "head"),
            P(None, "head"),
            P(None, "head"),
            P("head", None),
            P(),
            P(None, "mlp"),
            P(None, "mlp"),
            P("mlp", None),
            P(),
        ),
        check_vma=False,
    )
```
